128 devices in a mesh: ta: 16 (over y_hi, x, core), col: 8 (over y_lo, z).
Axes of the slice: x: 4, y: 4 (y_hi: 2, y_lo: 2; y = y_hi * 2 + y_lo), z: 4, core: 2. Of those that a mesh axis runs over, the one named last changes fastest.
Arguments:
- big_tokens: bfloat16 [8, 2048, 1024], P('col', 'ta'), may hold values from -6 to 6
- small_tokens: bfloat16 [32, 512, 1024], P('col', 'ta'), may hold values from -6 to 6
- big_actions: int32 [8, 8], P('col'), may hold values from 0 to 7
- small_actions: int32 [32, 8], P('col'), may hold values from 0 to 7
- big_order: int32 [8, 8], P('col'), may hold values from 0 to 7, each once within a row
- small_order: int32 [32, 8], P('col'), may hold values from 0 to 7, each once within a row
- small_live: int32 [32], P('col'), may hold values from 0 to 1, as said below
- action_table: bfloat16 [8, 1024], replicated, may hold values from -6 to 6
- norm1_gain: bfloat16 [1024], replicated, may hold values from 0.099609375 to 1.8984375
- norm1_bias: bfloat16 [1024], replicated, may hold values from -3 to 3
- spatial_qkv: bfloat16 [1024, 3072], replicated, may hold values from -0.1875 to 0.1875
- spatial_out: bfloat16 [1024, 1024], replicated, may hold values from -0.5 to 0.5
- spatial_out_bias: bfloat16 [1024], replicated, may hold values from -3 to 3
- norm2_gain: bfloat16 [1024], replicated, may hold values from 0.099609375 to 1.8984375
- norm2_bias: bfloat16 [1024], replicated, may hold values from -3 to 3
- temporal_qkv: bfloat16 [1024, 3072], replicated, may hold values from -0.1875 to 0.1875
- temporal_out: bfloat16 [1024, 1024], replicated, may hold values from -0.375 to 0.375
- temporal_out_bias: bfloat16 [1024], replicated, may hold values from -3 to 3
- norm3_gain: bfloat16 [1024], replicated, may hold values from 0.099609375 to 1.8984375
- norm3_bias: bfloat16 [1024], replicated, may hold values from -3 to 3
- ffn_in: bfloat16 [1024, 4096], replicated, may hold values from -0.1875 to 0.1875
- ffn_in_bias: bfloat16 [4096], replicated, may hold values from -3 to 3
- ffn_out: bfloat16 [4096, 1024], replicated, may hold values from -0.09375 to 0.09375
- ffn_out_bias: bfloat16 [1024], replicated, may hold values from -3 to 3
- big_cotangent: bfloat16 [8, 2048, 1024], P('col', 'ta'), may hold values from -6 to 6
- small_cotangent: bfloat16 [32, 512, 1024], P('col', 'ta'), may hold values from -6 to 6
Outputs:
- big_output: bfloat16 [8, 2048, 1024], P('col', 'ta')
- small_output: bfloat16 [32, 512, 1024], P('col', 'ta')
- big_input_grad: float32 [8, 2048, 1024], P('col', 'ta')
- small_input_grad: float32 [32, 512, 1024], P('col', 'ta')
- action_table_grad: float32 [8, 1024], replicated
- norm1_gain_grad: float32 [1024], replicated
- norm1_bias_grad: float32 [1024], replicated
- spatial_qkv_grad: float32 [1024, 3072], P('col')
- spatial_out_grad: float32 [1024, 1024], P('col')
- spatial_out_bias_grad: float32 [1024], replicated
- norm2_gain_grad: float32 [1024], replicated
- norm2_bias_grad: float32 [1024], replicated
- temporal_qkv_grad: float32 [1024, 3072], P('col')
- temporal_out_grad: float32 [1024, 1024], P('col')
- temporal_out_bias_grad: float32 [1024], replicated
- norm3_gain_grad: float32 [1024], replicated
- norm3_bias_grad: float32 [1024], replicated
- ffn_in_grad: float32 [1024, 4096], P('col')
- ffn_in_bias_grad: float32 [4096], replicated
- ffn_out_grad: float32 [4096, 1024], P('col')
- ffn_out_bias_grad: float32 [1024], replicated
The draws below stay inside these ranges and needn't reach their ends.
Inputs may be any that keep to these rules, and one draw needn't show every extreme that they name: `small_live`: the small slots of one index of col hold their clips first; each index of col holds 0 to 4 clips, some index holds 4, and some other index holds fewer than 4.
All inputs are finite; a program needn't handle non-finite values.
Results may differ from the reference program's by a relative error of at most 0.024.
Values may be sent and summed in bfloat16 or wider, within the bound.
A program may use at most 384 MiB of HBM per device.

```python
import jax
import jax.numpy as jnp
from jax import lax

D = 1024
HEAD_DIM = 64
FF = 4096
ACTIONS = 8
BIGH = 128
SMALLH = 32
SSLOT = 4
FRAMES = 8
N_TA = 16
N_COL = 8


def draw_small_live(key, part):
    key = jax.random.fold_in(key, 7)
    count_key, full_key, short_key, short_count_key = jax.random.split(key, 4)
    counts = jax.random.randint(count_key, (N_COL,), 0, SSLOT + 1)
    full_group = jax.random.randint(full_key, (), 0, N_COL)
    short_group = (full_group + jax.random.randint(short_key, (), 1, N_COL)) % N_COL
    short_count = jax.random.randint(short_count_key, (), 0, SSLOT)
    groups = jnp.arange(N_COL)
    counts = jnp.where(groups == full_group, SSLOT, counts)
    counts = jnp.where(groups == short_group, short_count, counts)
    slots = jnp.arange(SSLOT)
    return (slots[None, :] < counts[:, None]).astype(jnp.int32).reshape(-1)


def plant(values, key, smallest, largest):
    extent = values.shape
    spot = [jax.random.randint(jax.random.fold_in(key, axis), (), 0, extent[axis]) for axis in range(len(extent))]
    values = values.at[tuple(spot)].set(smallest)
    longest = extent.index(max(extent))
    spot[longest] = (spot[longest] + 1) % extent[longest]
    return values.at[tuple(spot)].set(largest)


def block_scale(rng, shape, shards, low, largest):
    level, own = 1.0, jax.random.fold_in(rng, 6)
    for position, blocks in shards:
        heights = jnp.exp(jax.random.uniform(jax.random.fold_in(own, position), (blocks,), jnp.float32, low / len(shards), largest / len(shards)))
        level = level * jnp.repeat(heights, shape[position] // blocks).reshape([-1 if axis == position else 1 for axis in range(len(shape))])
    return level


def normal_values(key, shape, deviation, bound, pieces=(), dtype=jnp.bfloat16):
    drawn = jax.random.normal(key, shape, jnp.float32) * deviation
    if len(pieces) > 0:
        drawn = block_scale(key, shape, pieces, -0.22, 0.18) * drawn
    return jnp.clip(drawn, min=-bound, max=bound).astype(dtype)


def setup_inputs(seed: int = 0) -> dict:
    splits = jax.random.split(jax.random.key(seed), 27)
    big_tokens = normal_values(splits[0], (N_COL, N_TA * BIGH, D), 1.0, 6.0, ((0, 8), (1, 16)))
    small_tokens = normal_values(splits[1], (N_COL * SSLOT, N_TA * SMALLH, D), 1.0, 6.0, ((0, 8), (1, 16)))
    big_actions = plant(jax.random.randint(splits[2], (N_COL, FRAMES), 0, ACTIONS), jax.random.fold_in(splits[2], 1), 0, ACTIONS - 1).astype(jnp.int32)
    small_actions = plant(jax.random.randint(splits[3], (N_COL * SSLOT, FRAMES), 0, ACTIONS), jax.random.fold_in(splits[3], 1), 0, ACTIONS - 1).astype(jnp.int32)
    big_order = jax.vmap(lambda own: jax.random.permutation(own, FRAMES))(jax.random.split(splits[4], N_COL)).reshape((N_COL, FRAMES)).astype(jnp.int32)
    small_order = jax.vmap(lambda own: jax.random.permutation(own, FRAMES))(jax.random.split(splits[5], (N_COL * SSLOT))).reshape((N_COL * SSLOT, FRAMES)).astype(jnp.int32)
    small_live = draw_small_live(jax.random.fold_in(splits[26], 71), 0)
    action_table = normal_values(splits[7], (ACTIONS, D), 1.0, 6.0)
    norm1_gain = jnp.clip(1.0 + 0.18 * jax.random.normal(splits[8], (D,), jnp.float32), 0.099609375, 1.8984375).astype(jnp.bfloat16)
    norm1_bias = normal_values(splits[9], (D,), 0.5, 3.0)
    spatial_qkv = normal_values(splits[10], (D, 3 * D), D ** -0.5, 0.1875)
    spatial_out = normal_values(splits[11], (D, D), (D // 8) ** -0.5, 0.5)
    spatial_out_bias = normal_values(splits[12], (D,), 0.5, 3.0)
    norm2_gain = jnp.clip(1.0 + 0.18 * jax.random.normal(splits[13], (D,), jnp.float32), 0.099609375, 1.8984375).astype(jnp.bfloat16)
    norm2_bias = normal_values(splits[14], (D,), 0.5, 3.0)
    temporal_qkv = normal_values(splits[15], (D, 3 * D), D ** -0.5, 0.1875)
    temporal_out = normal_values(splits[16], (D, D), (D // 4) ** -0.5, 0.375)
    temporal_out_bias = normal_values(splits[17], (D,), 0.5, 3.0)
    norm3_gain = jnp.clip(1.0 + 0.18 * jax.random.normal(splits[18], (D,), jnp.float32), 0.099609375, 1.8984375).astype(jnp.bfloat16)
    norm3_bias = normal_values(splits[19], (D,), 0.5, 3.0)
    ffn_in = normal_values(splits[20], (D, FF), D ** -0.5, 0.1875)
    ffn_in_bias = normal_values(splits[21], (FF,), 0.5, 3.0)
    ffn_out = normal_values(splits[22], (FF, D), FF ** -0.5, 0.09375)
    ffn_out_bias = normal_values(splits[23], (D,), 0.5, 3.0)
    big_cotangent = normal_values(splits[24], (N_COL, N_TA * BIGH, D), 1.0, 6.0, ((0, 8), (1, 16)))
    small_cotangent = normal_values(splits[25], (N_COL * SSLOT, N_TA * SMALLH, D), 1.0, 6.0, ((0, 8), (1, 16)))
    return {"big_tokens": big_tokens, "small_tokens": small_tokens, "big_actions": big_actions, "small_actions": small_actions, "big_order": big_order, "small_order": small_order, "small_live": small_live, "action_table": action_table, "norm1_gain": norm1_gain, "norm1_bias": norm1_bias, "spatial_qkv": spatial_qkv, "spatial_out": spatial_out, "spatial_out_bias": spatial_out_bias, "norm2_gain": norm2_gain, "norm2_bias": norm2_bias, "temporal_qkv": temporal_qkv, "temporal_out": temporal_out, "temporal_out_bias": temporal_out_bias, "norm3_gain": norm3_gain, "norm3_bias": norm3_bias, "ffn_in": ffn_in, "ffn_in_bias": ffn_in_bias, "ffn_out": ffn_out, "ffn_out_bias": ffn_out_bias, "big_cotangent": big_cotangent, "small_cotangent": small_cotangent}


@jax.custom_vjp
def low(v):
    return lax.optimization_barrier(v.astype(jnp.bfloat16)).astype(jnp.float32)

@jax.custom_vjp
def low_back(v):
    return v

def low_keep(v):
    return (low(v), None)

def low_pass(kept, grad):
    return (grad,)

def back_keep(v):
    return (v, None)

def back_low(kept, grad):
    return (low(grad),)
low.defvjp(low_keep, low_pass)
low_back.defvjp(back_keep, back_low)
EPSILON = 1e-05
MASKED_SCORE = -1e+30
HIGHEST = lax.Precision.HIGHEST

def normalize(rows, gain, shift):
    mean_row = lax.optimization_barrier(jnp.mean(rows, axis=-1, keepdims=True))
    centered = rows - mean_row
    variance = lax.optimization_barrier(jnp.mean(centered * centered, axis=-1, keepdims=True))
    return centered * lax.rsqrt(variance + EPSILON) * gain + shift

def project(activation, weight):
    return jnp.einsum('...k,kn->...n', activation, weight, precision=HIGHEST)

def attend(queries, key_rows, value_rows, visible):
    scale_factor = queries.shape[-1] ** (-0.5)
    scores = low_back(jnp.einsum('bqhe,bkhe->bhqk', queries, key_rows, precision=HIGHEST) * scale_factor)
    scores = jnp.where(visible, scores, MASKED_SCORE)
    row_max = lax.optimization_barrier(jnp.max(scores, axis=-1, keepdims=True))
    weights = jnp.exp(scores - row_max)
    probability = low(weights / lax.optimization_barrier(jnp.sum(weights, axis=-1, keepdims=True)))
    return jnp.einsum('bhqk,bkhe->bqhe', probability, value_rows, precision=HIGHEST)

def block_layer(tokens, action_ids, frame_order, parameters):
    action_rows, gain_one, shift_one, qkv_one, out_one, bias_one, gain_two, shift_two, qkv_two, out_two, bias_two, gain_three, shift_three, inner_weight, inner_bias, outer_weight, outer_bias = parameters
    clip_count, frame_count, token_count, model_width = tokens.shape
    head_count = model_width // HEAD_DIM
    action_pick = (action_ids[:, :, None] == jnp.arange(ACTIONS)[None, None, :]).astype(jnp.float32)
    resid_zero = tokens + project(action_pick, action_rows)[:, :, None, :]
    normed_one = low(normalize(resid_zero, gain_one, shift_one))
    packed_one = low(low_back(project(normed_one, qkv_one)))
    packed_one = packed_one.reshape(clip_count * frame_count, token_count, 3, head_count, HEAD_DIM)
    context_one = attend(packed_one[:, :, 0], packed_one[:, :, 1], packed_one[:, :, 2], True)
    context_one = low(low_back(context_one.reshape(clip_count, frame_count, token_count, model_width)))
    resid_one = resid_zero + low_back(project(context_one, out_one)) + bias_one
    normed_two = low(low_back(normalize(resid_one, gain_two, shift_two)))
    packed_two = low(low_back(project(normed_two, qkv_two)))
    by_position = jnp.swapaxes(packed_two, 1, 2).reshape(clip_count * token_count, frame_count, 3, head_count, HEAD_DIM)
    visible = frame_order[:, None, :] <= frame_order[:, :, None]
    visible = jnp.repeat(visible, token_count, axis=0)[:, None, :, :]
    context_two = attend(by_position[:, :, 0], by_position[:, :, 1], by_position[:, :, 2], visible)
    context_two = jnp.swapaxes(context_two.reshape(clip_count, token_count, frame_count, model_width), 1, 2)
    context_two = low(low_back(context_two))
    resid_two = resid_one + low_back(project(context_two, out_two)) + bias_two
    normed_three = low(normalize(resid_two, gain_three, shift_three))
    hidden = low_back(project(normed_three, inner_weight)) + inner_bias
    activated = low(jax.nn.gelu(hidden))
    return resid_two + low_back(project(activated, outer_weight)) + outer_bias

def reference(big_tokens, small_tokens, big_actions, small_actions, big_order, small_order, small_live, action_table, norm1_gain, norm1_bias, spatial_qkv, spatial_out, spatial_out_bias, norm2_gain, norm2_bias, temporal_qkv, temporal_out, temporal_out_bias, norm3_gain, norm3_bias, ffn_in, ffn_in_bias, ffn_out, ffn_out_bias, big_cotangent, small_cotangent):
    parameters = tuple((argument.astype(jnp.float32) for argument in (action_table, norm1_gain, norm1_bias, spatial_qkv, spatial_out, spatial_out_bias, norm2_gain, norm2_bias, temporal_qkv, temporal_out, temporal_out_bias, norm3_gain, norm3_bias, ffn_in, ffn_in_bias, ffn_out, ffn_out_bias)))
    big_rows = big_tokens.astype(jnp.float32).reshape(N_COL, FRAMES, 2 * BIGH, D)
    small_rows = small_tokens.astype(jnp.float32).reshape(N_COL * SSLOT, FRAMES, 2 * SMALLH, D)
    alive = small_live.astype(jnp.float32)[:, None, None, None]

    def forward(weights, big_in, small_in):
        return (block_layer(big_in, big_actions, big_order, weights), alive * block_layer(small_in, small_actions, small_order, weights))
    (big_result, small_result), pullback = jax.vjp(forward, parameters, big_rows, small_rows)
    grads, big_grad, small_grad = pullback((big_cotangent.astype(jnp.float32).reshape(big_rows.shape), small_cotangent.astype(jnp.float32).reshape(small_rows.shape)))
    big_shape = (N_COL, N_TA * BIGH, D)
    small_shape = (N_COL * SSLOT, N_TA * SMALLH, D)
    return (big_result.reshape(big_shape).astype(jnp.bfloat16), small_result.reshape(small_shape).astype(jnp.bfloat16), big_grad.reshape(big_shape), small_grad.reshape(small_shape), grads[0], grads[1], grads[2], grads[3], grads[4], grads[5], grads[6], grads[7], grads[8], grads[9], grads[10], grads[11], grads[12], grads[13], grads[14], grads[15], grads[16])
```

```python
import functools

import jax
import jax.numpy as jnp
from jax import lax
from jax.experimental import pallas as pl
from jax.experimental.pallas import tpu as pltpu
from jax.sharding import PartitionSpec as P

HEAD_DIM = 64
EPSILON = 1e-05
MASKED_SCORE = -1e30
MESH = pl.DeviceIdType.MESH
ANY = pl.BlockSpec(memory_space=pl.ANY)
LANES = 128
SPATIAL_FORMS = ("bqhe", "bkhe", "bhqk")

ORDERS = (("x", "y", "z"), ("y", "z", "x"), ("z", "x", "y"))
MATRICES = (
    ("ffn_out", (1, 1, 2)),
    ("ffn_in", (6, 6, 4)),
    ("temporal_out", (1, 2, 1)),
    ("temporal_qkv", (4, 4, 4)),
    ("spatial_out", (2, 1, 1)),
    ("spatial_qkv", (4, 4, 4)),
)


class Place:
    def __init__(self):
        ta, col = lax.axis_index("ta"), lax.axis_index("col")
        self.ta, self.col = ta, col
        self.y_hi, self.x, self.core = ta // 8, (ta // 2) % 4, ta % 2
        self.y_lo, self.z = col // 4, col % 4
        self.y = self.y_hi * 2 + self.y_lo

    def device(self, y_hi=None, x=None, core=None, y_lo=None, z=None):
        y_hi = self.y_hi if y_hi is None else y_hi
        x = self.x if x is None else x
        core = self.core if core is None else core
        y_lo = self.y_lo if y_lo is None else y_lo
        z = self.z if z is None else z
        return (y_hi * 8 + x * 2 + core, y_lo * 4 + z)

    def along(self, axis, step):
        if axis == "x":
            at = (self.x + step) % 4
            return self.device(x=at), at
        if axis == "z":
            at = (self.z + step) % 4
            return self.device(z=at), at
        at = (self.y + step) % 4
        return self.device(y_hi=at // 2, y_lo=at % 2), (at % 2) * 2 + at // 2


def greet(place):
    barrier = pltpu.get_barrier_semaphore()
    count = 1
    pl.semaphore_signal(barrier, inc=1, device_id=place.device(core=1 - place.core), device_id_type=MESH)
    for axis in ("x", "y", "z"):
        for step in (1, 2, 3):
            pl.semaphore_signal(barrier, inc=1, device_id=place.along(axis, step)[0], device_id_type=MESH)
            count += 1
    for step in (1, 2, 3):
        target = place.device(y_hi=1 - place.y_hi, x=(place.x + step) % 4)
        pl.semaphore_signal(barrier, inc=1, device_id=target, device_id_type=MESH)
        count += 1
    pl.semaphore_wait(barrier, count)


def lhs_block(at_ref, part, slot, second):
    if part == 0:
        block = at_ref[second // 2, :, second % 2, slot]
    elif part == 1:
        block = at_ref[slot // 2, second, slot % 2]
    else:
        block = at_ref[:, slot, :, second]
    return block.reshape(-1, block.shape[-1])


def chunk_product(at_ref, g_ref, part, slot, tile, width, emit):
    depth = at_ref.shape[4]
    right = g_ref[:, tile * LANES : (tile + width) * LANES]
    group = 1 if depth >= 64 else 4
    for base in range(0, 4, group):
        left = [lhs_block(at_ref, part, slot, base + i) for i in range(group)]
        left = left[0] if group == 1 else jnp.concatenate(left, axis=0)
        product = jnp.dot(left, right, preferred_element_type=jnp.float32)
        for column in range(width):
            emit(
                tile + column,
                base,
                group,
                product[:, column * LANES : (column + 1) * LANES].reshape(group, 4, depth, LANES),
            )


class Reduction:
    def __init__(self, place, index, shares, refs, sems):
        self.place, self.index, self.refs, self.sems = place, index, refs, sems
        self.bounds, start = [], 0
        for share in shares:
            self.bounds.append((start, start + share))
            start += share

    def load(self):
        r, s, i, core = self.refs, self.sems, self.index, self.place.core
        tokens = r["at_in"].shape[-1]
        half = r["g"].shape[1]
        mine = pl.ds(pl.multiple_of(core * half, LANES), half)
        other = pl.ds(pl.multiple_of((1 - core) * half, LANES), half)
        partner = self.place.device(core=1 - core)
        local = [
            pltpu.make_async_copy(r["at_in"], r["at"].at[:, :, :, :, :, :tokens], s["local"].at[i, 0]),
            pltpu.make_async_copy(r["g_in"].at[:, mine], r["g"].at[:tokens], s["local"].at[i, 1]),
        ]
        remote = [
            pltpu.make_async_remote_copy(
                r["at_in"], r["at"].at[:, :, :, :, :, tokens:], s["ex_send"].at[i, 0], s["ex_recv"].at[i, 0],
                device_id=partner, device_id_type=MESH,
            ),
            pltpu.make_async_remote_copy(
                r["g_in"].at[:, other], r["g"].at[tokens:], s["ex_send"].at[i, 1], s["ex_recv"].at[i, 1],
                device_id=partner, device_id_type=MESH,
            ),
        ]
        for copy in remote + local:
            copy.start()
        self.loads = (local, remote)

    def loaded(self):
        for copy in self.loads[0]:
            copy.wait()
        for copy in self.loads[1]:
            copy.wait_recv()

    def copy(self, part, stage, step):
        r, s, i = self.refs, self.sems, self.index
        low, high = self.bounds[part]
        device, slot = self.place.along(ORDERS[part][stage], step)
        if stage == 0:
            source = r["s1"].at[step - 1, low:high]
            target = r["r1"].at[step - 1, low:high]
        elif stage == 1:
            source = r["r1"].at[0, low:high, slot]
            target = r["r2"].at[step - 1, low:high]
        else:
            source = r["r2"].at[0, low:high, slot]
            target = r["r3"].at[step - 1, low:high]
        return pltpu.make_async_remote_copy(
            source, target, s["send"].at[i, part, stage, step - 1], s["recv"].at[i, part, stage, step - 1],
            device_id=device, device_id_type=MESH,
        )

    def first(self):
        r = self.refs
        for part in range(3):
            low, high = self.bounds[part]

            def one(step, _, part=part, low=low, high=high):
                slot = self.place.along(ORDERS[part][0], step)[1]

                def emit(tile, base, group, value):
                    r["s1"][step - 1, tile, base : base + group] = value.astype(jnp.bfloat16)

                for tile in range(low, high, 2):
                    chunk_product(r["at"], r["g"], part, slot, tile, min(2, high - tile), emit)
                self.copy(part, 0, step).start()
                return _

            lax.fori_loop(1, 4, one, 0)

    def second(self):
        r = self.refs
        for part in range(3):
            low, high = self.bounds[part]
            slot = self.place.along(ORDERS[part][0], 0)[1]
            for step in (1, 2, 3):
                self.copy(part, 0, step).wait_recv()

            def emit(tile, base, group, value):
                at = slice(base, base + group)
                total = value
                for i in range(3):
                    total = total + r["r1"][i, tile, at].astype(jnp.float32)
                r["r1"][0, tile, at] = total.astype(jnp.bfloat16)

            for tile in range(low, high, 2):
                chunk_product(r["at"], r["g"], part, slot, tile, min(2, high - tile), emit)
            for step in (1, 2, 3):
                self.copy(part, 1, step).start()

    def third(self):
        r = self.refs
        for part in range(3):
            low, high = self.bounds[part]
            slot = self.place.along(ORDERS[part][1], 0)[1]
            for step in (1, 2, 3):
                self.copy(part, 1, step).wait_recv()

            for tile in range(low, high):
                total = r["r1"][0, tile, slot].astype(jnp.float32)
                for i in range(3):
                    total = total + r["r2"][i, tile].astype(jnp.float32)
                r["r2"][0, tile] = total.astype(jnp.bfloat16)
            for step in (1, 2, 3):
                self.copy(part, 2, step).start()

    def mine(self):
        return self.place.y_hi * 4 + self.place.x

    def gather_copy(self, y_hi, x, slot):
        r, s, i, place = self.refs, self.sems, self.index, self.place
        block = r["ag"].at[slot, place.core]
        return pltpu.make_async_remote_copy(
            block, block, s["ag_send"].at[i, y_hi * 4 + x], s["ag_recv"].at[i, slot],
            device_id=place.device(y_hi=y_hi, x=x), device_id_type=MESH,
        )

    def others(self):
        place = self.place
        for y_step in (0, 1):
            y_hi = (place.y_hi + y_step) % 2
            for x_step in range(4):
                if y_step or x_step:
                    yield y_hi, (place.x + x_step) % 4

    def fourth(self):
        r = self.refs
        for part in range(3):
            low, high = self.bounds[part]
            slot = self.place.along(ORDERS[part][2], 0)[1]
            for step in (1, 2, 3):
                self.copy(part, 2, step).wait_recv()
            for tile in range(low, high):
                total = r["r2"][0, tile, slot].astype(jnp.float32)
                for i in range(3):
                    total = total + r["r3"][i, tile].astype(jnp.float32)
                r["ag"][self.mine(), self.place.core, tile] = total.astype(jnp.bfloat16)
        for y_hi, x in self.others():
            self.gather_copy(y_hi, x, self.mine()).start()

    def cross_copy(self):
        r, s, i, core = self.refs, self.sems, self.index, self.place.core
        block = r["ag"].at[:, core]
        return pltpu.make_async_remote_copy(
            block, block, s["cross"].at[i, 0], s["cross"].at[i, 1],
            device_id=self.place.device(core=1 - core), device_id_type=MESH,
        )

    def fifth(self):
        for y_hi, x in self.others():
            self.gather_copy(y_hi, x, y_hi * 4 + x).wait_recv()
        self.cross_copy().start()

    def out_copy(self):
        return pltpu.make_async_copy(self.refs["ag"], self.refs["out"], self.sems["local"].at[self.index, 2])

    def sixth(self):
        self.cross_copy().wait_recv()
        self.out_copy().start()

    def finish(self):
        self.out_copy().wait()
        self.cross_copy().wait_send()
        for copy in self.loads[1]:
            copy.wait_send()
        for y_hi, x in self.others():
            self.gather_copy(y_hi, x, self.mine()).wait_send()
        for part in range(3):
            for stage in range(3):
                for step in (1, 2, 3):
                    self.copy(part, stage, step).wait_send()


def gradient_kernel(*refs):
    count = len(MATRICES)
    names = ("at_in", "g_in", "out", "at", "g", "s1", "r1", "r2", "r3", "ag")
    groups = {name: refs[i * count : (i + 1) * count] for i, name in enumerate(names)}
    sem_names = ("local", "ex_send", "ex_recv", "send", "recv", "ag_send", "ag_recv", "cross")
    sems = dict(zip(sem_names, refs[len(names) * count :]))
    place = Place()
    work = [
        Reduction(place, i, shares, {name: groups[name][i] for name in names}, sems)
        for i, (_, shares) in enumerate(MATRICES)
    ]
    greet(place)
    for one in work:
        one.load()
    stages = ("first", "second", "third", "fourth", "fifth", "sixth")
    for turn in range(count + len(stages) - 1):
        for lag, stage in enumerate(stages):
            if 0 <= turn - lag < count:
                if lag == 0:
                    work[turn].loaded()
                getattr(work[turn - lag], stage)()
    for one in work:
        one.finish()


def reduce_gradients(pairs):
    lefts, rights, outs, scratch = [], [], [], {n: [] for n in ("at", "g", "s1", "r1", "r2", "r3", "ag")}
    bf16 = jnp.bfloat16
    flops = 0
    for activation, gradient in pairs:
        tokens, k = activation.shape
        n = gradient.shape[1]
        depth, tiles = k // 64, n // 2 // LANES
        flops += 2 * tokens * k * n
        lefts.append(activation.T.reshape(2, 4, 2, 4, depth, tokens))
        rights.append(gradient)
        outs.append(jax.ShapeDtypeStruct((8, 2, tiles, depth, LANES), bf16))
        scratch["at"].append(pltpu.VMEM((2, 4, 2, 4, depth, 2 * tokens), bf16))
        scratch["g"].append(pltpu.VMEM((2 * tokens, n // 2), bf16))
        scratch["s1"].append(pltpu.VMEM((3, tiles, 4, 4, depth, LANES), bf16))
        scratch["r1"].append(pltpu.VMEM((3, tiles, 4, 4, depth, LANES), bf16))
        scratch["r2"].append(pltpu.VMEM((3, tiles, 4, depth, LANES), bf16))
        scratch["r3"].append(pltpu.VMEM((3, tiles, depth, LANES), bf16))
        scratch["ag"].append(pltpu.VMEM((8, 2, tiles, depth, LANES), bf16))
    count = len(pairs)
    sem = pltpu.SemaphoreType.DMA
    results = pl.pallas_call(
        gradient_kernel,
        out_shape=outs,
        in_specs=[ANY] * (2 * count),
        out_specs=[ANY] * count,
        scratch_shapes=[one for group in scratch.values() for one in group]
        + [
            sem((count, 3)),
            sem((count, 2)),
            sem((count, 2)),
            sem((count, 3, 3, 3)),
            sem((count, 3, 3, 3)),
            sem((count, 8)),
            sem((count, 8)),
            sem((count, 2)),
        ],
        compiler_params=pltpu.CompilerParams(
            collective_id=0, has_side_effects=True, vmem_limit_bytes=58 * 2**20
        ),
        cost_estimate=pl.CostEstimate(flops=flops, bytes_accessed=40 * 2**20, transcendentals=0),
        name="gradient_sums",
    )(*lefts, *rights)
    finished = []
    for value in results:
        rows, cores, tiles, depth, lanes = value.shape
        value = value.transpose(0, 3, 1, 2, 4).reshape(rows * depth, cores * tiles * lanes)
        finished.append(value.astype(jnp.float32))
    return finished


def from_partner(value, axis):
    pairs = [(source, source ^ 1) for source in range(lax.axis_size(axis))]
    return lax.ppermute(value, axis, pairs)


def normalize(rows, gain, shift):
    mean_row = jnp.mean(rows, axis=-1, keepdims=True)
    centered = rows - mean_row
    variance = jnp.mean(centered * centered, axis=-1, keepdims=True)
    return centered * lax.rsqrt(variance + EPSILON) * gain + shift


def norm_backward(rows, gain, shift, gradient):
    unused_value, pullback = jax.vjp(normalize, rows, gain, shift)
    return pullback(gradient)


def project(activation, weight):
    return jnp.einsum("...k,kn->...n", activation, weight, preferred_element_type=jnp.float32)


def project_back(gradient, weight):
    return jnp.einsum("...n,kn->...k", gradient, weight, preferred_element_type=jnp.float32)


def score_rows(queries, key_rows, visible):
    scores = jnp.einsum("bqhe,bkhe->bhqk", queries, key_rows, preferred_element_type=jnp.float32)
    return jnp.where(visible, scores * queries.shape[-1] ** (-0.5), MASKED_SCORE)


def attend_forward(queries, key_rows, value_rows, visible):
    scores = score_rows(queries, key_rows, visible)
    row_max = jnp.max(scores, axis=-1, keepdims=True)
    weights = jnp.exp(scores - row_max)
    row_total = jnp.sum(weights, axis=-1, keepdims=True)
    probability = (weights / row_total).astype(jnp.bfloat16)
    context = jnp.einsum("bhqk,bkhe->bqhe", probability, value_rows, preferred_element_type=jnp.float32)
    return (context.astype(jnp.bfloat16), row_max + jnp.log(row_total))


def attend_backward(queries, key_rows, value_rows, visible, log_total, context_grad):
    scale_factor = queries.shape[-1] ** (-0.5)
    probability = jnp.exp(score_rows(queries, key_rows, visible) - log_total)
    prob_grad = jnp.einsum("bqhe,bkhe->bhqk", context_grad, value_rows, preferred_element_type=jnp.float32)
    row_delta = jnp.sum(probability * prob_grad, axis=-1, keepdims=True)
    score_grad = (probability * (prob_grad - row_delta)).astype(jnp.bfloat16)
    low_prob = probability.astype(jnp.bfloat16)
    query_grad = jnp.einsum("bhqk,bkhe->bqhe", score_grad, key_rows, preferred_element_type=jnp.float32)
    key_grad = jnp.einsum("bhqk,bqhe->bkhe", score_grad, queries, preferred_element_type=jnp.float32)
    value_grad = jnp.einsum("bhqk,bqhe->bkhe", low_prob, context_grad, preferred_element_type=jnp.float32)
    return (query_grad * scale_factor, key_grad * scale_factor, value_grad)


def to_positions(rows):
    width = rows.shape[-1]
    blocks = rows.reshape(2, 16, 8, width).swapaxes(0, 1)
    blocks = lax.all_to_all(blocks, "ta", split_axis=0, concat_axis=0, tiled=True)
    return blocks.reshape(8, 2, 16, width).swapaxes(0, 1).reshape(2, 128, width)


def to_frames(rows):
    width = rows.shape[-1]
    blocks = rows.reshape(2, 8, 16, width).swapaxes(0, 1).reshape(16, 2, 8, width)
    blocks = lax.all_to_all(blocks, "ta", split_axis=0, concat_axis=0, tiled=True)
    return blocks.swapaxes(0, 1).reshape(2, 128, width)


def body(
    big_tokens,
    small_tokens,
    big_actions,
    small_actions,
    big_order,
    small_order,
    small_live,
    action_table,
    norm1_gain,
    norm1_bias,
    spatial_qkv,
    spatial_out,
    spatial_out_bias,
    norm2_gain,
    norm2_bias,
    temporal_qkv,
    temporal_out,
    temporal_out_bias,
    norm3_gain,
    norm3_bias,
    ffn_in,
    ffn_in_bias,
    ffn_out,
    ffn_out_bias,
    big_cotangent,
    small_cotangent,
):
    f32, bf16 = jnp.float32, jnp.bfloat16
    width = big_tokens.shape[2]
    heads = width // HEAD_DIM
    ta = lax.axis_index("ta")
    frame = ta // 2
    gain_one, shift_one = norm1_gain.astype(f32), norm1_bias.astype(f32)
    gain_two, shift_two = norm2_gain.astype(f32), norm2_bias.astype(f32)
    gain_three, shift_three = norm3_gain.astype(f32), norm3_bias.astype(f32)

    def merge(big, small):
        return jnp.concatenate([big.reshape(1, 128, -1), small.reshape(1, 128, -1)], axis=0)

    alive = jnp.repeat(small_live.astype(f32), 32)
    alive = jnp.concatenate([jnp.ones((128,), f32), alive]).reshape(2, 128, 1)
    actions = jnp.concatenate([big_actions, small_actions], axis=0)
    chosen = jnp.arange(8)[None, :] == frame
    action_now = jnp.sum(jnp.where(chosen, actions, 0), axis=1)
    pick = action_now[:, None] == jnp.arange(8)[None, :]
    embedding = jnp.dot(pick.astype(bf16), action_table, preferred_element_type=f32)
    tokens = merge(big_tokens, small_tokens).astype(f32)
    embedded = jnp.concatenate([jnp.repeat(embedding[:1], 128, axis=0), jnp.repeat(embedding[1:], 32, axis=0)], axis=0)
    resid_zero = tokens + embedded.reshape(2, 128, width)
    slots = jnp.arange(128) // 32
    same_slot = slots[:, None] == jnp.concatenate([slots, slots])[None, :]
    spatial_mask = jnp.stack([jnp.ones_like(same_slot), same_slot])[:, None]
    mine = jnp.arange(4)[:, None] == ta // 4
    small_rank = jnp.sum(jnp.where(mine, small_order, 0), axis=0)
    rank = jnp.stack([big_order[0], small_rank], axis=1)
    rank = jnp.repeat(rank, 8, axis=1).reshape(128)
    spot = jnp.arange(128) % 16
    temporal_mask = (spot[:, None] == spot[None, :]) & (rank[None, :] <= rank[:, None])
    temporal_mask = temporal_mask[None, None]

    def split_heads(rows):
        return rows.reshape(rows.shape[0], rows.shape[1], heads, HEAD_DIM)

    normed_one = normalize(resid_zero, gain_one, shift_one).astype(bf16)
    packed_one = project(normed_one, spatial_qkv).astype(bf16)
    far = from_partner(packed_one[:, :, width:], "ta")
    joined = jnp.concatenate([packed_one[:, :, width:], far], axis=1)
    q1, k1, v1 = split_heads(packed_one[:, :, :width]), split_heads(joined[:, :, :width]), split_heads(joined[:, :, width:])
    context_one, log_one = attend_forward(q1, k1, v1, spatial_mask)
    context_one = context_one.reshape(2, 128, width)
    resid_one = resid_zero + project(context_one, spatial_out) + spatial_out_bias.astype(f32)
    normed_two = normalize(resid_one, gain_two, shift_two).astype(bf16)
    arranged = to_positions(normed_two)
    packed_two = project(arranged, temporal_qkv).astype(bf16)
    q2, k2, v2 = (split_heads(packed_two[:, :, i * width : (i + 1) * width]) for i in range(3))
    context_two, log_two = attend_forward(q2, k2, v2, temporal_mask)
    context_two = to_frames(context_two.reshape(2, 128, width))
    resid_two = resid_one + project(context_two, temporal_out) + temporal_out_bias.astype(f32)
    normed_three = normalize(resid_two, gain_three, shift_three).astype(bf16)
    hidden = project(normed_three, ffn_in) + ffn_in_bias.astype(f32)
    activated = jax.nn.gelu(hidden).astype(bf16)
    result = (resid_two + project(activated, ffn_out) + ffn_out_bias.astype(f32)) * alive
    result = result.astype(bf16)

    grad_three = merge(big_cotangent, small_cotangent).astype(f32) * alive
    grad_three_low = grad_three.astype(bf16)
    gelu_value, gelu_pull = jax.vjp(jax.nn.gelu, hidden)
    hidden_grad = gelu_pull(project_back(grad_three_low, ffn_out))[0]
    hidden_low = hidden_grad.astype(bf16)
    rows_grad, gain_three_grad, shift_three_grad = norm_backward(
        resid_two, gain_three, shift_three, project_back(hidden_low, ffn_in)
    )
    grad_two = grad_three + rows_grad
    grad_two_low = grad_two.astype(bf16)
    context_grad = to_positions(project_back(grad_two_low, temporal_out).astype(bf16))
    grads = attend_backward(q2, k2, v2, temporal_mask, log_two, split_heads(context_grad))
    packed_two_grad = jnp.concatenate([g.reshape(2, 128, width) for g in grads], axis=-1).astype(bf16)
    normed_two_grad = to_frames(project_back(packed_two_grad, temporal_qkv).astype(bf16)).astype(f32)
    rows_grad, gain_two_grad, shift_two_grad = norm_backward(resid_one, gain_two, shift_two, normed_two_grad)
    grad_one = grad_two + rows_grad
    grad_one_low = grad_one.astype(bf16)
    context_grad = project_back(grad_one_low, spatial_out).astype(bf16)
    query_grad, key_grad, value_grad = attend_backward(q1, k1, v1, spatial_mask, log_one, split_heads(context_grad))
    key_value = jnp.concatenate([key_grad.reshape(2, 256, width), value_grad.reshape(2, 256, width)], axis=-1)
    far = from_partner(key_value[:, 128:].astype(bf16), "ta").astype(f32)
    packed_one_grad = jnp.concatenate([query_grad.reshape(2, 128, width), key_value[:, :128] + far], axis=-1).astype(bf16)
    rows_grad, gain_one_grad, shift_one_grad = norm_backward(
        resid_zero, gain_one, shift_one, project_back(packed_one_grad, spatial_qkv)
    )
    grad_zero = grad_one + rows_grad
    frame_sums = jnp.concatenate(
        [jnp.sum(grad_zero[0], axis=0, keepdims=True), jnp.sum(grad_zero[1].reshape(4, 32, width), axis=1)], axis=0
    )
    table_grad = jnp.sum(jnp.where(pick[:, :, None], frame_sums[:, None, :], 0.0), axis=0)

    def rows_sum(value):
        return jnp.sum(value, axis=(0, 1)).reshape(-1, width)

    small = jnp.concatenate(
        [
            table_grad,
            gain_one_grad[None],
            shift_one_grad[None],
            rows_sum(grad_one),
            gain_two_grad[None],
            shift_two_grad[None],
            rows_sum(grad_two),
            gain_three_grad[None],
            shift_three_grad[None],
            rows_sum(hidden_grad),
            rows_sum(grad_three),
        ],
        axis=0,
    )
    small = lax.psum(small, ("ta", "col"))

    def flat(value):
        return value.reshape(256, value.shape[-1])

    g_fout, g_fin, g_tout, g_tqkv, g_sout, g_sqkv = reduce_gradients(
        [
            (flat(activated), flat(grad_three_low)),
            (flat(normed_three), flat(hidden_low)),
            (flat(context_two), flat(grad_two_low)),
            (flat(arranged), flat(packed_two_grad)),
            (flat(context_one), flat(grad_one_low)),
            (flat(normed_one), flat(packed_one_grad)),
        ]
    )
    return (
        result[0].reshape(1, 128, width),
        result[1].reshape(4, 32, width),
        grad_zero[0].reshape(1, 128, width),
        grad_zero[1].reshape(4, 32, width),
        small[:8],
        small[8],
        small[9],
        g_sqkv,
        g_sout,
        small[10],
        small[11],
        small[12],
        g_tqkv,
        g_tout,
        small[13],
        small[14],
        small[15],
        g_fin,
        small[16:20].reshape(-1),
        g_fout,
        small[20],
    )


def solution(mesh):
    spread, by_col = P("col", "ta", None), P("col", None)
    return jax.shard_map(
        body,
        mesh=mesh,
        in_specs=(spread, spread, by_col, by_col, by_col, by_col, P("col")) + (P(),) * 17 + (spread, spread),
        out_specs=(spread,) * 4
        + (P(),) * 3
        + (by_col, by_col, P(), P(), P(), by_col, by_col, P(), P(), P(), by_col, P(), by_col, P()),
        check_vma=False,
    )
```

```python
import functools
from types import SimpleNamespace as Names

import jax
import jax.numpy as jnp
from jax import lax
from jax.experimental import pallas as pl
from jax.experimental.pallas import tpu as pltpu
from jax.sharding import PartitionSpec as P

HEAD_DIM = 64
EPSILON = 1e-05
MASKED_SCORE = -1e30
MESH = pl.DeviceIdType.MESH
ANY = pl.BlockSpec(memory_space=pl.ANY)
VMEM = pl.BlockSpec(memory_space=pltpu.VMEM)
SMEM = pl.BlockSpec(memory_space=pltpu.SMEM)
LANES = 128
F32, BF16 = jnp.float32, jnp.bfloat16
ROWS, WIDTH, HIDDEN = 256, 1024, 4096
PAIRS = WIDTH // LANES
HIDE = 512

SP_KEY, SP_VALUE, SP_QUERY, SP_ROWS = 1024, 1536, 2048, 2304
TP_KEY, TP_VALUE, TP_QUERY, TP_ROWS = 512, 768, 1024, 1280

ORDERS = (("x", "y", "z"), ("y", "z", "x"), ("z", "x", "y"))
MATRICES = (
    (HIDDEN, WIDTH, (1, 1, 2)),
    (WIDTH, HIDDEN, (6, 6, 4)),
    (WIDTH, WIDTH, (1, 2, 1)),
    (WIDTH, 3 * WIDTH, (4, 4, 4)),
    (WIDTH, WIDTH, (2, 1, 1)),
    (WIDTH, 3 * WIDTH, (4, 4, 4)),
)
SEND_UNITS = (0, 16, 12, 0, 28, 16)


class Place:
    def __init__(self):
        ta, col = lax.axis_index("ta"), lax.axis_index("col")
        self.ta, self.col = ta, col
        self.y_hi, self.x, self.core = ta // 8, (ta // 2) % 4, ta % 2
        self.y_lo, self.z = col // 4, col % 4
        self.y = self.y_hi * 2 + self.y_lo
        self.partner = self.device(core=1 - self.core)

    def device(self, y_hi=None, x=None, core=None, y_lo=None, z=None):
        y_hi = self.y_hi if y_hi is None else y_hi
        x = self.x if x is None else x
        core = self.core if core is None else core
        y_lo = self.y_lo if y_lo is None else y_lo
        z = self.z if z is None else z
        return (y_hi * 8 + x * 2 + core, y_lo * 4 + z)

    def along(self, axis, step):
        if axis == "x":
            at = (self.x + step) % 4
            return self.device(x=at), at
        if axis == "z":
            at = (self.z + step) % 4
            return self.device(z=at), at
        at = (self.y + step) % 4
        return self.device(y_hi=at // 2, y_lo=at % 2), (at % 2) * 2 + at // 2

    def fellow(self, step):
        ta = (self.ta + step) % 16
        return (ta, self.col), ta


def greet(place, whole):
    barrier = pltpu.get_barrier_semaphore()

    def one(step, carry):
        pl.semaphore_signal(barrier, inc=1, device_id=place.fellow(step)[0], device_id_type=MESH)
        return carry

    lax.fori_loop(1, 16, one, 0)
    count = 15
    if whole:
        for axis, step in (("y", 1), ("y", 3), ("z", 1), ("z", 2), ("z", 3)):
            pl.semaphore_signal(barrier, inc=1, device_id=place.along(axis, step)[0], device_id_type=MESH)
            count += 1
    pl.semaphore_wait(barrier, count)


def remote(source, target, send, recv, device):
    return pltpu.make_async_remote_copy(source, target, send, recv, device_id=device, device_id_type=MESH)


def dot(left, right):
    return jnp.dot(left, right, preferred_element_type=F32)


def dot_nt(left, right):
    return lax.dot_general(left, right, (((1,), (1,)), ((), ())), preferred_element_type=F32)


def dot_tn(left, right):
    return lax.dot_general(left, right, (((0,), (0,)), ((), ())), preferred_element_type=F32)


def rows16(step):
    return pl.ds(pl.multiple_of(step * 16, 16), 16)


def lanes(step, width):
    return pl.ds(pl.multiple_of(step * width, width), width)


def interleave(big, small):
    width = big.shape[-1]
    pair = [one.reshape(-1, 1, 8, width) for one in (big, small)]
    return jnp.concatenate(pair, axis=1).reshape(-1, width)


def family(rows, which):
    width = rows.shape[-1]
    return rows.reshape(-1, 2, 8, width)[:, which].reshape(-1, width)


def half_masks(rows):
    lane = lax.broadcasted_iota(jnp.int32, (rows, LANES), 1)
    return lane < HEAD_DIM


def by_head(value, low):
    zero = jnp.zeros_like(value)
    return jnp.where(low, value, zero), jnp.where(low, zero, value)


def statistics(rows):
    mean = jnp.mean(rows, axis=-1, keepdims=True)
    centered = rows - mean
    variance = jnp.mean(centered * centered, axis=-1, keepdims=True)
    scale = lax.rsqrt(variance + EPSILON)
    return centered * scale, scale


def norm_forward(source, gain, shift, target, normals, scales, after=None):
    def one(step, carry):
        rows = rows16(step)
        normal, scale = statistics(source[rows])
        target[rows] = (normal * gain + shift).astype(BF16)
        normals[rows] = normal
        scales[rows] = jnp.broadcast_to(scale, (16, LANES))
        if after is not None:
            after(step)
        return carry

    lax.fori_loop(0, 16, one, 0, unroll=2)


def transpose_into(source, target):
    def one(step, carry):
        target[step] = source[:, lanes(step, LANES)].T
        return carry

    lax.fori_loop(0, PAIRS, one, 0)


class Swap:
    def __init__(self, place, send, recv, sems, index, to_positions, columns=slice(0, WIDTH)):
        self.place, self.send, self.recv, self.sems, self.index = place, send, recv, sems, index
        self.to_positions, self.columns = to_positions, columns

    def rows(self, ta):
        frames = rows16(ta)
        positions = rows16((ta % 2) * 8 + ta // 2)
        return (frames, positions) if self.to_positions else (positions, frames)

    def copy(self, step):
        device, ta = self.place.fellow(step)
        source = self.send.at[self.rows(ta)[0], self.columns]
        target = self.recv.at[self.rows(self.place.ta)[1], self.columns]
        return remote(source, target, self.sems.at[self.index, 0, step], self.sems.at[self.index, 1, step], device)

    def own(self):
        rows = self.rows(self.place.ta)
        source, target = self.send.at[rows[0], self.columns], self.recv.at[rows[1], self.columns]
        return pltpu.make_async_copy(source, target, self.sems.at[self.index, 0, 0])

    def start_block(self, ta):
        step = (ta - self.place.ta + 16) % 16

        @pl.when(step > 0)
        def _():
            self.copy(step).start()

        @pl.when(step == 0)
        def _():
            self.own().start()

    def start(self):
        def one(step, carry):
            self.copy(step).start()
            return carry

        lax.fori_loop(1, 16, one, 0)
        self.own().start()

    def wait(self):
        def one(step, carry):
            self.copy(step).wait_recv()
            return carry

        self.own().wait()
        lax.fori_loop(1, 16, one, 0)

    def sent(self):
        def one(step, carry):
            self.copy(step).wait_send()
            return carry

        lax.fori_loop(1, 16, one, 0)


HALVES = (slice(0, WIDTH // 2), slice(WIDTH // 2, WIDTH))


FORWARD_OUTS = dict(
    big_out=((128, WIDTH), BF16),
    small_out=((128, WIDTH), BF16),
    normal1=((ROWS, WIDTH), F32),
    normal2=((ROWS, WIDTH), F32),
    normal3=((ROWS, WIDTH), F32),
    scale1=((ROWS, LANES), F32),
    scale2=((ROWS, LANES), F32),
    scale3=((ROWS, LANES), F32),
    normed1_t=((PAIRS, LANES, ROWS), BF16),
    context1_t=((PAIRS, LANES, ROWS), BF16),
    normed2_t=((PAIRS, LANES, ROWS), BF16),
    context2_t=((PAIRS, LANES, ROWS), BF16),
    normed3_t=((PAIRS, LANES, ROWS), BF16),
    activated_t=((PAIRS, HIDE, ROWS), BF16),
    spatial=((PAIRS, SP_ROWS, LANES), BF16),
    temporal=((PAIRS, TP_ROWS, LANES), BF16),
    slope=((PAIRS, ROWS, HIDE), BF16),
)
FORWARD_WORK = dict(
    w_sqkv=((WIDTH, 3 * WIDTH), BF16),
    w_sout=((WIDTH, WIDTH), BF16),
    w_tqkv=((WIDTH, 3 * WIDTH), BF16),
    w_tout=((WIDTH, WIDTH), BF16),
    w_fin=((WIDTH, HIDDEN), BF16),
    w_fout=((HIDDEN, WIDTH), BF16),
    normed=((ROWS, WIDTH), BF16),
    context=((ROWS, WIDTH), BF16),
    arranged=((ROWS, WIDTH), BF16),
    context_send=((ROWS, WIDTH), BF16),
    context_back=((ROWS, WIDTH), BF16),
    normed3=((ROWS, WIDTH), BF16),
    total=((ROWS, WIDTH), F32),
    hidden=((ROWS, HIDE), F32),
    params=((16, WIDTH), F32),
    inner_bias=((PAIRS, HIDE), F32),
    table=((8, WIDTH), F32),
)


def named(keys, refs):
    return Names(**{key: refs.pop(0) for key in keys})


def forward_kernel(in_keys, vector_count, weight_keys, *refs):
    refs = list(refs)
    ins = named(in_keys, refs)
    vectors = [refs.pop(0) for _ in range(vector_count)]
    weights = named(weight_keys, refs)
    outs, keep, work = named(FORWARD_OUTS, refs), named(FORWARD_OUTS, refs), named(FORWARD_WORK, refs)
    w_sems, out_sems, swap_sems, far_sems = refs
    place = Place()
    params = work.params

    def param(row):
        return params[row : row + 1]

    loads = Names()
    for i, key in enumerate(weight_keys):
        setattr(loads, key, pltpu.make_async_copy(getattr(weights, key), getattr(work, key), w_sems.at[i]))
    loads.w_sqkv.start()
    for row, vector in enumerate(vectors):
        params[row : row + 1] = vector[...].astype(F32).reshape(1, WIDTH)
    for row in range(PAIRS):
        at = slice(row * HIDE, row * HIDE + HIDE)
        work.inner_bias[row : row + 1] = ins.inner_bias[at].astype(F32).reshape(1, HIDE)
    work.table[...] = ins.table[...].astype(F32)
    frame = place.ta // 2
    copies = []

    def save(source, target):
        copy = pltpu.make_async_copy(source, target, out_sems.at[len(copies)])
        copy.start()
        copies.append(copy)

    resid0, resid1, resid2 = keep.normal2, keep.normal3, work.total
    big_row = work.table[pl.ds(ins.big_actions[0, frame], 1)]

    def start_rows(step, carry):
        near = pl.ds(pl.multiple_of(step * 16, 16), 16)
        big = ins.big[near].astype(F32) + big_row
        small = ins.small[near].astype(F32) + work.table[pl.ds(ins.small_actions[step // 2, frame], 1)]
        rows = pl.ds(pl.multiple_of(step * 32, 32), 32)
        merged = interleave(big, small)
        resid0[rows] = merged
        normal, scale = statistics(merged)
        work.normed[rows] = (normal * param(0) + param(1)).astype(BF16)
        keep.normal1[rows] = normal
        keep.scale1[rows] = jnp.broadcast_to(scale, (32, LANES))
        return carry

    lax.fori_loop(0, 8, start_rows, 0)
    save(keep.normal1, outs.normal1)
    save(keep.scale1, outs.scale1)
    greet(place, False)

    spatial = keep.spatial
    loads.w_sqkv.wait()
    for key in weight_keys[1:]:
        getattr(loads, key).start()

    def spatial_project(column, base, per_family, scale):
        def one(step, carry):
            at = column + step
            value = dot(work.normed[...], work.w_sqkv[:, lanes(at, 256)]) * scale
            for which in range(2):
                one_family = family(value, which).astype(BF16)
                rows = pl.ds(base + which * per_family, 128)
                spatial[step * 2, rows] = one_family[:, :LANES]
                spatial[step * 2 + 1, rows] = one_family[:, LANES:]
            return carry

        lax.fori_loop(0, 4, one, 0)

    spatial_project(4, SP_KEY, 256, 1.0)
    spatial_project(8, SP_VALUE, 256, 1.0)
    far = []
    for i, base in enumerate((SP_KEY, SP_KEY + 256, SP_VALUE, SP_VALUE + 256)):
        far.append(
            remote(
                spatial.at[:, pl.ds(base, 128)], spatial.at[:, pl.ds(base + 128, 128)],
                far_sems.at[0, i], far_sems.at[1, i], place.partner,
            )
        )
    for copy in far:
        copy.start()
    spatial_project(0, SP_QUERY, 128, 0.125)
    transpose_into(work.normed, keep.normed1_t)
    save(keep.normed1_t, outs.normed1_t)
    for copy in far:
        copy.wait()

    low_q, low_k = half_masks(128), half_masks(256)
    key_slot = (lax.broadcasted_iota(jnp.int32, (256, 128), 0) % 128) // 32
    query_slot = lax.broadcasted_iota(jnp.int32, (256, 128), 1) // 32
    same_slot = key_slot == query_slot

    def softmax(scores):
        weights_ = jnp.exp(scores - jnp.max(scores, axis=0, keepdims=True))
        return (weights_ * (1.0 / jnp.sum(weights_, axis=0, keepdims=True))).astype(BF16)

    def spatial_pair(pair, carry):
        contexts = []
        for which in range(2):
            keys = spatial[pair, SP_KEY + which * 256 : SP_KEY + which * 256 + 256]
            values = spatial[pair, SP_VALUE + which * 256 : SP_VALUE + which * 256 + 256]
            queries = by_head(spatial[pair, SP_QUERY + which * 128 : SP_QUERY + which * 128 + 128], low_q)
            probs = []
            for head in range(2):
                scores = dot_nt(keys, queries[head])
                if which == 1:
                    scores = jnp.where(same_slot, scores, MASKED_SCORE)
                prob = softmax(scores)
                at = (which * 2 + head) * 256
                spatial[pair, at : at + 256] = prob
                probs.append(prob)
            contexts.append(
                dot_tn(jnp.concatenate(probs, axis=0), jnp.concatenate(by_head(values, low_k), axis=0))
            )
        work.context[:, lanes(pair, LANES)] = interleave(*contexts).astype(BF16)
        return carry

    lax.fori_loop(0, PAIRS, spatial_pair, 0)
    save(keep.spatial, outs.spatial)

    def project_into(source, weight, bias, before, target):
        def one(step, carry):
            at = lanes(step, 256)
            target[:, at] = dot(source[...], weight[:, at]) + params[bias : bias + 1, at] + before[:, at]
            return carry

        lax.fori_loop(0, WIDTH // 256, one, 0)

    loads.w_sout.wait()
    project_into(work.context, work.w_sout, 2, resid0, resid1)
    there = Swap(place, work.normed, work.arranged, swap_sems, 0, True)
    norm_forward(resid1, param(3), param(4), work.normed, keep.normal2, keep.scale2, there.start_block)
    save(keep.normal2, outs.normal2)
    save(keep.scale2, outs.scale2)
    transpose_into(work.context, keep.context1_t)
    save(keep.context1_t, outs.context1_t)
    loads.w_tqkv.wait()
    there.wait()

    temporal = keep.temporal

    def temporal_project(column, base, scale):
        def one(step, carry):
            value = dot(work.arranged[...], work.w_tqkv[:, lanes(column + step, 256)]) * scale
            value = value.astype(BF16)
            temporal[step * 2, base : base + ROWS] = value[:, :LANES]
            temporal[step * 2 + 1, base : base + ROWS] = value[:, LANES:]
            return carry

        lax.fori_loop(0, 4, one, 0)

    temporal_project(0, TP_QUERY, 0.125)
    temporal_project(4, TP_KEY, 1.0)
    temporal_project(8, TP_VALUE, 1.0)
    key_row = lax.broadcasted_iota(jnp.int32, (128, 128), 0)
    query_row = lax.broadcasted_iota(jnp.int32, (128, 128), 1)
    key_rank, query_rank = jnp.zeros_like(key_row), jnp.zeros_like(query_row)
    for at in range(8):
        big_rank, small_rank = ins.big_order[0, at], ins.small_order[place.ta // 4, at]
        key_rank = jnp.where(key_row // 16 == at, jnp.where(key_row % 16 < 8, big_rank, small_rank), key_rank)
        query_rank = jnp.where(query_row // 16 == at, jnp.where(query_row % 16 < 8, big_rank, small_rank), query_rank)
    seen = (key_row % 16 == query_row % 16) & (key_rank <= query_rank)

    def temporal_pair(pair, carry):
        contexts = []
        for half in range(2):
            keys = temporal[pair, TP_KEY + half * 128 : TP_KEY + half * 128 + 128]
            values = temporal[pair, TP_VALUE + half * 128 : TP_VALUE + half * 128 + 128]
            queries = by_head(temporal[pair, TP_QUERY + half * 128 : TP_QUERY + half * 128 + 128], low_q)
            probs = []
            for head in range(2):
                prob = softmax(jnp.where(seen, dot_nt(keys, queries[head]), MASKED_SCORE))
                at = (half * 2 + head) * 128
                temporal[pair, at : at + 128] = prob
                probs.append(prob)
            contexts.append(
                dot_tn(jnp.concatenate(probs, axis=0), jnp.concatenate(by_head(values, low_q), axis=0))
            )
        work.context_send[:, lanes(pair, LANES)] = jnp.concatenate(contexts, axis=0).astype(BF16)
        return carry

    back = [Swap(place, work.context_send, work.context_back, swap_sems, 1 + i, False, HALVES[i]) for i in range(2)]
    lax.fori_loop(0, PAIRS // 2, temporal_pair, 0)
    back[0].start()
    lax.fori_loop(PAIRS // 2, PAIRS, temporal_pair, 0)
    back[1].start()
    save(keep.temporal, outs.temporal)
    transpose_into(work.arranged, keep.normed2_t)
    save(keep.normed2_t, outs.normed2_t)
    loads.w_tout.wait()
    for i in range(2):
        back[i].wait()

        def add_half(step, carry, i=i):
            at = lanes(step, 256)
            value = dot(work.context_back[:, HALVES[i]], work.w_tout[HALVES[i], at])
            if i == 0:
                resid2[:, at] = value + params[5:6, at] + resid1[:, at]
            else:
                resid2[:, at] += value
            return carry

        lax.fori_loop(0, WIDTH // 256, add_half, 0)
    norm_forward(resid2, param(6), param(7), work.normed3, keep.normal3, keep.scale3)
    save(keep.normal3, outs.normal3)
    save(keep.scale3, outs.scale3)
    transpose_into(work.context_back, keep.context2_t)
    save(keep.context2_t, outs.context2_t)
    transpose_into(work.normed3, keep.normed3_t)
    save(keep.normed3_t, outs.normed3_t)

    total, hidden, slope = work.total, work.hidden, keep.slope
    total[...] += param(8)
    loads.w_fin.wait()
    loads.w_fout.wait()
    root = 0.7978845608028654

    def feed(step, carry):
        hidden[...] = dot(work.normed3[...], work.w_fin[:, lanes(step, HIDE)])

        def some(part, inner):
            rows = pl.ds(pl.multiple_of(part * 32, 32), 32)
            value = hidden[rows] + work.inner_bias[pl.ds(step, 1)]
            square = value * value
            bent = jnp.tanh(root * value * (1.0 + 0.044715 * square))
            half = 0.5 * (1.0 + bent)
            work.context_send[rows, :HIDE] = (value * half).astype(BF16)
            rise = half + 0.5 * value * (1.0 - bent * bent) * (root * (1.0 + 0.134145 * square))
            slope[step, rows] = rise.astype(BF16)
            return inner

        lax.fori_loop(0, 8, some, 0)
        active = work.context_send[:, :HIDE]
        for block in range(HIDE // LANES):
            at = slice(block * LANES, block * LANES + LANES)
            keep.activated_t[step, at] = work.context_send[:, at].T
        down = work.w_fout.at[pl.ds(pl.multiple_of(step * HIDE, HIDE), HIDE)]
        for column in range(WIDTH // 256):
            at = slice(column * 256, column * 256 + 256)
            total[:, at] += dot(active, down[:, at])
        return carry

    for one in back:
        one.sent()
    lax.fori_loop(0, PAIRS, feed, 0)
    save(keep.slope, outs.slope)
    save(keep.activated_t, outs.activated_t)

    def finish_rows(step, carry):
        value = total[pl.ds(pl.multiple_of(step * 32, 32), 32)]
        near = pl.ds(pl.multiple_of(step * 16, 16), 16)
        keep.big_out[near] = family(value, 0).astype(BF16)
        keep.small_out[near] = (family(value, 1) * ins.live[step // 2].astype(F32)).astype(BF16)
        return carry

    lax.fori_loop(0, 8, finish_rows, 0)
    save(keep.big_out, outs.big_out)
    save(keep.small_out, outs.small_out)
    there.sent()
    for copy in copies:
        copy.wait()


def forward(ins, scalars, vectors, weights):
    sem = pltpu.SemaphoreType.DMA
    kept, work = list(FORWARD_OUTS.values()), list(FORWARD_WORK.values())
    in_keys, weight_keys = tuple(vars(ins)) + tuple(vars(scalars)), tuple(vars(weights))
    results = pl.pallas_call(
        functools.partial(forward_kernel, in_keys, len(vectors), weight_keys),
        out_shape=[jax.ShapeDtypeStruct(shape, dtype) for shape, dtype in kept],
        in_specs=[VMEM] * len(vars(ins)) + [SMEM] * len(vars(scalars)) + [VMEM] * len(vectors) + [ANY] * len(weight_keys),
        out_specs=[ANY] * len(kept),
        scratch_shapes=[pltpu.VMEM(shape, dtype) for shape, dtype in kept + work]
        + [sem((len(weight_keys),)), sem((len(kept),)), sem((3, 2, 16)), sem((2, 4))],
        compiler_params=pltpu.CompilerParams(
            collective_id=1, has_side_effects=True, vmem_limit_bytes=62 * 2**20
        ),
        cost_estimate=pl.CostEstimate(flops=9 * 10**9, bytes_accessed=60 * 2**20, transcendentals=4 * 10**6),
        name="layer_forward",
    )(*vars(ins).values(), *vars(scalars).values(), *vectors, *vars(weights).values())
    return named(FORWARD_OUTS, list(results))


class Reduction:
    def __init__(self, place, index, refs, sems):
        self.place, self.index, self.refs, self.sems = place, index, refs, sems
        k, n, shares = MATRICES[index]
        self.half = n // 2
        self.depth = k // 64
        self.groups = self.depth // 16
        self.bounds, start = [], 0
        for share in shares:
            self.bounds.append((start, start + share))
            start += share
        self.units = start * self.groups
        self.first_unit = sum(m[1] // 2 // LANES * (m[0] // 1024) for m in MATRICES[:index])
        self.send_unit = SEND_UNITS[index]
        self.local_done = False

    def left_local(self):
        r, s, i = self.refs, self.sems, self.index
        return pltpu.make_async_copy(r.at_in, r.at.at[:, :, :, :, :, :ROWS], s.local.at[i, 0])

    def left_far(self):
        r, s, i = self.refs, self.sems, self.index
        target = r.at.at[:, :, :, :, :, ROWS:]
        return remote(r.at_in, target, s.ex_send.at[i, 0], s.ex_recv.at[i, 0], self.place.partner)

    def right_local(self):
        r, s, i, core = self.refs, self.sems, self.index, self.place.core
        source = r.source.at[:, lanes(core, self.half)]
        return pltpu.make_async_copy(source, r.g.at[:ROWS], s.local.at[i, 1])

    def right_far(self):
        r, s, i, core = self.refs, self.sems, self.index, self.place.core
        source = r.source.at[:, lanes(1 - core, self.half)]
        return remote(source, r.g.at[ROWS:], s.ex_send.at[i, 1], s.ex_recv.at[i, 1], self.place.partner)

    def lefts(self):
        self.left_far().start()
        self.left_local().start()

    def rights(self):
        self.right_far().start()
        self.right_local().start()

    def right_local_done(self):
        if not self.local_done:
            self.right_local().wait()
            self.local_done = True

    def rights_sent(self):
        self.right_local_done()
        self.right_far().wait_send()

    def loaded(self):
        self.left_far().wait_recv()
        self.right_far().wait_recv()
        self.left_local().wait()
        self.right_local_done()

    def span(self, part):
        low, high = self.bounds[part]
        return low * self.groups, high * self.groups

    def copy(self, part, stage, step):
        r, s, i = self.refs, self.sems, self.index
        low, high = self.span(part)
        here = slice(self.first_unit + low, self.first_unit + high)
        device, slot = self.place.along(ORDERS[part][stage], step)
        if stage == 1:
            source = r.r1.at[0, here, slot]
            target = r.r2.at[step - 1, here]
        else:
            source = r.r2.at[0, here, slot]
            target = r.r3.at[step - 1, here]
        return remote(
            source, target, s.send.at[i, part, stage, step - 1], s.recv.at[i, part, stage, step - 1], device
        )

    def left_block(self, part, slot, group):
        at = self.refs.at
        rows = slice(group * 16, group * 16 + 16)
        if part == 0:
            blocks = [at[y // 2, :, y % 2, slot, rows] for y in range(4)]
        elif part == 1:
            blocks = [at[slot // 2, :, slot % 2, :, rows]]
        else:
            blocks = [at[:, slot, :, x, rows] for x in range(4)]
        blocks = [block.reshape(-1, block.shape[-1]) for block in blocks]
        return blocks[0] if len(blocks) == 1 else jnp.concatenate(blocks, axis=0)

    def products(self, part, slot, emit):
        low, high = self.bounds[part]
        for group in range(self.groups):
            left = self.left_block(part, slot, group)
            for tile in range(low, high, 2):
                width = min(2, high - tile)
                value = dot(left, self.refs.g[:, tile * LANES : (tile + width) * LANES])
                for i in range(width):
                    one = value[:, i * LANES : (i + 1) * LANES].reshape(4, 4, 16, LANES)
                    emit((tile + i) * self.groups + group, one)

    def relay(self, part, way):
        r, s, i = self.refs, self.sems, self.index
        low, high = self.span(part)
        here = slice(self.first_unit + low, self.first_unit + high)
        half = slice(way * 2, way * 2 + 2)
        device = self.place.along(ORDERS[part][0], 3 if way else 1)[0]
        source = r.s1.at[0, self.send_unit + low : self.send_unit + high, half]
        target = r.r1.at[2, here, half]
        return remote(source, target, s.send.at[i, part, 0, way], s.recv.at[i, part, 0, way], device)

    def direct(self, part, way):
        r, s, i = self.refs, self.sems, self.index
        low, high = self.span(part)
        here = slice(self.first_unit + low, self.first_unit + high)
        device = self.place.along(ORDERS[part][0], 3 if way else 1)[0]
        source = r.s1.at[1 + way, self.send_unit + low : self.send_unit + high]
        target = r.r1.at[way, here]
        return remote(source, target, s.send.at[i, part, 0, 2 + way], s.recv.at[i, part, 0, 2 + way], device)

    def first(self):
        r = self.refs
        for part in range(3):
            slot = self.place.along(ORDERS[part][0], 2)[1]

            def emit(unit, value):
                r.s1[0, self.send_unit + unit] = value.astype(BF16)

            self.products(part, slot, emit)
            for way in range(2):
                self.relay(part, way).start()

    def pass_on(self):
        r = self.refs
        for part in range(3):
            for way in range(2):
                self.relay(part, way).wait_recv()
                slot = self.place.along(ORDERS[part][0], 3 if way else 1)[1]

                def emit(unit, value, way=way):
                    at = self.first_unit + unit
                    for half in range(2):
                        some = slice(half * 2, half * 2 + 2)
                        one = value[some]
                        if half == way:
                            one = one + r.r1[2, at, some].astype(F32)
                        r.s1[1 + way, self.send_unit + unit, some] = one.astype(BF16)

                self.products(part, slot, emit)
                self.direct(part, way).start()

    def first_sent(self):
        for part in range(3):
            for way in range(2):
                self.relay(part, way).wait_send()
                self.direct(part, way).wait_send()

    def second(self):
        r = self.refs
        for part in range(3):
            slot = self.place.along(ORDERS[part][0], 0)[1]
            for way in range(2):
                self.direct(part, way).wait_recv()

            def emit(unit, value):
                at = self.first_unit + unit
                for i in range(2):
                    value = value + r.r1[i, at].astype(F32)
                r.r1[0, at] = value.astype(BF16)

            self.products(part, slot, emit)
            for step in (1, 2, 3):
                self.copy(part, 1, step).start()

    def third(self):
        r = self.refs
        for part in range(3):
            slot = self.place.along(ORDERS[part][1], 0)[1]
            for step in (1, 2, 3):
                self.copy(part, 1, step).wait_recv()

            def one(unit, carry, slot=slot):
                value = r.r1[0, unit, slot].astype(F32)
                for i in range(3):
                    value = value + r.r2[i, unit].astype(F32)
                r.r2[0, unit] = value.astype(BF16)
                return carry

            low, high = self.span(part)
            lax.fori_loop(self.first_unit + low, self.first_unit + high, one, 0)
            for step in (1, 2, 3):
                self.copy(part, 2, step).start()

    def mine(self):
        return self.place.y_hi * 4 + self.place.x

    def rows_of(self, slot):
        return pl.ds(pl.multiple_of(slot * self.depth, self.depth), self.depth)

    def gather_copy(self, y_hi, x, slot):
        r, s, i, place = self.refs, self.sems, self.index, self.place
        target = r.out.at[self.rows_of(slot), lanes(place.core, self.half)]
        return remote(
            r.piece, target, s.ag_send.at[i, y_hi * 4 + x], s.ag_recv.at[i, slot],
            place.device(y_hi=y_hi, x=x),
        )

    def own_copy(self):
        target = self.refs.out.at[self.rows_of(self.mine()), lanes(self.place.core, self.half)]
        return pltpu.make_async_copy(self.refs.piece, target, self.sems.local.at[self.index, 2])

    def others(self):
        place = self.place
        for y_step in (0, 1):
            y_hi = (place.y_hi + y_step) % 2
            for x_step in range(4):
                if y_step or x_step:
                    yield y_hi, (place.x + x_step) % 4

    def fourth(self):
        r = self.refs
        for part in range(3):
            slot = self.place.along(ORDERS[part][2], 0)[1]
            for step in (1, 2, 3):
                self.copy(part, 2, step).wait_recv()
            low, high = self.span(part)
            for unit in range(low, high):
                at = self.first_unit + unit
                value = r.r2[0, at, slot].astype(F32)
                for i in range(3):
                    value = value + r.r3[i, at].astype(F32)
                tile, group = unit // self.groups, unit % self.groups
                r.piece[group * 16 : group * 16 + 16, tile * LANES : tile * LANES + LANES] = value.astype(BF16)
        self.own_copy().start()
        for y_hi, x in self.others():
            self.gather_copy(y_hi, x, self.mine()).start()

    def cross_copy(self):
        r, s, i, core = self.refs, self.sems, self.index, self.place.core
        block = r.out.at[:, lanes(core, self.half)]
        return remote(block, block, s.cross.at[i, 0], s.cross.at[i, 1], self.place.partner)

    def fifth(self):
        self.own_copy().wait()
        for y_hi, x in self.others():
            self.gather_copy(y_hi, x, y_hi * 4 + x).wait_recv()
        self.cross_copy().start()

    def finish(self):
        self.cross_copy().wait()
        self.left_far().wait_send()
        for y_hi, x in self.others():
            self.gather_copy(y_hi, x, self.mine()).wait_send()
        for part in range(3):
            for stage in (1, 2):
                for step in (1, 2, 3):
                    self.copy(part, stage, step).wait_send()


GAIN1, SHIFT1, SPATIAL_BIAS, GAIN2, SHIFT2, TEMPORAL_BIAS, GAIN3, SHIFT3, INNER, OUTER = 8, 9, 10, 11, 12, 13, 14, 15, 16, 20


class SmallSums:
    def __init__(self, place, refs, sems):
        self.place, self.refs, self.sems = place, refs, sems

    def share(self, core):
        return pl.ds(pl.multiple_of(core * 16, 16), 16)

    def cross(self):
        r, core = self.refs, self.place.core
        return remote(
            r.sums.at[self.share(1 - core)], r.sums_core, self.sems.at[0, 0, 0], self.sems.at[1, 0, 0],
            self.place.partner,
        )

    def along(self, stage, step):
        device = self.place.along("xyz"[stage], step)[0]
        return remote(
            self.refs.sums_total.at[stage], self.refs.sums_recv.at[stage, step - 1],
            self.sems.at[0, stage + 1, step - 1], self.sems.at[1, stage + 1, step - 1], device,
        )

    def final(self):
        block = self.refs.sums_final.at[self.share(self.place.core)]
        return remote(block, block, self.sems.at[0, 4, 0], self.sems.at[1, 4, 0], self.place.partner)

    def begin(self):
        self.cross().start()

    def step0(self):
        r = self.refs
        self.cross().wait()
        r.sums_total[0] = r.sums[self.share(self.place.core)] + r.sums_core[...]
        for step in (1, 2, 3):
            self.along(0, step).start()

    def advance(self, stage):
        r = self.refs
        value = r.sums_total[stage]
        for step in (1, 2, 3):
            self.along(stage, step).wait_recv()
            value = value + r.sums_recv[stage, step - 1]
        if stage < 2:
            r.sums_total[stage + 1] = value
            for step in (1, 2, 3):
                self.along(stage + 1, step).start()
        else:
            r.sums_final[self.share(self.place.core)] = value
            self.final().start()

    def finish(self, out, sem):
        self.final().wait()
        copy = pltpu.make_async_copy(self.refs.sums_final, out, sem)
        copy.start()
        for stage in range(3):
            for step in (1, 2, 3):
                self.along(stage, step).wait_send()
        copy.wait()


BACK_OUTS = dict(
    big_grad=((128, WIDTH), F32),
    small_grad=((128, WIDTH), F32),
    small_sums=((32, WIDTH), F32),
)
SLOTS = 3
BACK_WORK = dict(
    s1=((3, 32, 4, 4, 16, LANES), BF16),
    r1=((3, 64, 4, 4, 16, LANES), BF16),
    r2=((3, 64, 4, 16, LANES), BF16),
    r3=((3, 64, 16, LANES), BF16),
    tall=((SLOTS, HIDE, WIDTH), BF16),
    broad=((SLOTS, WIDTH, HIDE), BF16),
    slope_in=((SLOTS, ROWS, HIDE), BF16),
    record=((SLOTS, SP_ROWS, LANES), BF16),
    resid=((ROWS, WIDTH), F32),
    grad=((ROWS, WIDTH), F32),
    total=((ROWS, WIDTH), F32),
    low3=((ROWS, WIDTH), BF16),
    low2=((ROWS, WIDTH), BF16),
    low1=((ROWS, WIDTH), BF16),
    hidden_low=((ROWS, HIDDEN), BF16),
    packed=((ROWS, 3 * WIDTH), BF16),
    swap_send=((ROWS, WIDTH), BF16),
    context_back=((ROWS, WIDTH), BF16),
    normed_back=((ROWS, WIDTH), BF16),
    context_grad=((2, 128, WIDTH), BF16),
    far_send=((ROWS, 2 * WIDTH), BF16),
    far_recv=((ROWS, 2 * WIDTH), BF16),
    inner_sums=((PAIRS, HIDE), F32),
    sums=((32, WIDTH), F32),
    sums_core=((16, WIDTH), F32),
    sums_total=((3, 16, WIDTH), F32),
    sums_recv=((3, 3, 16, WIDTH), F32),
    sums_final=((32, WIDTH), F32),
    frame_sums=((8, WIDTH), F32),
    scale=((ROWS, LANES), F32),
    gains=((8, WIDTH), F32),
)


BACK_SEMS = dict(
    local=(6, 3),
    ex_send=(6, 2),
    ex_recv=(6, 2),
    send=(6, 3, 3, 4),
    recv=(6, 3, 3, 4),
    ag_send=(6, 8),
    ag_recv=(6, 8),
    cross=(6, 2),
    ring=(4, SLOTS),
    io=(5,),
    swap=(3, 2, 16),
    far=(2,),
    sums=(2, 5, 3),
)


def backward_kernel(in_keys, saved_keys, weight_keys, *refs):
    refs = list(refs)
    count = len(MATRICES)
    ins = named(in_keys, refs)
    gains = [refs.pop(0) for _ in range(3)]
    lefts = [refs.pop(0) for _ in range(count)]
    saved, weights, outs = named(saved_keys, refs), named(weight_keys, refs), named(BACK_OUTS, refs)
    matrix_outs = [refs.pop(0) for _ in range(count)]
    work = named(BACK_WORK, refs)
    ats, gs, pieces = ([refs.pop(0) for _ in range(count)] for _ in range(3))
    sems = named(BACK_SEMS, refs)
    ring_sems, io_sems, swap_sems, far_sems, sum_sems = sems.ring, sems.io, sems.swap, sems.far, sems.sums
    place = Place()
    frame = place.ta // 2
    sources = (work.low3, work.hidden_low, work.low2, work.packed, work.low1, work.packed)
    reductions = []
    for i in range(count):
        own = Names(at_in=lefts[i], at=ats[i], g=gs[i], piece=pieces[i], out=matrix_outs[i], source=sources[i])
        own.s1, own.r1, own.r2, own.r3 = work.s1, work.r1, work.r2, work.r3
        reductions.append(Reduction(place, i, own, sems))
    fout, fin, tout, tqkv, sout, sqkv = reductions
    small = SmallSums(place, work, sum_sems)

    def tall(source, base, index):
        slot = (base + index) % SLOTS
        rows = pl.ds(pl.multiple_of(index * HIDE, HIDE), HIDE)
        return pltpu.make_async_copy(source.at[rows], work.tall.at[slot], ring_sems.at[0, slot])

    def broad(source, base, index):
        slot = (base + index) % SLOTS
        return pltpu.make_async_copy(
            source.at[:, lanes(index, HIDE)], work.broad.at[slot], ring_sems.at[1, slot]
        )

    def slope(base, index):
        slot = (base + index) % SLOTS
        return pltpu.make_async_copy(saved.slope.at[index], work.slope_in.at[slot], ring_sems.at[2, slot])

    def record(source, base, index):
        slot = (base + index) % SLOTS
        return pltpu.make_async_copy(
            source.at[index], work.record.at[slot, pl.ds(0, source.shape[1])], ring_sems.at[3, slot]
        )

    def open_stream(maker, count):
        for index in range(min(SLOTS, count)):
            maker(index).start()

    def refill(maker, count, index):
        @pl.when(index + SLOTS < count)
        def _():
            maker(index + SLOTS).start()

    fout_tiles = functools.partial(tall, weights.w_fout, 0)
    tout_tiles = functools.partial(tall, weights.w_tout, 8)
    sout_tiles = functools.partial(tall, weights.w_sout, 10)
    fin_tiles = functools.partial(broad, weights.w_fin, 0)
    tqkv_tiles = functools.partial(broad, weights.w_tqkv, 8)
    sqkv_tiles = functools.partial(broad, weights.w_sqkv, 14)
    slopes = functools.partial(slope, 0)
    temporal_records = functools.partial(record, saved.temporal, 0)
    spatial_records = functools.partial(record, saved.spatial, 8)

    class Kept:
        def __init__(self, normals, scales):
            self.copies = (
                pltpu.make_async_copy(normals, work.resid, io_sems.at[0]),
                pltpu.make_async_copy(scales, work.scale, io_sems.at[4]),
            )
            for copy in self.copies:
                copy.start()

        def wait(self):
            for copy in self.copies:
                copy.wait()

    open_stream(fout_tiles, 8)
    open_stream(slopes, 8)
    open_stream(fin_tiles, 8)
    kept3 = Kept(saved.normal3, saved.scale3)
    open_stream(temporal_records, 8)
    work.sums[...] = jnp.zeros_like(work.sums)
    for row, gain in enumerate(gains):
        work.gains[row : row + 1] = gain[...].astype(F32).reshape(1, WIDTH)
    greet(place, True)
    for one in reductions:
        one.lefts()

    grad, total = work.grad, work.total

    def start_rows(step, carry):
        near = pl.ds(pl.multiple_of(step * 16, 16), 16)
        big = ins.big_cot[near].astype(F32)
        little = ins.small_cot[near].astype(F32) * ins.live[step // 2].astype(F32)
        merged = interleave(big, little)
        rows = pl.ds(pl.multiple_of(step * 32, 32), 32)
        grad[rows] = merged
        work.low3[rows] = merged.astype(BF16)
        total[rows] = jnp.zeros_like(merged)
        work.sums[OUTER : OUTER + 1] += jnp.sum(merged, axis=0, keepdims=True)
        return carry

    lax.fori_loop(0, 8, start_rows, 0)
    fout.rights()

    def feed(step, carry):
        slopes(step).wait()
        fout_tiles(step).wait()
        fin_tiles(step).wait()
        slot = step % SLOTS
        down = dot_nt(work.low3[...], work.tall[slot]) * work.slope_in[slot].astype(F32)
        work.inner_sums[pl.ds(step, 1)] = jnp.sum(down, axis=0, keepdims=True)
        low = down.astype(BF16)
        work.hidden_low[:, lanes(step, HIDE)] = low
        for column in range(WIDTH // 256):
            at = slice(column * 256, column * 256 + 256)
            total[:, at] += dot_nt(low, work.broad[slot, at])
        refill(slopes, 8, step)
        refill(fout_tiles, 8, step)
        refill(fin_tiles, 8, step)
        return carry

    lax.fori_loop(0, 4, feed, 0)
    fout.loaded()
    fout.first()
    lax.fori_loop(4, 8, feed, 0)
    fin.rights()
    open_stream(tout_tiles, 2)
    open_stream(sout_tiles, 1)
    open_stream(tqkv_tiles, 6)
    for part in range(PAIRS):
        at = part % 2 * HIDE
        work.sums[INNER + part // 2 : INNER + part // 2 + 1, at : at + HIDE] = work.inner_sums[part : part + 1]

    def norm_back(gradient, gain_row, row, low, bias_row):
        gain = work.gains[gain_row : gain_row + 1]

        def one(step, carry):
            rows = rows16(step)
            error = gradient[rows].astype(F32)
            normal, scale = work.resid[rows], work.scale[rows, 0:1]
            scaled = error * gain
            mean_one = jnp.mean(scaled, axis=-1, keepdims=True)
            mean_two = jnp.mean(scaled * normal, axis=-1, keepdims=True)
            value = grad[rows] + (scaled - mean_one - normal * mean_two) * scale
            grad[rows] = value
            if low is not None:
                low[rows] = value.astype(BF16)
            gains = error * normal
            sums = [part[:8] + part[8:] for part in (gains, error, value)]
            return tuple(a + b for a, b in zip(carry, sums))

        zero = jnp.zeros((8, WIDTH), F32)
        sums = lax.fori_loop(0, 16, one, (zero, zero, zero), unroll=2)
        work.sums[row : row + 1] = jnp.sum(sums[0], axis=0, keepdims=True)
        work.sums[row + 1 : row + 2] = jnp.sum(sums[1], axis=0, keepdims=True)
        if bias_row is not None:
            work.sums[bias_row : bias_row + 1] = jnp.sum(sums[2], axis=0, keepdims=True)

    kept3.wait()
    norm_back(total, 2, GAIN3, work.low2, TEMPORAL_BIAS)
    kept2 = Kept(saved.normal2, saved.scale2)
    tout.rights()

    there = [Swap(place, work.swap_send, work.context_back, swap_sems, i, True, HALVES[i]) for i in range(2)]
    for index in range(2):
        tout_tiles(index).wait()
        slot = (8 + index) % SLOTS
        work.swap_send[:, HALVES[index]] = dot_nt(work.low2[...], work.tall[slot]).astype(BF16)
        there[index].start()
    sout_tiles(1).start()
    fout.pass_on()
    fin.loaded()
    fin.first()
    there[0].wait()

    low_lanes = half_masks(128)
    low_lanes_wide = half_masks(256)

    def attention_back(probs, keys, values, queries, upstream, wide):
        key_low = low_lanes_wide if wide else low_lanes
        upstreams = by_head(upstream, low_lanes)
        errors = []
        for head in range(2):
            prob = probs[head].astype(F32)
            back = dot_nt(values, upstreams[head])
            delta = jnp.sum(prob * back, axis=0, keepdims=True)
            errors.append((prob * (back - delta)).astype(BF16))
        key_grad = dot(jnp.concatenate(errors, axis=1), jnp.concatenate(by_head(queries, low_lanes), axis=0))
        value_grad = dot(jnp.concatenate(probs, axis=1), jnp.concatenate(upstreams, axis=0))
        query_grad = dot_tn(jnp.concatenate(errors, axis=0), jnp.concatenate(by_head(keys, key_low), axis=0))
        return query_grad * 0.125, key_grad, value_grad

    def temporal_pair(pair, carry):
        temporal_records(pair).wait()
        slot = pair % SLOTS
        for half in range(2):
            base = half * 128

            def rows(start, half=half):
                return work.record[slot, start + half * 128 : start + half * 128 + 128]

            probs = [work.record[slot, (half * 2 + h) * 128 : (half * 2 + h) * 128 + 128] for h in range(2)]
            upstream = work.context_back[base : base + 128, lanes(pair, LANES)]
            grads = attention_back(probs, rows(TP_KEY), rows(TP_VALUE), rows(TP_QUERY), upstream, False)
            for i, value in enumerate(grads):
                work.packed[base : base + 128, lanes(pair + i * PAIRS, LANES)] = value.astype(BF16)
        refill(temporal_records, 8, pair)
        return carry

    lax.fori_loop(0, PAIRS // 2, temporal_pair, 0)
    there[1].wait()
    lax.fori_loop(PAIRS // 2, PAIRS, temporal_pair, 0)
    open_stream(spatial_records, 8)
    tqkv.rights()
    fin.pass_on()

    def project_back(maker, base, start, stop):
        def one(step, carry):
            maker(step).wait()
            slot = (base + step) % SLOTS
            low = work.packed[:, lanes(step, HIDE)]
            for column in range(WIDTH // 256):
                at = slice(column * 256, column * 256 + 256)
                value = dot_nt(low, work.broad[slot, at])
                total[:, at] += value
            refill(maker, 6, step)
            return carry

        if start == 0:
            total[...] = jnp.zeros_like(total)
        lax.fori_loop(start, stop, one, 0)

    project_back(tqkv_tiles, 8, 0, 6)
    open_stream(sqkv_tiles, 6)
    for one in there:
        one.sent()
    work.swap_send[...] = total[...].astype(BF16)
    back = Swap(place, work.swap_send, work.normed_back, swap_sems, 2, False)
    back.start()
    fout.second()
    fout.first_sent()
    tout.loaded()
    tout.first()
    back.wait()

    kept2.wait()
    norm_back(work.normed_back, 1, GAIN2, work.low1, SPATIAL_BIAS)
    kept1 = Kept(saved.normal1, saved.scale1)
    sout.rights()
    for index in range(2):
        sout_tiles(index).wait()
        slot = (10 + index) % SLOTS
        at = slice(index * HIDE, index * HIDE + HIDE)
        value = dot_nt(work.low1[...], work.tall[slot])
        for which in range(2):
            work.context_grad[which, :, at] = family(value, which).astype(BF16)
    tqkv.rights_sent()
    tqkv.loaded()
    tqkv.first()
    fin.second()
    tout.pass_on()

    def spatial_pair(pair, carry):
        spatial_records(pair).wait()
        slot = (8 + pair) % SLOTS
        all_grads = []
        for which in range(2):

            def rows(start, count, which=which):
                return work.record[slot, start + which * count : start + which * count + count]

            probs = [work.record[slot, (which * 2 + h) * 256 : (which * 2 + h) * 256 + 256] for h in range(2)]
            upstream = work.context_grad[which, :, lanes(pair, LANES)]
            all_grads.append(
                attention_back(
                    probs, rows(SP_KEY, 256), rows(SP_VALUE, 256), rows(SP_QUERY, 128), upstream, True
                )
            )
        for i in range(3):
            value = interleave(all_grads[0][i][:128], all_grads[1][i][:128])
            work.packed[:, lanes(pair + i * PAIRS, LANES)] = value.astype(BF16)
        for i in (1, 2):
            value = interleave(all_grads[0][i][128:], all_grads[1][i][128:])
            work.far_send[:, lanes(pair + (i - 1) * PAIRS, LANES)] = value.astype(BF16)
        refill(spatial_records, 8, pair)
        return carry

    lax.fori_loop(0, PAIRS, spatial_pair, 0)
    far = remote(work.far_send, work.far_recv, far_sems.at[0], far_sems.at[1], place.partner)
    far.start()
    tqkv.pass_on()
    fin.first_sent()
    sout.loaded()
    sout.first()
    fout.third()
    far.wait()

    def join(step, carry):
        rows = rows16(step)
        value = work.packed[rows, WIDTH:].astype(F32) + work.far_recv[rows].astype(F32)
        work.packed[rows, WIDTH:] = value.astype(BF16)
        return carry

    lax.fori_loop(0, 16, join, 0)
    sqkv.rights()
    project_back(sqkv_tiles, 14, 0, 2)
    sqkv.loaded()
    sqkv.first()
    project_back(sqkv_tiles, 14, 2, 6)
    sqkv.pass_on()
    sout.pass_on()
    tout.second()
    tqkv.second()
    kept1.wait()
    norm_back(total, 0, GAIN1, None, None)
    fin.third()

    def finish_rows(step, carry):
        value = grad[pl.ds(pl.multiple_of(step * 32, 32), 32)]
        big, little = family(value, 0), family(value, 1)
        near = pl.ds(pl.multiple_of(step * 16, 16), 16)
        total[near] = big
        total[pl.ds(pl.multiple_of(128 + step * 16, 16), 16)] = little
        work.frame_sums[0:1] += jnp.sum(big, axis=0, keepdims=True)
        work.frame_sums[pl.ds(1 + step // 2, 1)] += jnp.sum(little, axis=0, keepdims=True)
        return carry

    work.frame_sums[...] = jnp.zeros_like(work.frame_sums)
    lax.fori_loop(0, 8, finish_rows, 0)
    out_copies = [
        pltpu.make_async_copy(total.at[:128], outs.big_grad, io_sems.at[1]),
        pltpu.make_async_copy(total.at[128:], outs.small_grad, io_sems.at[2]),
    ]
    for copy in out_copies:
        copy.start()
    table, at_row = jnp.zeros((8, WIDTH), F32), lax.broadcasted_iota(jnp.int32, (8, WIDTH), 0)
    for i in range(5):
        action = ins.big_actions[0, frame] if i == 0 else ins.small_actions[i - 1, frame]
        table = table + jnp.where(at_row == action, work.frame_sums[i : i + 1], 0.0)
    work.sums[0:8] = table
    small.begin()
    fout.fourth()
    sout.second()
    small.step0()
    tout.third()
    fin.fourth()
    sqkv.second()
    small.advance(0)
    tqkv.third()
    sout.third()
    small.advance(1)
    fout.fifth()
    sqkv.third()
    tout.fourth()
    fin.fifth()
    small.advance(2)
    tqkv.fourth()
    sout.fourth()
    sqkv.fourth()
    tout.fifth()
    tqkv.fifth()
    sout.fifth()
    sqkv.fifth()
    small.finish(outs.small_sums, io_sems.at[3])
    for one in reductions:
        one.finish()
    for one in (tout, tqkv, sout, sqkv):
        one.first_sent()
    for one in (fout, fin, tout, sout, sqkv):
        one.rights_sent()
    back.sent()
    for copy in out_copies:
        copy.wait()


def backward(ins, scalars, gains, lefts, saved, weights):
    sem = pltpu.SemaphoreType.DMA
    count = len(MATRICES)
    work = [pltpu.VMEM(shape, dtype) for shape, dtype in BACK_WORK.values()]
    work += [pltpu.VMEM((2, 4, 2, 4, k // 64, 2 * ROWS), BF16) for k, _, _ in MATRICES]
    work += [pltpu.VMEM((2 * ROWS, n // 2), BF16) for _, n, _ in MATRICES]
    work += [pltpu.VMEM((k // 64, n // 2), BF16) for k, n, _ in MATRICES]
    work += [sem(shape) for shape in BACK_SEMS.values()]
    shapes = list(BACK_OUTS.values()) + [((k // 8, n), BF16) for k, n, _ in MATRICES]
    in_keys, saved_keys, weight_keys = tuple(vars(ins)) + tuple(vars(scalars)), tuple(vars(saved)), tuple(vars(weights))
    return pl.pallas_call(
        functools.partial(backward_kernel, in_keys, saved_keys, weight_keys),
        out_shape=[jax.ShapeDtypeStruct(shape, dtype) for shape, dtype in shapes],
        in_specs=[VMEM] * len(vars(ins))
        + [SMEM] * len(vars(scalars))
        + [VMEM] * len(gains)
        + [ANY] * (count + len(saved_keys) + len(weight_keys)),
        out_specs=[ANY] * len(shapes),
        scratch_shapes=work,
        compiler_params=pltpu.CompilerParams(
            collective_id=2, has_side_effects=True, vmem_limit_bytes=63 * 2**20
        ),
        cost_estimate=pl.CostEstimate(flops=18 * 10**9, bytes_accessed=80 * 2**20, transcendentals=0),
        name="layer_backward",
    )(
        *vars(ins).values(),
        *vars(scalars).values(),
        *gains,
        *[left.reshape(2, 4, 2, 4, k // 64, ROWS) for left, (k, _, _) in zip(lefts, MATRICES)],
        *vars(saved).values(),
        *vars(weights).values(),
    )


SUM_VECTORS = (
    (GAIN1, 1),
    (SHIFT1, 1),
    (SPATIAL_BIAS, 1),
    (GAIN2, 1),
    (SHIFT2, 1),
    (TEMPORAL_BIAS, 1),
    (GAIN3, 1),
    (SHIFT3, 1),
    (INNER, 4),
    (OUTER, 1),
)


def widen_kernel(*refs):
    refs = list(refs)
    count, passed = len(MATRICES), 4
    narrow = [refs.pop(0) for _ in range(count)]
    plain = [refs.pop(0) for _ in range(passed)]
    sums = refs.pop(0)
    wide = [refs.pop(0) for _ in range(count)]
    plain_out = [refs.pop(0) for _ in range(passed)]
    table, vectors = refs.pop(0), [refs.pop(0) for _ in SUM_VECTORS]
    narrow_in, wide_out = refs[:count], refs[count : 2 * count]
    sems = refs[2 * count]
    loads = [pltpu.make_async_copy(narrow[i], narrow_in[i], sems.at[0, i]) for i in range(count)]
    stores = [pltpu.make_async_copy(wide_out[i], wide[i], sems.at[1, i]) for i in range(count)]
    moves = [pltpu.make_async_copy(plain[i], plain_out[i], sems.at[2, i]) for i in range(passed)]
    for copy in loads + moves:
        copy.start()
    table[...] = sums[0:8]
    for (row, rows), vector in zip(SUM_VECTORS, vectors):
        for i in range(rows):
            vector[i * WIDTH : (i + 1) * WIDTH] = sums[row + i]
    for i in range(count):
        loads[i].wait()

        def one(step, carry, i=i):
            wide_out[i][rows16(step)] = narrow_in[i][rows16(step)].astype(F32)
            return carry

        lax.fori_loop(0, narrow_in[i].shape[0] // 16, one, 0, unroll=2)
        stores[i].start()
    for copy in stores + moves:
        copy.wait()


def widen(matrices, plain, sums):
    count = len(matrices)
    vectors = [jax.ShapeDtypeStruct((rows * WIDTH,), F32) for _, rows in SUM_VECTORS]
    shapes = [jax.ShapeDtypeStruct(one.shape, F32) for one in matrices]
    scratch = [pltpu.VMEM(one.shape, BF16) for one in matrices] + [pltpu.VMEM(one.shape, F32) for one in matrices]
    results = pl.pallas_call(
        widen_kernel,
        out_shape=shapes
        + [jax.ShapeDtypeStruct(one.shape, one.dtype) for one in plain]
        + [jax.ShapeDtypeStruct((8, WIDTH), F32)]
        + vectors,
        in_specs=[ANY] * (count + len(plain)) + [VMEM],
        out_specs=[ANY] * (count + len(plain)) + [VMEM] * (1 + len(vectors)),
        scratch_shapes=scratch + [pltpu.SemaphoreType.DMA((3, count))],
        compiler_params=pltpu.CompilerParams(vmem_limit_bytes=62 * 2**20),
        cost_estimate=pl.CostEstimate(flops=0, bytes_accessed=14 * 2**20, transcendentals=0),
        name="widen",
    )(*matrices, *plain, sums)
    results = list(results)
    wide = [results.pop(0) for _ in range(count)]
    passed = [results.pop(0) for _ in plain]
    return wide, passed, results


def body(
    big_tokens,
    small_tokens,
    big_actions,
    small_actions,
    big_order,
    small_order,
    small_live,
    action_table,
    norm1_gain,
    norm1_bias,
    spatial_qkv,
    spatial_out,
    spatial_out_bias,
    norm2_gain,
    norm2_bias,
    temporal_qkv,
    temporal_out,
    temporal_out_bias,
    norm3_gain,
    norm3_bias,
    ffn_in,
    ffn_in_bias,
    ffn_out,
    ffn_out_bias,
    big_cotangent,
    small_cotangent,
):
    scalars = Names(
        big_actions=big_actions,
        small_actions=small_actions,
        big_order=big_order,
        small_order=small_order,
        live=small_live,
    )
    vectors = (
        norm1_gain,
        norm1_bias,
        spatial_out_bias,
        norm2_gain,
        norm2_bias,
        temporal_out_bias,
        norm3_gain,
        norm3_bias,
        ffn_out_bias,
    )
    weights = Names(
        w_sqkv=spatial_qkv,
        w_sout=spatial_out,
        w_tqkv=temporal_qkv,
        w_tout=temporal_out,
        w_fin=ffn_in,
        w_fout=ffn_out,
    )
    saved = forward(
        Names(
            big=big_tokens.reshape(128, WIDTH),
            small=small_tokens.reshape(128, WIDTH),
            table=action_table,
            inner_bias=ffn_in_bias,
        ),
        scalars,
        vectors,
        weights,
    )
    big_grad, small_grad, sums, *matrices = backward(
        Names(big_cot=big_cotangent.reshape(128, WIDTH), small_cot=small_cotangent.reshape(128, WIDTH)),
        Names(big_actions=big_actions, small_actions=small_actions, live=small_live),
        (norm1_gain, norm2_gain, norm3_gain),
        (saved.activated_t, saved.normed3_t, saved.context2_t, saved.normed2_t, saved.context1_t, saved.normed1_t),
        Names(
            normal1=saved.normal1,
            normal2=saved.normal2,
            normal3=saved.normal3,
            scale1=saved.scale1,
            scale2=saved.scale2,
            scale3=saved.scale3,
            spatial=saved.spatial,
            temporal=saved.temporal,
            slope=saved.slope,
        ),
        weights,
    )
    matrices, passed, small = widen(matrices, (saved.big_out, saved.small_out, big_grad, small_grad), sums)
    g_fout, g_fin, g_tout, g_tqkv, g_sout, g_sqkv = matrices
    table, gain1, shift1, bias_s, gain2, shift2, bias_t, gain3, shift3, bias_in, bias_out = small
    return (
        passed[0].reshape(1, 128, WIDTH),
        passed[1].reshape(4, 32, WIDTH),
        passed[2].reshape(1, 128, WIDTH),
        passed[3].reshape(4, 32, WIDTH),
        table,
        gain1,
        shift1,
        g_sqkv,
        g_sout,
        bias_s,
        gain2,
        shift2,
        g_tqkv,
        g_tout,
        bias_t,
        gain3,
        shift3,
        g_fin,
        bias_in,
        g_fout,
        bias_out,
    )


def solution(mesh):
    spread, by_col = P("col", "ta", None), P("col", None)
    return jax.shard_map(
        body,
        mesh=mesh,
        in_specs=(spread, spread, by_col, by_col, by_col, by_col, P("col")) + (P(),) * 17 + (spread, spread),
        out_specs=(spread,) * 4
        + (P(),) * 3
        + (by_col, by_col, P(), P(), P(), by_col, by_col, P(), P(), P(), by_col, P(), by_col, P()),
        check_vma=False,
    )
```

```python
import functools
from types import SimpleNamespace as Names

import jax
import jax.numpy as jnp
from jax import lax
from jax.experimental import pallas as pl
from jax.experimental.pallas import tpu as pltpu
from jax.sharding import PartitionSpec as P

HEAD_DIM = 64
EPSILON = 1e-05
MASKED_SCORE = -1e30
MESH = pl.DeviceIdType.MESH
ANY = pl.BlockSpec(memory_space=pl.ANY)
VMEM = pl.BlockSpec(memory_space=pltpu.VMEM)
SMEM = pl.BlockSpec(memory_space=pltpu.SMEM)
LANES = 128
F32, BF16 = jnp.float32, jnp.bfloat16
ROWS, WIDTH, HIDDEN = 256, 1024, 4096
PAIRS = WIDTH // LANES
HIDE = 512

SP_KEY, SP_VALUE, SP_QUERY, SP_ROWS = 1024, 1536, 2048, 2304
TP_KEY, TP_VALUE, TP_QUERY, TP_ROWS = 512, 768, 1024, 1280

ORDERS = (("x", "y", "z"), ("y", "z", "x"), ("z", "x", "y"))
MATRICES = (
    (HIDDEN, WIDTH, (1, 1, 2)),
    (WIDTH, HIDDEN, (4, 6, 6)),
    (WIDTH, WIDTH, (1, 1, 2)),
    (WIDTH, 3 * WIDTH, (4, 4, 4)),
    (WIDTH, WIDTH, (1, 1, 2)),
    (WIDTH, 3 * WIDTH, (4, 4, 4)),
)
ALL, XY, Z = (0, 1, 2), (0, 1), (2,)
SEND_UNITS = (0, 16, 12, 0, 28, 16)


class Place:
    def __init__(self):
        ta, col = lax.axis_index("ta"), lax.axis_index("col")
        self.ta, self.col = ta, col
        self.y_hi, self.x, self.core = ta // 8, (ta // 2) % 4, ta % 2
        self.y_lo, self.z = col // 4, col % 4
        self.y = self.y_hi * 2 + self.y_lo
        self.partner = self.device(core=1 - self.core)

    def device(self, y_hi=None, x=None, core=None, y_lo=None, z=None):
        y_hi = self.y_hi if y_hi is None else y_hi
        x = self.x if x is None else x
        core = self.core if core is None else core
        y_lo = self.y_lo if y_lo is None else y_lo
        z = self.z if z is None else z
        return (y_hi * 8 + x * 2 + core, y_lo * 4 + z)

    def along(self, axis, step):
        if axis == "x":
            at = (self.x + step) % 4
            return self.device(x=at), at
        if axis == "z":
            at = (self.z + step) % 4
            return self.device(z=at), at
        at = (self.y + step) % 4
        return self.device(y_hi=at // 2, y_lo=at % 2), (at % 2) * 2 + at // 2

    def fellow(self, step):
        ta = (self.ta + step) % 16
        return (ta, self.col), ta


def greet(place, whole):
    barrier = pltpu.get_barrier_semaphore()

    def one(step, carry):
        pl.semaphore_signal(barrier, inc=1, device_id=place.fellow(step)[0], device_id_type=MESH)
        return carry

    lax.fori_loop(1, 16, one, 0)
    count = 15
    if whole:
        for axis, step in (("y", 1), ("y", 3), ("z", 1), ("z", 2), ("z", 3)):
            pl.semaphore_signal(barrier, inc=1, device_id=place.along(axis, step)[0], device_id_type=MESH)
            count += 1
    pl.semaphore_wait(barrier, count)


def remote(source, target, send, recv, device):
    return pltpu.make_async_remote_copy(source, target, send, recv, device_id=device, device_id_type=MESH)


def dot(left, right):
    return jnp.dot(left, right, preferred_element_type=F32)


def dot_nt(left, right):
    return lax.dot_general(left, right, (((1,), (1,)), ((), ())), preferred_element_type=F32)


def dot_tn(left, right):
    return lax.dot_general(left, right, (((0,), (0,)), ((), ())), preferred_element_type=F32)


def rows16(step):
    return pl.ds(pl.multiple_of(step * 16, 16), 16)


def lanes(step, width):
    return pl.ds(pl.multiple_of(step * width, width), width)


def interleave(big, small):
    width = big.shape[-1]
    pair = [one.reshape(-1, 1, 8, width) for one in (big, small)]
    return jnp.concatenate(pair, axis=1).reshape(-1, width)


def family(rows, which):
    width = rows.shape[-1]
    return rows.reshape(-1, 2, 8, width)[:, which].reshape(-1, width)


def half_masks(rows):
    lane = lax.broadcasted_iota(jnp.int32, (rows, LANES), 1)
    return lane < HEAD_DIM


def by_head(value, low):
    zero = jnp.zeros_like(value)
    return jnp.where(low, value, zero), jnp.where(low, zero, value)


def statistics(rows):
    mean = jnp.mean(rows, axis=-1, keepdims=True)
    centered = rows - mean
    variance = jnp.mean(centered * centered, axis=-1, keepdims=True)
    scale = lax.rsqrt(variance + EPSILON)
    return centered * scale, scale


def norm_forward(source, gain, shift, target, normals, scales, after=None):
    def one(step, carry):
        rows = rows16(step)
        normal, scale = statistics(source[rows])
        target[rows] = (normal * gain + shift).astype(BF16)
        normals[rows] = normal
        scales[rows] = jnp.broadcast_to(scale, (16, LANES))
        if after is not None:
            after(step)
        return carry

    lax.fori_loop(0, 16, one, 0, unroll=2)


def transpose_into(source, target):
    def one(step, carry):
        target[step] = source[:, lanes(step, LANES)].T
        return carry

    lax.fori_loop(0, PAIRS, one, 0)


class Swap:
    def __init__(self, place, send, recv, sems, index, to_positions, columns=slice(0, WIDTH)):
        self.place, self.send, self.recv, self.sems, self.index = place, send, recv, sems, index
        self.to_positions, self.columns = to_positions, columns

    def rows(self, ta):
        frames = rows16(ta)
        positions = rows16((ta % 2) * 8 + ta // 2)
        return (frames, positions) if self.to_positions else (positions, frames)

    def copy(self, step):
        device, ta = self.place.fellow(step)
        source = self.send.at[self.rows(ta)[0], self.columns]
        target = self.recv.at[self.rows(self.place.ta)[1], self.columns]
        return remote(source, target, self.sems.at[self.index, 0, step], self.sems.at[self.index, 1, step], device)

    def own(self):
        rows = self.rows(self.place.ta)
        source, target = self.send.at[rows[0], self.columns], self.recv.at[rows[1], self.columns]
        return pltpu.make_async_copy(source, target, self.sems.at[self.index, 0, 0])

    def start_block(self, ta):
        step = (ta - self.place.ta + 16) % 16

        @pl.when(step > 0)
        def _():
            self.copy(step).start()

        @pl.when(step == 0)
        def _():
            self.own().start()

    def start(self):
        def one(step, carry):
            self.copy(step).start()
            return carry

        lax.fori_loop(1, 16, one, 0)
        self.own().start()

    def wait(self):
        def one(step, carry):
            self.copy(step).wait_recv()
            return carry

        self.own().wait()
        lax.fori_loop(1, 16, one, 0)

    def sent(self):
        def one(step, carry):
            self.copy(step).wait_send()
            return carry

        lax.fori_loop(1, 16, one, 0)


HALVES = (slice(0, WIDTH // 2), slice(WIDTH // 2, WIDTH))


FORWARD_OUTS = dict(
    big_out=((128, WIDTH), BF16),
    small_out=((128, WIDTH), BF16),
    normal1=((ROWS, WIDTH), F32),
    normal2=((ROWS, WIDTH), F32),
    normal3=((ROWS, WIDTH), F32),
    scale1=((ROWS, LANES), F32),
    scale2=((ROWS, LANES), F32),
    scale3=((ROWS, LANES), F32),
    normed1_t=((PAIRS, LANES, ROWS), BF16),
    context1_t=((PAIRS, LANES, ROWS), BF16),
    normed2_t=((PAIRS, LANES, ROWS), BF16),
    context2_t=((PAIRS, LANES, ROWS), BF16),
    normed3_t=((PAIRS, LANES, ROWS), BF16),
    activated_t=((PAIRS, HIDE, ROWS), BF16),
    spatial=((PAIRS, SP_ROWS, LANES), BF16),
    temporal=((PAIRS, TP_ROWS, LANES), BF16),
    slope=((PAIRS, ROWS, HIDE), BF16),
)
FORWARD_WORK = dict(
    w_sqkv=((WIDTH, 3 * WIDTH), BF16),
    w_sout=((WIDTH, WIDTH), BF16),
    w_tqkv=((WIDTH, 3 * WIDTH), BF16),
    w_tout=((WIDTH, WIDTH), BF16),
    w_fin=((WIDTH, HIDDEN), BF16),
    w_fout=((HIDDEN, WIDTH), BF16),
    normed=((ROWS, WIDTH), BF16),
    context=((ROWS, WIDTH), BF16),
    arranged=((ROWS, WIDTH), BF16),
    context_send=((ROWS, WIDTH), BF16),
    context_back=((ROWS, WIDTH), BF16),
    normed3=((ROWS, WIDTH), BF16),
    total=((ROWS, WIDTH), F32),
    hidden=((ROWS, HIDE), F32),
    params=((16, WIDTH), F32),
    inner_bias=((PAIRS, HIDE), F32),
    table=((8, WIDTH), F32),
)


def named(keys, refs):
    return Names(**{key: refs.pop(0) for key in keys})


def forward_kernel(in_keys, vector_count, weight_keys, *refs):
    refs = list(refs)
    ins = named(in_keys, refs)
    vectors = [refs.pop(0) for _ in range(vector_count)]
    weights = named(weight_keys, refs)
    outs, keep, work = named(FORWARD_OUTS, refs), named(FORWARD_OUTS, refs), named(FORWARD_WORK, refs)
    w_sems, out_sems, swap_sems, far_sems = refs
    place = Place()
    params = work.params

    def param(row):
        return params[row : row + 1]

    loads = Names()
    for i, key in enumerate(weight_keys):
        setattr(loads, key, pltpu.make_async_copy(getattr(weights, key), getattr(work, key), w_sems.at[i]))
    loads.w_sqkv.start()
    for row, vector in enumerate(vectors):
        params[row : row + 1] = vector[...].astype(F32).reshape(1, WIDTH)
    for row in range(PAIRS):
        at = slice(row * HIDE, row * HIDE + HIDE)
        work.inner_bias[row : row + 1] = ins.inner_bias[at].astype(F32).reshape(1, HIDE)
    work.table[...] = ins.table[...].astype(F32)
    frame = place.ta // 2
    copies = []

    def save(source, target):
        copy = pltpu.make_async_copy(source, target, out_sems.at[len(copies)])
        copy.start()
        copies.append(copy)

    resid0, resid1, resid2 = keep.normal2, keep.normal3, work.total
    big_row = work.table[pl.ds(ins.big_actions[0, frame], 1)]

    def start_rows(step, carry):
        near = pl.ds(pl.multiple_of(step * 16, 16), 16)
        big = ins.big[near].astype(F32) + big_row
        small = ins.small[near].astype(F32) + work.table[pl.ds(ins.small_actions[step // 2, frame], 1)]
        rows = pl.ds(pl.multiple_of(step * 32, 32), 32)
        merged = interleave(big, small)
        resid0[rows] = merged
        normal, scale = statistics(merged)
        work.normed[rows] = (normal * param(0) + param(1)).astype(BF16)
        keep.normal1[rows] = normal
        keep.scale1[rows] = jnp.broadcast_to(scale, (32, LANES))
        return carry

    lax.fori_loop(0, 8, start_rows, 0)
    save(keep.normal1, outs.normal1)
    save(keep.scale1, outs.scale1)
    greet(place, False)

    spatial = keep.spatial
    loads.w_sqkv.wait()
    for key in weight_keys[1:]:
        getattr(loads, key).start()

    def spatial_project(column, base, per_family, scale):
        def one(step, carry):
            at = column + step
            value = dot(work.normed[...], work.w_sqkv[:, lanes(at, 256)]) * scale
            for which in range(2):
                one_family = family(value, which).astype(BF16)
                rows = pl.ds(base + which * per_family, 128)
                spatial[step * 2, rows] = one_family[:, :LANES]
                spatial[step * 2 + 1, rows] = one_family[:, LANES:]
            return carry

        lax.fori_loop(0, 4, one, 0)

    spatial_project(4, SP_KEY, 256, 1.0)
    spatial_project(8, SP_VALUE, 256, 1.0)
    far = []
    for i, base in enumerate((SP_KEY, SP_KEY + 256, SP_VALUE, SP_VALUE + 256)):
        far.append(
            remote(
                spatial.at[:, pl.ds(base, 128)], spatial.at[:, pl.ds(base + 128, 128)],
                far_sems.at[0, i], far_sems.at[1, i], place.partner,
            )
        )
    for copy in far:
        copy.start()
    spatial_project(0, SP_QUERY, 128, 0.125)
    transpose_into(work.normed, keep.normed1_t)
    save(keep.normed1_t, outs.normed1_t)
    for copy in far:
        copy.wait()

    low_q, low_k = half_masks(128), half_masks(256)
    key_slot = (lax.broadcasted_iota(jnp.int32, (256, 128), 0) % 128) // 32
    query_slot = lax.broadcasted_iota(jnp.int32, (256, 128), 1) // 32
    same_slot = key_slot == query_slot

    def softmax(scores):
        weights_ = jnp.exp(scores - jnp.max(scores, axis=0, keepdims=True))
        return (weights_ * (1.0 / jnp.sum(weights_, axis=0, keepdims=True))).astype(BF16)

    def spatial_pair(pair, carry):
        contexts = []
        for which in range(2):
            keys = spatial[pair, SP_KEY + which * 256 : SP_KEY + which * 256 + 256]
            values = spatial[pair, SP_VALUE + which * 256 : SP_VALUE + which * 256 + 256]
            queries = by_head(spatial[pair, SP_QUERY + which * 128 : SP_QUERY + which * 128 + 128], low_q)
            probs = []
            for head in range(2):
                scores = dot_nt(keys, queries[head])
                if which == 1:
                    scores = jnp.where(same_slot, scores, MASKED_SCORE)
                prob = softmax(scores)
                at = (which * 2 + head) * 256
                spatial[pair, at : at + 256] = prob
                probs.append(prob)
            contexts.append(
                dot_tn(jnp.concatenate(probs, axis=0), jnp.concatenate(by_head(values, low_k), axis=0))
            )
        work.context[:, lanes(pair, LANES)] = interleave(*contexts).astype(BF16)
        return carry

    lax.fori_loop(0, PAIRS, spatial_pair, 0)
    save(keep.spatial, outs.spatial)

    def project_into(source, weight, bias, before, target):
        def one(step, carry):
            at = lanes(step, 256)
            target[:, at] = dot(source[...], weight[:, at]) + params[bias : bias + 1, at] + before[:, at]
            return carry

        lax.fori_loop(0, WIDTH // 256, one, 0)

    loads.w_sout.wait()
    project_into(work.context, work.w_sout, 2, resid0, resid1)
    there = Swap(place, work.normed, work.arranged, swap_sems, 0, True)
    norm_forward(resid1, param(3), param(4), work.normed, keep.normal2, keep.scale2, there.start_block)
    save(keep.normal2, outs.normal2)
    save(keep.scale2, outs.scale2)
    transpose_into(work.context, keep.context1_t)
    save(keep.context1_t, outs.context1_t)
    loads.w_tqkv.wait()
    there.wait()

    temporal = keep.temporal

    def temporal_project(column, base, scale):
        def one(step, carry):
            value = dot(work.arranged[...], work.w_tqkv[:, lanes(column + step, 256)]) * scale
            value = value.astype(BF16)
            temporal[step * 2, base : base + ROWS] = value[:, :LANES]
            temporal[step * 2 + 1, base : base + ROWS] = value[:, LANES:]
            return carry

        lax.fori_loop(0, 4, one, 0)

    temporal_project(0, TP_QUERY, 0.125)
    temporal_project(4, TP_KEY, 1.0)
    temporal_project(8, TP_VALUE, 1.0)
    key_row = lax.broadcasted_iota(jnp.int32, (128, 128), 0)
    query_row = lax.broadcasted_iota(jnp.int32, (128, 128), 1)
    key_rank, query_rank = jnp.zeros_like(key_row), jnp.zeros_like(query_row)
    for at in range(8):
        big_rank, small_rank = ins.big_order[0, at], ins.small_order[place.ta // 4, at]
        key_rank = jnp.where(key_row // 16 == at, jnp.where(key_row % 16 < 8, big_rank, small_rank), key_rank)
        query_rank = jnp.where(query_row // 16 == at, jnp.where(query_row % 16 < 8, big_rank, small_rank), query_rank)
    seen = (key_row % 16 == query_row % 16) & (key_rank <= query_rank)

    def temporal_pair(pair, carry):
        contexts = []
        for half in range(2):
            keys = temporal[pair, TP_KEY + half * 128 : TP_KEY + half * 128 + 128]
            values = temporal[pair, TP_VALUE + half * 128 : TP_VALUE + half * 128 + 128]
            queries = by_head(temporal[pair, TP_QUERY + half * 128 : TP_QUERY + half * 128 + 128], low_q)
            probs = []
            for head in range(2):
                prob = softmax(jnp.where(seen, dot_nt(keys, queries[head]), MASKED_SCORE))
                at = (half * 2 + head) * 128
                temporal[pair, at : at + 128] = prob
                probs.append(prob)
            contexts.append(
                dot_tn(jnp.concatenate(probs, axis=0), jnp.concatenate(by_head(values, low_q), axis=0))
            )
        work.context_send[:, lanes(pair, LANES)] = jnp.concatenate(contexts, axis=0).astype(BF16)
        return carry

    back = [Swap(place, work.context_send, work.context_back, swap_sems, 1 + i, False, HALVES[i]) for i in range(2)]
    lax.fori_loop(0, PAIRS // 2, temporal_pair, 0)
    back[0].start()
    lax.fori_loop(PAIRS // 2, PAIRS, temporal_pair, 0)
    back[1].start()
    save(keep.temporal, outs.temporal)
    transpose_into(work.arranged, keep.normed2_t)
    save(keep.normed2_t, outs.normed2_t)
    loads.w_tout.wait()
    for i in range(2):
        back[i].wait()

        def add_half(step, carry, i=i):
            at = lanes(step, 256)
            value = dot(work.context_back[:, HALVES[i]], work.w_tout[HALVES[i], at])
            if i == 0:
                resid2[:, at] = value + params[5:6, at] + resid1[:, at]
            else:
                resid2[:, at] += value
            return carry

        lax.fori_loop(0, WIDTH // 256, add_half, 0)
    norm_forward(resid2, param(6), param(7), work.normed3, keep.normal3, keep.scale3)
    save(keep.normal3, outs.normal3)
    save(keep.scale3, outs.scale3)
    transpose_into(work.context_back, keep.context2_t)
    save(keep.context2_t, outs.context2_t)
    transpose_into(work.normed3, keep.normed3_t)
    save(keep.normed3_t, outs.normed3_t)

    total, hidden, slope = work.total, work.hidden, keep.slope
    total[...] += param(8)
    loads.w_fin.wait()
    loads.w_fout.wait()
    root = 0.7978845608028654

    def feed(step, carry):
        hidden[...] = dot(work.normed3[...], work.w_fin[:, lanes(step, HIDE)])

        def some(part, inner):
            rows = pl.ds(pl.multiple_of(part * 32, 32), 32)
            value = hidden[rows] + work.inner_bias[pl.ds(step, 1)]
            square = value * value
            bent = jnp.tanh(root * value * (1.0 + 0.044715 * square))
            half = 0.5 * (1.0 + bent)
            work.context_send[rows, :HIDE] = (value * half).astype(BF16)
            rise = half + 0.5 * value * (1.0 - bent * bent) * (root * (1.0 + 0.134145 * square))
            slope[step, rows] = rise.astype(BF16)
            return inner

        lax.fori_loop(0, 8, some, 0)
        active = work.context_send[:, :HIDE]
        for block in range(HIDE // LANES):
            at = slice(block * LANES, block * LANES + LANES)
            keep.activated_t[step, at] = work.context_send[:, at].T
        down = work.w_fout.at[pl.ds(pl.multiple_of(step * HIDE, HIDE), HIDE)]
        for column in range(WIDTH // 256):
            at = slice(column * 256, column * 256 + 256)
            total[:, at] += dot(active, down[:, at])
        return carry

    for one in back:
        one.sent()
    lax.fori_loop(0, PAIRS, feed, 0)
    save(keep.slope, outs.slope)
    save(keep.activated_t, outs.activated_t)

    def finish_rows(step, carry):
        value = total[pl.ds(pl.multiple_of(step * 32, 32), 32)]
        near = pl.ds(pl.multiple_of(step * 16, 16), 16)
        keep.big_out[near] = family(value, 0).astype(BF16)
        keep.small_out[near] = (family(value, 1) * ins.live[step // 2].astype(F32)).astype(BF16)
        return carry

    lax.fori_loop(0, 8, finish_rows, 0)
    save(keep.big_out, outs.big_out)
    save(keep.small_out, outs.small_out)
    there.sent()
    for copy in copies:
        copy.wait()


def forward(ins, scalars, vectors, weights):
    sem = pltpu.SemaphoreType.DMA
    kept, work = list(FORWARD_OUTS.values()), list(FORWARD_WORK.values())
    in_keys, weight_keys = tuple(vars(ins)) + tuple(vars(scalars)), tuple(vars(weights))
    results = pl.pallas_call(
        functools.partial(forward_kernel, in_keys, len(vectors), weight_keys),
        out_shape=[jax.ShapeDtypeStruct(shape, dtype) for shape, dtype in kept],
        in_specs=[VMEM] * len(vars(ins)) + [SMEM] * len(vars(scalars)) + [VMEM] * len(vectors) + [ANY] * len(weight_keys),
        out_specs=[ANY] * len(kept),
        scratch_shapes=[pltpu.VMEM(shape, dtype) for shape, dtype in kept + work]
        + [sem((len(weight_keys),)), sem((len(kept),)), sem((3, 2, 16)), sem((2, 4))],
        compiler_params=pltpu.CompilerParams(
            collective_id=1, has_side_effects=True, vmem_limit_bytes=62 * 2**20
        ),
        cost_estimate=pl.CostEstimate(flops=9 * 10**9, bytes_accessed=60 * 2**20, transcendentals=4 * 10**6),
        name="layer_forward",
    )(*vars(ins).values(), *vars(scalars).values(), *vectors, *vars(weights).values())
    return named(FORWARD_OUTS, list(results))


class Reduction:
    def __init__(self, place, index, refs, sems):
        self.place, self.index, self.refs, self.sems = place, index, refs, sems
        k, n, shares = MATRICES[index]
        self.half = n // 2
        self.depth = k // 64
        self.groups = self.depth // 16
        self.bounds, start = [], 0
        for share in shares:
            self.bounds.append((start, start + share))
            start += share
        self.units = start * self.groups
        self.first_unit = sum(m[1] // 2 // LANES * (m[0] // 1024) for m in MATRICES[:index])
        self.send_unit = SEND_UNITS[index]
        self.local_done = False
        self.straight = index >= 4

    def left_local(self):
        r, s, i = self.refs, self.sems, self.index
        return pltpu.make_async_copy(r.at_in, r.at.at[:, :, :, :, :, :ROWS], s.local.at[i, 0])

    def left_far(self):
        r, s, i = self.refs, self.sems, self.index
        target = r.at.at[:, :, :, :, :, ROWS:]
        return remote(r.at_in, target, s.ex_send.at[i, 0], s.ex_recv.at[i, 0], self.place.partner)

    def right_local(self):
        r, s, i, core = self.refs, self.sems, self.index, self.place.core
        source = r.source.at[:, lanes(core, self.half)]
        return pltpu.make_async_copy(source, r.g.at[:ROWS], s.local.at[i, 1])

    def right_far(self):
        r, s, i, core = self.refs, self.sems, self.index, self.place.core
        source = r.source.at[:, lanes(1 - core, self.half)]
        return remote(source, r.g.at[ROWS:], s.ex_send.at[i, 1], s.ex_recv.at[i, 1], self.place.partner)

    def lefts(self):
        self.left_far().start()
        self.left_local().start()

    def rights(self):
        self.right_far().start()
        self.right_local().start()

    def right_local_done(self):
        if not self.local_done:
            self.right_local().wait()
            self.local_done = True

    def rights_sent(self):
        self.right_local_done()
        self.right_far().wait_send()

    def loaded(self):
        self.left_far().wait_recv()
        self.right_far().wait_recv()
        self.left_local().wait()
        self.right_local_done()

    def span(self, part):
        low, high = self.bounds[part]
        return low * self.groups, high * self.groups

    def copy(self, part, stage, step):
        r, s, i = self.refs, self.sems, self.index
        low, high = self.span(part)
        here = slice(self.first_unit + low, self.first_unit + high)
        device, slot = self.place.along(ORDERS[part][stage], step)
        if stage == 1:
            source = r.r1.at[0, here, slot]
            target = r.r2.at[step - 1, here]
        else:
            source = r.r2.at[0, here, slot]
            target = r.r3.at[step - 1, here]
        return remote(
            source, target, s.send.at[i, part, stage, step - 1], s.recv.at[i, part, stage, step - 1], device
        )

    def left_block(self, part, slot, group):
        at = self.refs.at
        rows = slice(group * 16, group * 16 + 16)
        if part == 0:
            blocks = [at[y // 2, :, y % 2, slot, rows] for y in range(4)]
        elif part == 1:
            blocks = [at[slot // 2, :, slot % 2, :, rows]]
        else:
            blocks = [at[:, slot, :, x, rows] for x in range(4)]
        blocks = [block.reshape(-1, block.shape[-1]) for block in blocks]
        return blocks[0] if len(blocks) == 1 else jnp.concatenate(blocks, axis=0)

    def products(self, part, slot, emit):
        low, high = self.bounds[part]
        for group in range(self.groups):
            left = self.left_block(part, slot, group)
            for tile in range(low, high, 2):
                width = min(2, high - tile)
                value = dot(left, self.refs.g[:, tile * LANES : (tile + width) * LANES])
                for i in range(width):
                    one = value[:, i * LANES : (i + 1) * LANES].reshape(4, 4, 16, LANES)
                    emit((tile + i) * self.groups + group, one)

    def relay(self, part, way):
        r, s, i = self.refs, self.sems, self.index
        low, high = self.span(part)
        here = slice(self.first_unit + low, self.first_unit + high)
        half = slice(way * 2, way * 2 + 2)
        device = self.place.along(ORDERS[part][0], 3 if way else 1)[0]
        source = r.s1.at[0, self.send_unit + low : self.send_unit + high, half]
        target = r.r1.at[2, here, half]
        return remote(source, target, s.send.at[i, part, 0, way], s.recv.at[i, part, 0, way], device)

    def direct(self, part, way):
        r, s, i = self.refs, self.sems, self.index
        low, high = self.span(part)
        here = slice(self.first_unit + low, self.first_unit + high)
        device = self.place.along(ORDERS[part][0], 3 if way else 1)[0]
        source = r.s1.at[1 + way, self.send_unit + low : self.send_unit + high]
        target = r.r1.at[way, here]
        return remote(source, target, s.send.at[i, part, 0, 2 + way], s.recv.at[i, part, 0, 2 + way], device)

    def first(self, parts=ALL):
        r = self.refs
        for part in parts:
            slot = self.place.along(ORDERS[part][0], 2)[1]

            def emit(unit, value):
                r.s1[0, self.send_unit + unit] = value.astype(BF16)

            self.products(part, slot, emit)
            for way in range(2):
                self.relay(part, way).start()

    def pass_on(self, parts=ALL):
        r = self.refs
        for part in parts:
            for way in range(2):
                self.relay(part, way).wait_recv()
                slot = self.place.along(ORDERS[part][0], 3 if way else 1)[1]

                def emit(unit, value, way=way):
                    at = self.first_unit + unit
                    for half in range(2):
                        some = slice(half * 2, half * 2 + 2)
                        one = value[some]
                        if half == way:
                            one = one + r.r1[2, at, some].astype(F32)
                        r.s1[1 + way, self.send_unit + unit, some] = one.astype(BF16)

                self.products(part, slot, emit)
                self.direct(part, way).start()

    def relay_sent(self):
        for part in range(3):
            for way in range(2):
                self.relay(part, way).wait_send()

    def direct_sent(self):
        for part in range(3):
            for way in range(2):
                self.direct(part, way).wait_send()

    def second(self, parts=ALL):
        r = self.refs
        for part in parts:
            slot = self.place.along(ORDERS[part][0], 0)[1]
            for way in range(2):
                self.direct(part, way).wait_recv()

            def emit(unit, value):
                at = self.first_unit + unit
                for i in range(2):
                    value = value + r.r1[i, at].astype(F32)
                r.r1[0, at] = value.astype(BF16)

            self.products(part, slot, emit)
            for step in (1, 2, 3):
                self.copy(part, 1, step).start()

    def third(self, parts=ALL):
        r = self.refs
        for part in parts:
            slot = self.place.along(ORDERS[part][1], 0)[1]
            for step in (1, 2, 3):
                self.copy(part, 1, step).wait_recv()

            def one(unit, carry, slot=slot):
                value = r.r1[0, unit, slot].astype(F32)
                for i in range(3):
                    value = value + r.r2[i, unit].astype(F32)
                r.r2[0, unit] = value.astype(BF16)
                return carry

            low, high = self.span(part)
            lax.fori_loop(self.first_unit + low, self.first_unit + high, one, 0)
            for step in (1, 2, 3):
                self.copy(part, 2, step).start()

    def mine(self):
        return self.place.y_hi * 4 + self.place.x

    def gather_copy(self, y_hi, x, slot):
        r, s, i, place = self.refs, self.sems, self.index, self.place
        target = r.out.at[slot // 4, slot % 4, :, lanes(place.core, self.half)]
        return remote(
            r.piece.at[place.y_hi], target, s.ag_send.at[i, y_hi * 4 + x], s.ag_recv.at[i, slot],
            place.device(y_hi=y_hi, x=x),
        )

    def twin_copy(self):
        r, s, i, place = self.refs, self.sems, self.index, self.place
        block = r.piece.at[place.y_hi]
        return remote(block, block, s.ag_send.at[i, 0], s.ag_recv.at[i, 0], place.device(y_hi=1 - place.y_hi))

    def line_copy(self, step):
        r, s, i, place = self.refs, self.sems, self.index, self.place
        target = r.out.at[:, place.x, :, lanes(place.core, self.half)]
        device = place.device(x=(place.x + step) % 4)
        return remote(r.piece, target, s.ag_send.at[i, step], s.ag_recv.at[i, step], device)

    def own_copy(self):
        place, i, piece = self.place, self.index, self.refs.piece
        columns = lanes(place.core, self.half)
        if self.straight:
            target = self.refs.out.at[place.y_hi, place.x, :, columns]
            return pltpu.make_async_copy(piece.at[place.y_hi], target, self.sems.local.at[i, 2])
        return pltpu.make_async_copy(piece, self.refs.out.at[:, place.x, :, columns], self.sems.local.at[i, 2])

    def others(self):
        place = self.place
        for y_step in (0, 1):
            y_hi = (place.y_hi + y_step) % 2
            for x_step in range(4):
                if y_step or x_step:
                    yield y_hi, (place.x + x_step) % 4

    def fourth(self, parts=ALL):
        r = self.refs
        for part in parts:
            slot = self.place.along(ORDERS[part][2], 0)[1]
            for step in (1, 2, 3):
                self.copy(part, 2, step).wait_recv()
            low, high = self.span(part)
            for unit in range(low, high):
                at = self.first_unit + unit
                value = r.r2[0, at, slot].astype(F32)
                for i in range(3):
                    value = value + r.r3[i, at].astype(F32)
                tile, group = unit // self.groups, unit % self.groups
                rows, columns = slice(group * 16, group * 16 + 16), slice(tile * LANES, tile * LANES + LANES)
                r.piece[self.place.y_hi, rows, columns] = value.astype(BF16)
    def gather(self):
        if self.straight:
            self.own_copy().start()
            for y_hi, x in self.others():
                self.gather_copy(y_hi, x, self.mine()).start()
        else:
            self.twin_copy().start()

    def spread(self):
        if not self.straight:
            self.twin_copy().wait_recv()
            self.own_copy().start()
            for step in (1, 2, 3):
                self.line_copy(step).start()

    def cross_copy(self):
        r, s, i, core = self.refs, self.sems, self.index, self.place.core
        block = r.out.at[:, :, :, lanes(core, self.half)]
        return remote(block, block, s.cross.at[i, 0], s.cross.at[i, 1], self.place.partner)

    def fifth(self):
        self.own_copy().wait()
        if self.straight:
            for y_hi, x in self.others():
                self.gather_copy(y_hi, x, y_hi * 4 + x).wait_recv()
        else:
            for step in (1, 2, 3):
                self.line_copy(step).wait_recv()
        self.cross_copy().start()

    def finish(self):
        self.cross_copy().wait()
        self.left_far().wait_send()
        if self.straight:
            for y_hi, x in self.others():
                self.gather_copy(y_hi, x, self.mine()).wait_send()
        else:
            self.twin_copy().wait_send()
            for step in (1, 2, 3):
                self.line_copy(step).wait_send()
        for part in range(3):
            for stage in (1, 2):
                for step in (1, 2, 3):
                    self.copy(part, stage, step).wait_send()


GAIN1, SHIFT1, SPATIAL_BIAS, GAIN2, SHIFT2, TEMPORAL_BIAS, GAIN3, SHIFT3, INNER, OUTER = 8, 9, 10, 11, 12, 13, 14, 15, 16, 20


class SmallSums:
    def __init__(self, place, refs, sems):
        self.place, self.refs, self.sems = place, refs, sems

    def share(self, core):
        return slice(None), lanes(core, WIDTH // 2)

    def cross(self):
        r, core = self.refs, self.place.core
        return remote(
            r.sums.at[self.share(1 - core)], r.sums_core, self.sems.at[0, 0, 0], self.sems.at[1, 0, 0],
            self.place.partner,
        )

    def along(self, stage, step):
        device = self.place.along("xyz"[stage], step)[0]
        return remote(
            self.refs.sums_total.at[stage], self.refs.sums_recv.at[stage, step - 1],
            self.sems.at[0, stage + 1, step - 1], self.sems.at[1, stage + 1, step - 1], device,
        )

    def final(self):
        block = self.refs.sums_final.at[self.share(self.place.core)]
        return remote(block, block, self.sems.at[0, 4, 0], self.sems.at[1, 4, 0], self.place.partner)

    def begin(self):
        self.cross().start()

    def step0(self):
        r = self.refs
        self.cross().wait()
        r.sums_total[0] = r.sums[self.share(self.place.core)] + r.sums_core[...]
        for step in (1, 2, 3):
            self.along(0, step).start()

    def advance(self, stage):
        r = self.refs
        value = r.sums_total[stage]
        for step in (1, 2, 3):
            self.along(stage, step).wait_recv()
            value = value + r.sums_recv[stage, step - 1]
        if stage < 2:
            r.sums_total[stage + 1] = value
            for step in (1, 2, 3):
                self.along(stage + 1, step).start()
        else:
            r.sums_final[self.share(self.place.core)] = value
            self.final().start()

    def finish(self, out, sem):
        self.final().wait()
        copy = pltpu.make_async_copy(self.refs.sums_final, out, sem)
        copy.start()
        for stage in range(3):
            for step in (1, 2, 3):
                self.along(stage, step).wait_send()
        copy.wait()


BACK_OUTS = dict(
    big_grad=((128, WIDTH), F32),
    small_grad=((128, WIDTH), F32),
    small_sums=((24, WIDTH), F32),
)
SLOTS = 3
BACK_WORK = dict(
    s1=((3, 32, 4, 4, 16, LANES), BF16),
    r1=((3, 64, 4, 4, 16, LANES), BF16),
    r2=((3, 64, 4, 16, LANES), BF16),
    r3=((3, 64, 16, LANES), BF16),
    tall=((SLOTS, HIDE, WIDTH), BF16),
    broad=((SLOTS, WIDTH, HIDE), BF16),
    slope_in=((SLOTS, ROWS, HIDE), BF16),
    record=((SLOTS, SP_ROWS, LANES), BF16),
    resid=((ROWS, WIDTH), F32),
    grad=((ROWS, WIDTH), F32),
    total=((ROWS, WIDTH), F32),
    low3=((ROWS, WIDTH), BF16),
    low2=((ROWS, WIDTH), BF16),
    low1=((ROWS, WIDTH), BF16),
    hidden_low=((ROWS, HIDDEN), BF16),
    packed=((ROWS, 3 * WIDTH), BF16),
    swap_send=((ROWS, WIDTH), BF16),
    context_back=((ROWS, WIDTH), BF16),
    normed_back=((ROWS, WIDTH), BF16),
    context_grad=((2, 128, WIDTH), BF16),
    far_send=((ROWS, 2 * WIDTH), BF16),
    far_recv=((ROWS, 2 * WIDTH), BF16),
    inner_sums=((PAIRS, HIDE), F32),
    sums=((24, WIDTH), F32),
    sums_core=((24, WIDTH // 2), F32),
    sums_total=((3, 24, WIDTH // 2), F32),
    sums_recv=((3, 3, 24, WIDTH // 2), F32),
    sums_final=((24, WIDTH), F32),
    frame_sums=((8, WIDTH), F32),
    scale=((ROWS, LANES), F32),
    gains=((8, WIDTH), F32),
)


BACK_SEMS = dict(
    local=(6, 3),
    ex_send=(6, 2),
    ex_recv=(6, 2),
    send=(6, 3, 3, 4),
    recv=(6, 3, 3, 4),
    ag_send=(6, 8),
    ag_recv=(6, 8),
    cross=(6, 2),
    ring=(4, SLOTS),
    io=(5,),
    swap=(3, 2, 16),
    far=(2,),
    sums=(2, 5, 3),
)


def backward_kernel(in_keys, saved_keys, weight_keys, *refs):
    refs = list(refs)
    count = len(MATRICES)
    ins = named(in_keys, refs)
    gains = [refs.pop(0) for _ in range(3)]
    lefts = [refs.pop(0) for _ in range(count)]
    saved, weights, outs = named(saved_keys, refs), named(weight_keys, refs), named(BACK_OUTS, refs)
    matrix_outs = [refs.pop(0) for _ in range(count)]
    work = named(BACK_WORK, refs)
    ats, gs, pieces = ([refs.pop(0) for _ in range(count)] for _ in range(3))
    sems = named(BACK_SEMS, refs)
    ring_sems, io_sems, swap_sems, far_sems, sum_sems = sems.ring, sems.io, sems.swap, sems.far, sems.sums
    place = Place()
    frame = place.ta // 2
    sources = (work.low3, work.hidden_low, work.low2, work.packed, work.low1, work.packed)
    reductions = []
    for i in range(count):
        own = Names(at_in=lefts[i], at=ats[i], g=gs[i], piece=pieces[i], out=matrix_outs[i], source=sources[i])
        own.s1, own.r1, own.r2, own.r3 = work.s1, work.r1, work.r2, work.r3
        reductions.append(Reduction(place, i, own, sems))
    fout, fin, tout, tqkv, sout, sqkv = reductions
    small = SmallSums(place, work, sum_sems)

    def tall(source, base, index):
        slot = (base + index) % SLOTS
        rows = pl.ds(pl.multiple_of(index * HIDE, HIDE), HIDE)
        return pltpu.make_async_copy(source.at[rows], work.tall.at[slot], ring_sems.at[0, slot])

    def broad(source, base, index):
        slot = (base + index) % SLOTS
        return pltpu.make_async_copy(
            source.at[:, lanes(index, HIDE)], work.broad.at[slot], ring_sems.at[1, slot]
        )

    def slope(base, index):
        slot = (base + index) % SLOTS
        return pltpu.make_async_copy(saved.slope.at[index], work.slope_in.at[slot], ring_sems.at[2, slot])

    def record(source, base, index):
        slot = (base + index) % SLOTS
        return pltpu.make_async_copy(
            source.at[index], work.record.at[slot, pl.ds(0, source.shape[1])], ring_sems.at[3, slot]
        )

    def open_stream(maker, count):
        for index in range(min(SLOTS, count)):
            maker(index).start()

    def refill(maker, count, index):
        @pl.when(index + SLOTS < count)
        def _():
            maker(index + SLOTS).start()

    fout_tiles = functools.partial(tall, weights.w_fout, 0)
    tout_tiles = functools.partial(tall, weights.w_tout, 8)
    sout_tiles = functools.partial(tall, weights.w_sout, 10)
    fin_tiles = functools.partial(broad, weights.w_fin, 0)
    tqkv_tiles = functools.partial(broad, weights.w_tqkv, 8)
    sqkv_tiles = functools.partial(broad, weights.w_sqkv, 14)
    slopes = functools.partial(slope, 0)
    temporal_records = functools.partial(record, saved.temporal, 0)
    spatial_records = functools.partial(record, saved.spatial, 8)

    class Kept:
        def __init__(self, normals, scales):
            self.copies = (
                pltpu.make_async_copy(normals, work.resid, io_sems.at[0]),
                pltpu.make_async_copy(scales, work.scale, io_sems.at[4]),
            )
            for copy in self.copies:
                copy.start()

        def wait(self):
            for copy in self.copies:
                copy.wait()

    open_stream(fout_tiles, 8)
    open_stream(slopes, 8)
    open_stream(fin_tiles, 8)
    kept3 = Kept(saved.normal3, saved.scale3)
    open_stream(temporal_records, 8)
    work.sums[...] = jnp.zeros_like(work.sums)
    for row, gain in enumerate(gains):
        work.gains[row : row + 1] = gain[...].astype(F32).reshape(1, WIDTH)
    greet(place, True)
    for one in reductions:
        one.lefts()

    grad, total = work.grad, work.total

    def start_rows(step, carry):
        near = pl.ds(pl.multiple_of(step * 16, 16), 16)
        big = ins.big_cot[near].astype(F32)
        little = ins.small_cot[near].astype(F32) * ins.live[step // 2].astype(F32)
        merged = interleave(big, little)
        rows = pl.ds(pl.multiple_of(step * 32, 32), 32)
        grad[rows] = merged
        work.low3[rows] = merged.astype(BF16)
        total[rows] = jnp.zeros_like(merged)
        work.sums[OUTER : OUTER + 1] += jnp.sum(merged, axis=0, keepdims=True)
        return carry

    lax.fori_loop(0, 8, start_rows, 0)
    fout.rights()

    def feed(step, carry):
        slopes(step).wait()
        fout_tiles(step).wait()
        fin_tiles(step).wait()
        slot = step % SLOTS
        down = dot_nt(work.low3[...], work.tall[slot]) * work.slope_in[slot].astype(F32)
        work.inner_sums[pl.ds(step, 1)] = jnp.sum(down, axis=0, keepdims=True)
        low = down.astype(BF16)
        work.hidden_low[:, lanes(step, HIDE)] = low
        for column in range(WIDTH // 256):
            at = slice(column * 256, column * 256 + 256)
            total[:, at] += dot_nt(low, work.broad[slot, at])
        refill(slopes, 8, step)
        refill(fout_tiles, 8, step)
        refill(fin_tiles, 8, step)
        return carry

    lax.fori_loop(0, 4, feed, 0)
    fout.loaded()
    fout.first()
    lax.fori_loop(4, 8, feed, 0)
    fin.rights()
    open_stream(tout_tiles, 2)
    open_stream(sout_tiles, 1)
    open_stream(tqkv_tiles, 6)
    for part in range(PAIRS):
        at = part % 2 * HIDE
        work.sums[INNER + part // 2 : INNER + part // 2 + 1, at : at + HIDE] = work.inner_sums[part : part + 1]

    def norm_back(gradient, gain_row, row, low, bias_row):
        gain = work.gains[gain_row : gain_row + 1]

        def one(step, carry):
            rows = rows16(step)
            error = gradient[rows].astype(F32)
            normal, scale = work.resid[rows], work.scale[rows, 0:1]
            scaled = error * gain
            mean_one = jnp.mean(scaled, axis=-1, keepdims=True)
            mean_two = jnp.mean(scaled * normal, axis=-1, keepdims=True)
            value = grad[rows] + (scaled - mean_one - normal * mean_two) * scale
            grad[rows] = value
            if low is not None:
                low[rows] = value.astype(BF16)
            gains = error * normal
            sums = [part[:8] + part[8:] for part in (gains, error, value)]
            return tuple(a + b for a, b in zip(carry, sums))

        zero = jnp.zeros((8, WIDTH), F32)
        sums = lax.fori_loop(0, 16, one, (zero, zero, zero), unroll=2)
        work.sums[row : row + 1] = jnp.sum(sums[0], axis=0, keepdims=True)
        work.sums[row + 1 : row + 2] = jnp.sum(sums[1], axis=0, keepdims=True)
        if bias_row is not None:
            work.sums[bias_row : bias_row + 1] = jnp.sum(sums[2], axis=0, keepdims=True)

    kept3.wait()
    norm_back(total, 2, GAIN3, work.low2, TEMPORAL_BIAS)
    kept2 = Kept(saved.normal2, saved.scale2)
    tout.rights()

    there = [Swap(place, work.swap_send, work.context_back, swap_sems, i, True, HALVES[i]) for i in range(2)]
    for index in range(2):
        tout_tiles(index).wait()
        slot = (8 + index) % SLOTS
        work.swap_send[:, HALVES[index]] = dot_nt(work.low2[...], work.tall[slot]).astype(BF16)
        there[index].start()
    sout_tiles(1).start()
    fout.pass_on(Z)
    fin.loaded()
    fin.first(Z)
    there[0].wait()
    fout.pass_on(XY)
    fin.first(XY)

    low_lanes = half_masks(128)
    low_lanes_wide = half_masks(256)

    def attention_back(probs, keys, values, queries, upstream, wide):
        key_low = low_lanes_wide if wide else low_lanes
        upstreams = by_head(upstream, low_lanes)
        errors = []
        for head in range(2):
            prob = probs[head].astype(F32)
            back = dot_nt(values, upstreams[head])
            delta = jnp.sum(prob * back, axis=0, keepdims=True)
            errors.append((prob * (back - delta)).astype(BF16))
        key_grad = dot(jnp.concatenate(errors, axis=1), jnp.concatenate(by_head(queries, low_lanes), axis=0))
        value_grad = dot(jnp.concatenate(probs, axis=1), jnp.concatenate(upstreams, axis=0))
        query_grad = dot_tn(jnp.concatenate(errors, axis=0), jnp.concatenate(by_head(keys, key_low), axis=0))
        return query_grad * 0.125, key_grad, value_grad

    def temporal_pair(pair, carry):
        temporal_records(pair).wait()
        slot = pair % SLOTS
        for half in range(2):
            base = half * 128

            def rows(start, half=half):
                return work.record[slot, start + half * 128 : start + half * 128 + 128]

            probs = [work.record[slot, (half * 2 + h) * 128 : (half * 2 + h) * 128 + 128] for h in range(2)]
            upstream = work.context_back[base : base + 128, lanes(pair, LANES)]
            grads = attention_back(probs, rows(TP_KEY), rows(TP_VALUE), rows(TP_QUERY), upstream, False)
            for i, value in enumerate(grads):
                work.packed[base : base + 128, lanes(pair + i * PAIRS, LANES)] = value.astype(BF16)
        refill(temporal_records, 8, pair)
        return carry

    lax.fori_loop(0, PAIRS // 2, temporal_pair, 0)
    there[1].wait()
    lax.fori_loop(PAIRS // 2, PAIRS, temporal_pair, 0)
    open_stream(spatial_records, 8)
    tqkv.rights()

    def project_back(maker, base, start, stop):
        def one(step, carry):
            maker(step).wait()
            slot = (base + step) % SLOTS
            low = work.packed[:, lanes(step, HIDE)]
            for column in range(WIDTH // 256):
                at = slice(column * 256, column * 256 + 256)
                value = dot_nt(low, work.broad[slot, at])
                total[:, at] += value
            refill(maker, 6, step)
            return carry

        if start == 0:
            total[...] = jnp.zeros_like(total)
        lax.fori_loop(start, stop, one, 0)

    project_back(tqkv_tiles, 8, 0, 3)
    fin.pass_on(Z)
    fout.relay_sent()
    tout.loaded()
    tout.first()
    tqkv.loaded()
    tqkv.first()
    project_back(tqkv_tiles, 8, 3, 6)
    open_stream(sqkv_tiles, 6)
    for one in there:
        one.sent()
    work.swap_send[...] = total[...].astype(BF16)
    back = Swap(place, work.swap_send, work.normed_back, swap_sems, 2, False)
    back.start()
    fout.second((1,))
    fout.direct_sent()
    back.wait()
    tout.pass_on()
    tqkv.pass_on()
    fin.pass_on(XY)
    fout.second((0, 2))

    kept2.wait()
    norm_back(work.normed_back, 1, GAIN2, work.low1, SPATIAL_BIAS)
    kept1 = Kept(saved.normal1, saved.scale1)
    sout.rights()
    for index in range(2):
        sout_tiles(index).wait()
        slot = (10 + index) % SLOTS
        at = slice(index * HIDE, index * HIDE + HIDE)
        value = dot_nt(work.low1[...], work.tall[slot])
        for which in range(2):
            work.context_grad[which, :, at] = family(value, which).astype(BF16)
    tqkv.rights_sent()

    def spatial_pair(pair, carry):
        spatial_records(pair).wait()
        slot = (8 + pair) % SLOTS
        all_grads = []
        for which in range(2):

            def rows(start, count, which=which):
                return work.record[slot, start + which * count : start + which * count + count]

            probs = [work.record[slot, (which * 2 + h) * 256 : (which * 2 + h) * 256 + 256] for h in range(2)]
            upstream = work.context_grad[which, :, lanes(pair, LANES)]
            all_grads.append(
                attention_back(
                    probs, rows(SP_KEY, 256), rows(SP_VALUE, 256), rows(SP_QUERY, 128), upstream, True
                )
            )
        for i in range(3):
            value = interleave(all_grads[0][i][:128], all_grads[1][i][:128])
            work.packed[:, lanes(pair + i * PAIRS, LANES)] = value.astype(BF16)
        for i in (1, 2):
            value = interleave(all_grads[0][i][128:], all_grads[1][i][128:])
            work.far_send[:, lanes(pair + (i - 1) * PAIRS, LANES)] = value.astype(BF16)
        refill(spatial_records, 8, pair)
        return carry

    lax.fori_loop(0, PAIRS // 2, spatial_pair, 0)
    fin.second(Z)
    lax.fori_loop(PAIRS // 2, PAIRS, spatial_pair, 0)
    far = remote(work.far_send, work.far_recv, far_sems.at[0], far_sems.at[1], place.partner)
    far.start()
    fin.relay_sent()
    sout.loaded()
    sout.first()
    fin.second(XY)
    far.wait()

    def join(step, carry):
        rows = rows16(step)
        value = work.packed[rows, WIDTH:].astype(F32) + work.far_recv[rows].astype(F32)
        work.packed[rows, WIDTH:] = value.astype(BF16)
        return carry

    lax.fori_loop(0, 16, join, 0)
    sqkv.rights()
    project_back(sqkv_tiles, 14, 0, 2)
    sqkv.loaded()
    sqkv.first()
    fout.third()
    project_back(sqkv_tiles, 14, 2, 4)
    fin.direct_sent()
    sqkv.pass_on()
    sout.pass_on()
    project_back(sqkv_tiles, 14, 4, 6)
    tout.second()
    tqkv.second()
    fout.fourth()
    fout.gather()
    kept1.wait()
    norm_back(total, 0, GAIN1, None, None)

    def finish_rows(step, carry):
        value = grad[pl.ds(pl.multiple_of(step * 32, 32), 32)]
        big, little = family(value, 0), family(value, 1)
        near = pl.ds(pl.multiple_of(step * 16, 16), 16)
        total[near] = big
        total[pl.ds(pl.multiple_of(128 + step * 16, 16), 16)] = little
        work.frame_sums[0:1] += jnp.sum(big, axis=0, keepdims=True)
        work.frame_sums[pl.ds(1 + step // 2, 1)] += jnp.sum(little, axis=0, keepdims=True)
        return carry

    work.frame_sums[...] = jnp.zeros_like(work.frame_sums)
    lax.fori_loop(0, 8, finish_rows, 0)
    out_copies = [
        pltpu.make_async_copy(total.at[:128], outs.big_grad, io_sems.at[1]),
        pltpu.make_async_copy(total.at[128:], outs.small_grad, io_sems.at[2]),
    ]
    for copy in out_copies:
        copy.start()
    table, at_row = jnp.zeros((8, WIDTH), F32), lax.broadcasted_iota(jnp.int32, (8, WIDTH), 0)
    for i in range(5):
        action = ins.big_actions[0, frame] if i == 0 else ins.small_actions[i - 1, frame]
        table = table + jnp.where(at_row == action, work.frame_sums[i : i + 1], 0.0)
    work.sums[0:8] = table
    small.begin()
    fin.third()
    small.step0()
    sqkv.second()
    sout.second()
    fout.spread()
    tout.third()
    tqkv.third()
    small.advance(0)
    fin.fourth()
    fin.gather()
    sqkv.third()
    sout.third()
    small.advance(1)
    tout.fourth()
    tout.gather()
    tqkv.fourth()
    tqkv.gather()
    fout.fifth()
    fin.spread()
    sqkv.fourth()
    sqkv.gather()
    sout.fourth()
    sout.gather()
    small.advance(2)
    tout.spread()
    tqkv.spread()
    fin.fifth()
    sqkv.fifth()
    sout.fifth()
    tout.fifth()
    tqkv.fifth()
    small.finish(outs.small_sums, io_sems.at[3])
    for one in reductions:
        one.finish()
    for one in (tout, tqkv, sout, sqkv):
        one.relay_sent()
        one.direct_sent()
    for one in (fout, fin, tout, sout, sqkv):
        one.rights_sent()
    back.sent()
    for copy in out_copies:
        copy.wait()


def backward(ins, scalars, gains, lefts, saved, weights):
    sem = pltpu.SemaphoreType.DMA
    count = len(MATRICES)
    work = [pltpu.VMEM(shape, dtype) for shape, dtype in BACK_WORK.values()]
    work += [pltpu.VMEM((2, 4, 2, 4, k // 64, 2 * ROWS), BF16) for k, _, _ in MATRICES]
    work += [pltpu.VMEM((2 * ROWS, n // 2), BF16) for _, n, _ in MATRICES]
    work += [pltpu.VMEM((2, k // 64, n // 2), BF16) for k, n, _ in MATRICES]
    work += [sem(shape) for shape in BACK_SEMS.values()]
    shapes = list(BACK_OUTS.values()) + [((2, 4, k // 64, n), BF16) for k, n, _ in MATRICES]
    in_keys, saved_keys, weight_keys = tuple(vars(ins)) + tuple(vars(scalars)), tuple(vars(saved)), tuple(vars(weights))
    return pl.pallas_call(
        functools.partial(backward_kernel, in_keys, saved_keys, weight_keys),
        out_shape=[jax.ShapeDtypeStruct(shape, dtype) for shape, dtype in shapes],
        in_specs=[VMEM] * len(vars(ins))
        + [SMEM] * len(vars(scalars))
        + [VMEM] * len(gains)
        + [ANY] * (count + len(saved_keys) + len(weight_keys)),
        out_specs=[ANY] * len(shapes),
        scratch_shapes=work,
        compiler_params=pltpu.CompilerParams(
            collective_id=2, has_side_effects=True, vmem_limit_bytes=63 * 2**20
        ),
        cost_estimate=pl.CostEstimate(flops=18 * 10**9, bytes_accessed=80 * 2**20, transcendentals=0),
        name="layer_backward",
    )(
        *vars(ins).values(),
        *vars(scalars).values(),
        *gains,
        *[left.reshape(2, 4, 2, 4, k // 64, ROWS) for left, (k, _, _) in zip(lefts, MATRICES)],
        *vars(saved).values(),
        *vars(weights).values(),
    )


SUM_VECTORS = (
    (GAIN1, 1),
    (SHIFT1, 1),
    (SPATIAL_BIAS, 1),
    (GAIN2, 1),
    (SHIFT2, 1),
    (TEMPORAL_BIAS, 1),
    (GAIN3, 1),
    (SHIFT3, 1),
    (INNER, 4),
    (OUTER, 1),
)


def widen_kernel(*refs):
    refs = list(refs)
    count, passed = len(MATRICES), 4
    narrow = [refs.pop(0) for _ in range(count)]
    plain = [refs.pop(0) for _ in range(passed)]
    sums = refs.pop(0)
    wide = [refs.pop(0) for _ in range(count)]
    plain_out = [refs.pop(0) for _ in range(passed)]
    table, vectors = refs.pop(0), [refs.pop(0) for _ in SUM_VECTORS]
    narrow_in, wide_out = refs[:count], refs[count : 2 * count]
    between, sems = refs[2 * count : 2 * count + passed], refs[2 * count + passed]
    loads = [pltpu.make_async_copy(narrow[i], narrow_in[i], sems.at[0, i]) for i in range(count)]
    stores = [pltpu.make_async_copy(wide_out[i], wide[i], sems.at[1, i]) for i in range(count)]
    reads = [pltpu.make_async_copy(plain[i], between[i], sems.at[2, i]) for i in range(passed)]
    moves = [pltpu.make_async_copy(between[i], plain_out[i], sems.at[3, i]) for i in range(passed)]
    for copy in loads + reads:
        copy.start()
    table[...] = sums[0:8]
    for (row, rows), vector in zip(SUM_VECTORS, vectors):
        for i in range(rows):
            vector[i * WIDTH : (i + 1) * WIDTH] = sums[row + i]
    for i in range(count):
        loads[i].wait()

        def one(step, carry, i=i):
            wide_out[i][rows16(step)] = narrow_in[i][rows16(step)].astype(F32)
            return carry

        lax.fori_loop(0, narrow_in[i].shape[0] // 16, one, 0, unroll=2)
        stores[i].start()
    for read, move in zip(reads, moves):
        read.wait()
        move.start()
    for copy in stores + moves:
        copy.wait()


def widen(matrices, plain, sums):
    count = len(matrices)
    vectors = [jax.ShapeDtypeStruct((rows * WIDTH,), F32) for _, rows in SUM_VECTORS]
    shapes = [jax.ShapeDtypeStruct(one.shape, F32) for one in matrices]
    scratch = [pltpu.VMEM(one.shape, BF16) for one in matrices] + [pltpu.VMEM(one.shape, F32) for one in matrices]
    scratch += [pltpu.VMEM(one.shape, one.dtype) for one in plain]
    results = pl.pallas_call(
        widen_kernel,
        out_shape=shapes
        + [jax.ShapeDtypeStruct(one.shape, one.dtype) for one in plain]
        + [jax.ShapeDtypeStruct((8, WIDTH), F32)]
        + vectors,
        in_specs=[ANY] * (count + len(plain)) + [VMEM],
        out_specs=[ANY] * (count + len(plain)) + [VMEM] * (1 + len(vectors)),
        scratch_shapes=scratch + [pltpu.SemaphoreType.DMA((4, count))],
        compiler_params=pltpu.CompilerParams(vmem_limit_bytes=62 * 2**20),
        cost_estimate=pl.CostEstimate(flops=0, bytes_accessed=14 * 2**20, transcendentals=0),
        name="widen",
    )(*matrices, *plain, sums)
    results = list(results)
    wide = [results.pop(0) for _ in range(count)]
    passed = [results.pop(0) for _ in plain]
    return wide, passed, results


def body(
    big_tokens,
    small_tokens,
    big_actions,
    small_actions,
    big_order,
    small_order,
    small_live,
    action_table,
    norm1_gain,
    norm1_bias,
    spatial_qkv,
    spatial_out,
    spatial_out_bias,
    norm2_gain,
    norm2_bias,
    temporal_qkv,
    temporal_out,
    temporal_out_bias,
    norm3_gain,
    norm3_bias,
    ffn_in,
    ffn_in_bias,
    ffn_out,
    ffn_out_bias,
    big_cotangent,
    small_cotangent,
):
    scalars = Names(
        big_actions=big_actions,
        small_actions=small_actions,
        big_order=big_order,
        small_order=small_order,
        live=small_live,
    )
    vectors = (
        norm1_gain,
        norm1_bias,
        spatial_out_bias,
        norm2_gain,
        norm2_bias,
        temporal_out_bias,
        norm3_gain,
        norm3_bias,
        ffn_out_bias,
    )
    weights = Names(
        w_sqkv=spatial_qkv,
        w_sout=spatial_out,
        w_tqkv=temporal_qkv,
        w_tout=temporal_out,
        w_fin=ffn_in,
        w_fout=ffn_out,
    )
    saved = forward(
        Names(
            big=big_tokens.reshape(128, WIDTH),
            small=small_tokens.reshape(128, WIDTH),
            table=action_table,
            inner_bias=ffn_in_bias,
        ),
        scalars,
        vectors,
        weights,
    )
    big_grad, small_grad, sums, *matrices = backward(
        Names(big_cot=big_cotangent.reshape(128, WIDTH), small_cot=small_cotangent.reshape(128, WIDTH)),
        Names(big_actions=big_actions, small_actions=small_actions, live=small_live),
        (norm1_gain, norm2_gain, norm3_gain),
        (saved.activated_t, saved.normed3_t, saved.context2_t, saved.normed2_t, saved.context1_t, saved.normed1_t),
        Names(
            normal1=saved.normal1,
            normal2=saved.normal2,
            normal3=saved.normal3,
            scale1=saved.scale1,
            scale2=saved.scale2,
            scale3=saved.scale3,
            spatial=saved.spatial,
            temporal=saved.temporal,
            slope=saved.slope,
        ),
        weights,
    )
    matrices = [one.reshape(-1, one.shape[-1]) for one in matrices]
    matrices, passed, small = widen(matrices, (saved.big_out, saved.small_out, big_grad, small_grad), sums)
    g_fout, g_fin, g_tout, g_tqkv, g_sout, g_sqkv = matrices
    table, gain1, shift1, bias_s, gain2, shift2, bias_t, gain3, shift3, bias_in, bias_out = small
    return (
        passed[0].reshape(1, 128, WIDTH),
        passed[1].reshape(4, 32, WIDTH),
        passed[2].reshape(1, 128, WIDTH),
        passed[3].reshape(4, 32, WIDTH),
        table,
        gain1,
        shift1,
        g_sqkv,
        g_sout,
        bias_s,
        gain2,
        shift2,
        g_tqkv,
        g_tout,
        bias_t,
        gain3,
        shift3,
        g_fin,
        bias_in,
        g_fout,
        bias_out,
    )


def solution(mesh):
    spread, by_col = P("col", "ta", None), P("col", None)
    return jax.shard_map(
        body,
        mesh=mesh,
        in_specs=(spread, spread, by_col, by_col, by_col, by_col, P("col")) + (P(),) * 17 + (spread, spread),
        out_specs=(spread,) * 4
        + (P(),) * 3
        + (by_col, by_col, P(), P(), P(), by_col, by_col, P(), P(), P(), by_col, P(), by_col, P()),
        check_vma=False,
    )
```

```python
import functools
from types import SimpleNamespace as Names

import jax
import jax.numpy as jnp
from jax import lax
from jax.experimental import pallas as pl
from jax.experimental.pallas import tpu as pltpu
from jax.sharding import PartitionSpec as P

HEAD_DIM = 64
EPSILON = 1e-05
MASKED_SCORE = -1e30
MESH = pl.DeviceIdType.MESH
ANY = pl.BlockSpec(memory_space=pl.ANY)
VMEM = pl.BlockSpec(memory_space=pltpu.VMEM)
SMEM = pl.BlockSpec(memory_space=pltpu.SMEM)
LANES = 128
F32, BF16 = jnp.float32, jnp.bfloat16
ROWS, WIDTH, HIDDEN = 256, 1024, 4096
PAIRS = WIDTH // LANES
HIDE = 512

SP_KEY, SP_VALUE, SP_QUERY, SP_ROWS = 1024, 1536, 2048, 2304
TP_KEY, TP_VALUE, TP_QUERY, TP_ROWS = 512, 768, 1024, 1280

ORDERS = (("x", "y", "z"), ("y", "z", "x"), ("z", "x", "y"))
MATRICES = (
    (HIDDEN, WIDTH, (1, 1, 2)),
    (WIDTH, HIDDEN, (4, 6, 6)),
    (WIDTH, WIDTH, (1, 1, 2)),
    (WIDTH, 3 * WIDTH, (4, 4, 4)),
    (WIDTH, WIDTH, (1, 1, 2)),
    (WIDTH, 3 * WIDTH, (4, 4, 4)),
)
ALL, XY, Z = (0, 1, 2), (0, 1), (2,)
SEND_UNITS = (0, 16, 12, 0, 28, 16)


class Place:
    def __init__(self):
        ta, col = lax.axis_index("ta"), lax.axis_index("col")
        self.ta, self.col = ta, col
        self.y_hi, self.x, self.core = ta // 8, (ta // 2) % 4, ta % 2
        self.y_lo, self.z = col // 4, col % 4
        self.y = self.y_hi * 2 + self.y_lo
        self.partner = self.device(core=1 - self.core)

    def device(self, y_hi=None, x=None, core=None, y_lo=None, z=None):
        y_hi = self.y_hi if y_hi is None else y_hi
        x = self.x if x is None else x
        core = self.core if core is None else core
        y_lo = self.y_lo if y_lo is None else y_lo
        z = self.z if z is None else z
        return (y_hi * 8 + x * 2 + core, y_lo * 4 + z)

    def along(self, axis, step):
        if axis == "x":
            at = (self.x + step) % 4
            return self.device(x=at), at
        if axis == "z":
            at = (self.z + step) % 4
            return self.device(z=at), at
        at = (self.y + step) % 4
        return self.device(y_hi=at // 2, y_lo=at % 2), (at % 2) * 2 + at // 2

    def fellow(self, step):
        ta = (self.ta + step) % 16
        return (ta, self.col), ta


def greet(place, whole):
    barrier = pltpu.get_barrier_semaphore()

    def one(step, carry):
        pl.semaphore_signal(barrier, inc=1, device_id=place.fellow(step)[0], device_id_type=MESH)
        return carry

    lax.fori_loop(1, 16, one, 0)
    count = 15
    if whole:
        for axis, step in (("y", 1), ("y", 3), ("z", 1), ("z", 2), ("z", 3)):
            pl.semaphore_signal(barrier, inc=1, device_id=place.along(axis, step)[0], device_id_type=MESH)
            count += 1
    pl.semaphore_wait(barrier, count)


def remote(source, target, send, recv, device):
    return pltpu.make_async_remote_copy(source, target, send, recv, device_id=device, device_id_type=MESH)


def dot(left, right):
    return jnp.dot(left, right, preferred_element_type=F32)


def dot_nt(left, right):
    return lax.dot_general(left, right, (((1,), (1,)), ((), ())), preferred_element_type=F32)


def dot_tn(left, right):
    return lax.dot_general(left, right, (((0,), (0,)), ((), ())), preferred_element_type=F32)


def rows16(step):
    return pl.ds(pl.multiple_of(step * 16, 16), 16)


def lanes(step, width):
    return pl.ds(pl.multiple_of(step * width, width), width)


def interleave(big, small):
    width = big.shape[-1]
    pair = [one.reshape(-1, 1, 8, width) for one in (big, small)]
    return jnp.concatenate(pair, axis=1).reshape(-1, width)


def family(rows, which):
    width = rows.shape[-1]
    return rows.reshape(-1, 2, 8, width)[:, which].reshape(-1, width)


def half_masks(rows):
    lane = lax.broadcasted_iota(jnp.int32, (rows, LANES), 1)
    return lane < HEAD_DIM


def by_head(value, low):
    zero = jnp.zeros_like(value)
    return jnp.where(low, value, zero), jnp.where(low, zero, value)


def join_heads(value, low):
    return jnp.where(low, value[:128], value[128:])


def statistics(rows):
    mean = jnp.mean(rows, axis=-1, keepdims=True)
    centered = rows - mean
    variance = jnp.mean(centered * centered, axis=-1, keepdims=True)
    scale = lax.rsqrt(variance + EPSILON)
    return centered * scale, scale


def norm_forward(source, gain, shift, target, normals, scales, after=None):
    def one(step, carry):
        rows = rows16(step)
        normal, scale = statistics(source[rows])
        target[rows] = (normal * gain + shift).astype(BF16)
        normals[rows] = normal
        scales[rows] = jnp.broadcast_to(scale, (16, LANES))
        if after is not None:
            after(step)
        return carry

    lax.fori_loop(0, 16, one, 0, unroll=4)


def transpose_into(source, target):
    def one(step, carry):
        target[step] = source[:, lanes(step, LANES)].T
        return carry

    lax.fori_loop(0, PAIRS, one, 0, unroll=4)


class Swap:
    def __init__(self, place, send, recv, sems, index, to_positions, columns=slice(0, WIDTH)):
        self.place, self.send, self.recv, self.sems, self.index = place, send, recv, sems, index
        self.to_positions, self.columns = to_positions, columns

    def rows(self, ta):
        frames = rows16(ta)
        positions = rows16((ta % 2) * 8 + ta // 2)
        return (frames, positions) if self.to_positions else (positions, frames)

    def copy(self, step):
        device, ta = self.place.fellow(step)
        source = self.send.at[self.rows(ta)[0], self.columns]
        target = self.recv.at[self.rows(self.place.ta)[1], self.columns]
        return remote(source, target, self.sems.at[self.index, 0, step], self.sems.at[self.index, 1, step], device)

    def own(self):
        rows = self.rows(self.place.ta)
        source, target = self.send.at[rows[0], self.columns], self.recv.at[rows[1], self.columns]
        return pltpu.make_async_copy(source, target, self.sems.at[self.index, 0, 0])

    def start_block(self, ta):
        step = (ta - self.place.ta + 16) % 16

        @pl.when(step > 0)
        def _():
            self.copy(step).start()

        @pl.when(step == 0)
        def _():
            self.own().start()

    def start(self):
        def one(step, carry):
            self.copy(step).start()
            return carry

        lax.fori_loop(1, 16, one, 0)
        self.own().start()

    def wait(self):
        def one(step, carry):
            self.copy(step).wait_recv()
            return carry

        self.own().wait()
        lax.fori_loop(1, 16, one, 0)

    def sent(self):
        def one(step, carry):
            self.copy(step).wait_send()
            return carry

        lax.fori_loop(1, 16, one, 0)


HALVES = (slice(0, WIDTH // 2), slice(WIDTH // 2, WIDTH))


FORWARD_OUTS = dict(
    big_out=((128, WIDTH), BF16),
    small_out=((128, WIDTH), BF16),
    normal1=((ROWS, WIDTH), F32),
    normal2=((ROWS, WIDTH), F32),
    normal3=((ROWS, WIDTH), F32),
    scale1=((ROWS, LANES), F32),
    scale2=((ROWS, LANES), F32),
    scale3=((ROWS, LANES), F32),
    spatial=((PAIRS, SP_ROWS, LANES), BF16),
    temporal=((PAIRS, TP_ROWS, LANES), BF16),
    slope=((PAIRS, ROWS, HIDE), BF16),
)
FORWARD_LEFTS = dict(
    activated_t=((PAIRS, HIDE, ROWS), BF16),
    normed3_t=((PAIRS, LANES, ROWS), BF16),
    context2_t=((PAIRS, LANES, ROWS), BF16),
    normed2_t=((PAIRS, LANES, ROWS), BF16),
    context1_t=((PAIRS, LANES, ROWS), BF16),
    normed1_t=((PAIRS, LANES, ROWS), BF16),
)
FORWARD_WORK = dict(
    w_sqkv=((WIDTH, 3 * WIDTH), BF16),
    w_sout=((WIDTH, WIDTH), BF16),
    w_tqkv=((WIDTH, 3 * WIDTH), BF16),
    w_tout=((WIDTH, WIDTH), BF16),
    w_fin=((WIDTH, HIDDEN), BF16),
    w_fout=((HIDDEN, WIDTH), BF16),
    normed=((ROWS, WIDTH), BF16),
    context=((ROWS, WIDTH), BF16),
    arranged=((ROWS, WIDTH), BF16),
    context_send=((ROWS, WIDTH), BF16),
    context_back=((ROWS, WIDTH), BF16),
    normed3=((ROWS, WIDTH), BF16),
    total=((ROWS, WIDTH), F32),
    hidden=((2, ROWS, HIDE), F32),
    params=((16, WIDTH), F32),
    inner_bias=((PAIRS, HIDE), F32),
    table=((8, WIDTH), F32),
)


def named(keys, refs):
    return Names(**{key: refs.pop(0) for key in keys})


def forward_kernel(in_keys, vector_count, weight_keys, *refs):
    refs = list(refs)
    ins = named(in_keys, refs)
    vectors = [refs.pop(0) for _ in range(vector_count)]
    weights = named(weight_keys, refs)
    kept = FORWARD_OUTS | FORWARD_LEFTS
    outs, keep, work = named(kept, refs), named(kept, refs), named(FORWARD_WORK, refs)
    w_sems, out_sems, swap_sems, far_sems, pair_sems, feed_sems = refs
    place = Place()
    params = work.params

    def param(row):
        return params[row : row + 1]

    loads = Names()
    for i, key in enumerate(weight_keys):
        setattr(loads, key, pltpu.make_async_copy(getattr(weights, key), getattr(work, key), w_sems.at[i]))
    loads.w_sqkv.start()
    for row, vector in enumerate(vectors):
        params[row : row + 1] = vector[...].astype(F32).reshape(1, WIDTH)
    for row in range(PAIRS):
        at = slice(row * HIDE, row * HIDE + HIDE)
        work.inner_bias[row : row + 1] = ins.inner_bias[at].astype(F32).reshape(1, HIDE)
    work.table[...] = ins.table[...].astype(F32)
    frame = place.ta // 2
    copies = []

    def save(source, target):
        copy = pltpu.make_async_copy(source, target, out_sems.at[len(copies)])
        copy.start()
        copies.append(copy)

    shared = []

    def share(source, target):
        save(source, target.at[:, :, :ROWS])
        i = len(shared)
        copy = remote(source, target.at[:, :, ROWS:], pair_sems.at[0, i], pair_sems.at[1, i], place.partner)
        copy.start()
        shared.append(copy)

    resid0, resid1, resid2 = keep.normal2, keep.normal3, work.total
    big_row = work.table[pl.ds(ins.big_actions[0, frame], 1)]

    def start_rows(step, carry):
        near = pl.ds(pl.multiple_of(step * 16, 16), 16)
        big = ins.big[near].astype(F32) + big_row
        small = ins.small[near].astype(F32) + work.table[pl.ds(ins.small_actions[step // 2, frame], 1)]
        rows = pl.ds(pl.multiple_of(step * 32, 32), 32)
        merged = interleave(big, small)
        resid0[rows] = merged
        normal, scale = statistics(merged)
        work.normed[rows] = (normal * param(0) + param(1)).astype(BF16)
        keep.normal1[rows] = normal
        keep.scale1[rows] = jnp.broadcast_to(scale, (32, LANES))
        return carry

    lax.fori_loop(0, 8, start_rows, 0)
    save(keep.normal1, outs.normal1)
    save(keep.scale1, outs.scale1)
    greet(place, False)

    spatial = keep.spatial
    loads.w_sqkv.wait()
    for key in weight_keys[1:]:
        getattr(loads, key).start()

    def spatial_project(column, base, per_family, scale):
        def one(step, carry):
            at = column + step
            value = dot(work.normed[...], work.w_sqkv[:, lanes(at, 256)]) * scale
            for which in range(2):
                one_family = family(value, which).astype(BF16)
                rows = pl.ds(base + which * per_family, 128)
                spatial[step * 2, rows] = one_family[:, :LANES]
                spatial[step * 2 + 1, rows] = one_family[:, LANES:]
            return carry

        lax.fori_loop(0, 4, one, 0, unroll=2)

    spatial_project(4, SP_KEY, 256, 1.0)
    spatial_project(8, SP_VALUE, 256, 1.0)
    far = []
    for i, base in enumerate((SP_KEY, SP_KEY + 256, SP_VALUE, SP_VALUE + 256)):
        far.append(
            remote(
                spatial.at[:, pl.ds(base, 128)], spatial.at[:, pl.ds(base + 128, 128)],
                far_sems.at[0, i], far_sems.at[1, i], place.partner,
            )
        )
    for copy in far:
        copy.start()
    spatial_project(0, SP_QUERY, 128, 0.125)
    transpose_into(work.normed, keep.normed1_t)
    share(keep.normed1_t, outs.normed1_t)
    for copy in far:
        copy.wait()

    low_q = half_masks(128)
    key_slot = (lax.broadcasted_iota(jnp.int32, (256, 256), 0) % 128) // 32
    query_slot = (lax.broadcasted_iota(jnp.int32, (256, 256), 1) % 128) // 32
    same_slot = key_slot == query_slot

    def softmax(scores):
        weights_ = jnp.exp(scores - jnp.max(scores, axis=0, keepdims=True))
        return (weights_ * (1.0 / jnp.sum(weights_, axis=0, keepdims=True))).astype(BF16)

    def attend(keys, values, queries, visible):
        scores = dot_nt(keys, jnp.concatenate(by_head(queries, low_q), axis=0))
        if visible is not None:
            scores = jnp.where(visible, scores, MASKED_SCORE)
        probs = softmax(scores)
        return (probs[:, :LANES], probs[:, LANES:]), join_heads(dot_tn(probs, values), low_q)

    def spatial_pairs(step, carry):
        loaded = []
        for pair in (step * 2, step * 2 + 1):
            for which in range(2):
                keys = spatial[pair, SP_KEY + which * 256 : SP_KEY + which * 256 + 256]
                values = spatial[pair, SP_VALUE + which * 256 : SP_VALUE + which * 256 + 256]
                queries = spatial[pair, SP_QUERY + which * 128 : SP_QUERY + which * 128 + 128]
                loaded.append((keys, values, queries, same_slot if which else None))
        done = [attend(*one) for one in loaded]
        for i in range(2):
            pair = step * 2 + i
            for which in range(2):
                for head in range(2):
                    at = (which * 2 + head) * 256
                    spatial[pair, at : at + 256] = done[i * 2 + which][0][head]
            value = interleave(done[i * 2][1], done[i * 2 + 1][1])
            work.context[:, lanes(pair, LANES)] = value.astype(BF16)
        return carry

    lax.fori_loop(0, PAIRS // 2, spatial_pairs, 0)
    save(keep.spatial, outs.spatial)

    def project_into(source, weight, bias, before, target):
        def one(step, carry):
            at = lanes(step, 256)
            target[:, at] = dot(source[...], weight[:, at]) + params[bias : bias + 1, at] + before[:, at]
            return carry

        lax.fori_loop(0, WIDTH // 256, one, 0, unroll=2)

    loads.w_sout.wait()
    project_into(work.context, work.w_sout, 2, resid0, resid1)
    there = Swap(place, work.normed, work.arranged, swap_sems, 0, True)
    norm_forward(resid1, param(3), param(4), work.normed, keep.normal2, keep.scale2, there.start_block)
    save(keep.normal2, outs.normal2)
    save(keep.scale2, outs.scale2)
    transpose_into(work.context, keep.context1_t)
    share(keep.context1_t, outs.context1_t)
    loads.w_tqkv.wait()
    there.wait()

    temporal = keep.temporal

    def temporal_project(column, base, scale):
        def one(step, carry):
            value = dot(work.arranged[...], work.w_tqkv[:, lanes(column + step, 256)]) * scale
            value = value.astype(BF16)
            temporal[step * 2, base : base + ROWS] = value[:, :LANES]
            temporal[step * 2 + 1, base : base + ROWS] = value[:, LANES:]
            return carry

        lax.fori_loop(0, 4, one, 0, unroll=2)

    temporal_project(0, TP_QUERY, 0.125)
    temporal_project(4, TP_KEY, 1.0)
    temporal_project(8, TP_VALUE, 1.0)
    key_row = lax.broadcasted_iota(jnp.int32, (128, 256), 0)
    query_row = lax.broadcasted_iota(jnp.int32, (128, 256), 1) % 128
    key_rank, query_rank = jnp.zeros_like(key_row), jnp.zeros_like(query_row)
    for at in range(8):
        big_rank, small_rank = ins.big_order[0, at], ins.small_order[place.ta // 4, at]
        key_rank = jnp.where(key_row // 16 == at, jnp.where(key_row % 16 < 8, big_rank, small_rank), key_rank)
        query_rank = jnp.where(query_row // 16 == at, jnp.where(query_row % 16 < 8, big_rank, small_rank), query_rank)
    seen = (key_row % 16 == query_row % 16) & (key_rank <= query_rank)

    def temporal_pairs(step, carry):
        loaded = []
        for pair in (step * 2, step * 2 + 1):
            for half in range(2):
                keys = temporal[pair, TP_KEY + half * 128 : TP_KEY + half * 128 + 128]
                values = temporal[pair, TP_VALUE + half * 128 : TP_VALUE + half * 128 + 128]
                queries = temporal[pair, TP_QUERY + half * 128 : TP_QUERY + half * 128 + 128]
                loaded.append((keys, values, queries, seen))
        done = [attend(*one) for one in loaded]
        for i in range(2):
            pair = step * 2 + i
            for half in range(2):
                for head in range(2):
                    at = (half * 2 + head) * 128
                    temporal[pair, at : at + 128] = done[i * 2 + half][0][head]
                at = slice(half * 128, half * 128 + 128)
                work.context_send[at, lanes(pair, LANES)] = done[i * 2 + half][1].astype(BF16)
        return carry

    back = [Swap(place, work.context_send, work.context_back, swap_sems, 1 + i, False, HALVES[i]) for i in range(2)]
    lax.fori_loop(0, PAIRS // 4, temporal_pairs, 0)
    back[0].start()
    lax.fori_loop(PAIRS // 4, PAIRS // 2, temporal_pairs, 0)
    back[1].start()
    save(keep.temporal, outs.temporal)
    transpose_into(work.arranged, keep.normed2_t)
    share(keep.normed2_t, outs.normed2_t)
    loads.w_tout.wait()
    for i in range(2):
        back[i].wait()

        def add_half(step, carry, i=i):
            at = lanes(step, 256)
            value = dot(work.context_back[:, HALVES[i]], work.w_tout[HALVES[i], at])
            if i == 0:
                resid2[:, at] = value + params[5:6, at] + resid1[:, at]
            else:
                resid2[:, at] += value
            return carry

        lax.fori_loop(0, WIDTH // 256, add_half, 0, unroll=2)
    norm_forward(resid2, param(6), param(7), work.normed3, keep.normal3, keep.scale3)
    save(keep.normal3, outs.normal3)
    save(keep.scale3, outs.scale3)
    transpose_into(work.context_back, keep.context2_t)
    share(keep.context2_t, outs.context2_t)
    transpose_into(work.normed3, keep.normed3_t)
    share(keep.normed3_t, outs.normed3_t)

    total, hidden, slope = work.total, work.hidden, keep.slope
    total[...] += param(8)
    loads.w_fin.wait()
    loads.w_fout.wait()
    root = 0.7978845608028654

    def inner(step, slot):
        hidden[slot] = dot(work.normed3[...], work.w_fin[:, lanes(step, HIDE)])

    def feed_copies(step):
        here, there_ = keep.activated_t.at[step], outs.activated_t.at[step]
        return (
            pltpu.make_async_copy(here, there_.at[:, :ROWS], feed_sems.at[0, step]),
            remote(here, there_.at[:, ROWS:], feed_sems.at[1, step], feed_sems.at[2, step], place.partner),
            pltpu.make_async_copy(slope.at[step], outs.slope.at[step], feed_sems.at[3, step]),
        )

    def feed(step, slot, ahead):
        value = hidden[slot] + work.inner_bias[pl.ds(step, 1)]
        if ahead:
            inner(step + 1, 1 - slot)
        square = value * value
        bent = jnp.tanh(root * value * (1.0 + 0.044715 * square))
        half = 0.5 * (1.0 + bent)
        active = (value * half).astype(BF16)
        rise = half + 0.5 * value * (1.0 - bent * bent) * (root * (1.0 + 0.134145 * square))
        slope[step] = rise.astype(BF16)
        for block in range(HIDE // LANES):
            at = slice(block * LANES, block * LANES + LANES)
            keep.activated_t[step, at] = active[:, at].T
        down = work.w_fout.at[pl.ds(pl.multiple_of(step * HIDE, HIDE), HIDE)]
        for column in range(WIDTH // 256):
            at = slice(column * 256, column * 256 + 256)
            total[:, at] += dot(active, down[:, at])
        for copy in feed_copies(step):
            copy.start()

    def feed_two(step, carry):
        feed(step * 2, 0, True)
        feed(step * 2 + 1, 1, True)
        return carry

    for one in back:
        one.sent()
    inner(0, 0)
    lax.fori_loop(0, PAIRS // 2 - 1, feed_two, 0)
    feed(PAIRS - 2, 0, True)
    feed(PAIRS - 1, 1, False)

    def finish_rows(step, carry):
        value = total[pl.ds(pl.multiple_of(step * 32, 32), 32)]
        near = pl.ds(pl.multiple_of(step * 16, 16), 16)
        keep.big_out[near] = family(value, 0).astype(BF16)
        keep.small_out[near] = (family(value, 1) * ins.live[step // 2].astype(F32)).astype(BF16)
        return carry

    lax.fori_loop(0, 8, finish_rows, 0)
    save(keep.big_out, outs.big_out)
    save(keep.small_out, outs.small_out)
    there.sent()
    for copy in copies + shared + [one for step in range(PAIRS) for one in feed_copies(step)]:
        copy.wait()


def forward(ins, scalars, vectors, weights):
    sem = pltpu.SemaphoreType.DMA
    lefts, work = list(FORWARD_LEFTS.values()), list(FORWARD_WORK.values())
    kept = list(FORWARD_OUTS.values()) + lefts
    results = list(FORWARD_OUTS.values()) + [((rows, depth, 2 * columns), dtype) for (rows, depth, columns), dtype in lefts]
    in_keys, weight_keys = tuple(vars(ins)) + tuple(vars(scalars)), tuple(vars(weights))
    results = pl.pallas_call(
        functools.partial(forward_kernel, in_keys, len(vectors), weight_keys),
        out_shape=[jax.ShapeDtypeStruct(shape, dtype) for shape, dtype in results],
        in_specs=[VMEM] * len(vars(ins)) + [SMEM] * len(vars(scalars)) + [VMEM] * len(vectors) + [ANY] * len(weight_keys),
        out_specs=[ANY] * len(kept),
        scratch_shapes=[pltpu.VMEM(shape, dtype) for shape, dtype in kept + work]
        + [sem((len(weight_keys),)), sem((len(kept),)), sem((3, 2, 16)), sem((2, 4)), sem((2, 6)), sem((4, PAIRS))],
        compiler_params=pltpu.CompilerParams(
            collective_id=1, has_side_effects=True, vmem_limit_bytes=62 * 2**20
        ),
        cost_estimate=pl.CostEstimate(flops=9 * 10**9, bytes_accessed=60 * 2**20, transcendentals=4 * 10**6),
        name="layer_forward",
    )(*vars(ins).values(), *vars(scalars).values(), *vectors, *vars(weights).values())
    return named(FORWARD_OUTS | FORWARD_LEFTS, list(results))


class Reduction:
    def __init__(self, place, index, refs, sems):
        self.place, self.index, self.refs, self.sems = place, index, refs, sems
        k, n, shares = MATRICES[index]
        self.half = n // 2
        self.depth = k // 64
        self.groups = self.depth // 16
        self.bounds, start = [], 0
        for share in shares:
            self.bounds.append((start, start + share))
            start += share
        self.units = start * self.groups
        self.first_unit = sum(m[1] // 2 // LANES * (m[0] // 1024) for m in MATRICES[:index])
        self.send_unit = SEND_UNITS[index]
        self.local_done = False
        self.straight = index >= 4
        self.whole_parts = XY if index == 0 else ()

    def left_local(self):
        return pltpu.make_async_copy(self.refs.at_in, self.refs.at, self.sems.local.at[self.index, 0])

    def right_local(self):
        r, s, i, core = self.refs, self.sems, self.index, self.place.core
        source = r.source.at[:, lanes(core, self.half)]
        return pltpu.make_async_copy(source, r.g.at[:ROWS], s.local.at[i, 1])

    def right_far(self):
        r, s, i, core = self.refs, self.sems, self.index, self.place.core
        source = r.source.at[:, lanes(1 - core, self.half)]
        return remote(source, r.g.at[ROWS:], s.ex_send.at[i, 1], s.ex_recv.at[i, 1], self.place.partner)

    def lefts(self):
        self.left_local().start()

    def rights(self):
        self.right_far().start()
        self.right_local().start()

    def right_local_done(self):
        if not self.local_done:
            self.right_local().wait()
            self.local_done = True

    def rights_sent(self):
        self.right_local_done()
        self.right_far().wait_send()

    def loaded(self):
        self.right_far().wait_recv()
        self.left_local().wait()
        self.right_local_done()

    def span(self, part):
        low, high = self.bounds[part]
        return low * self.groups, high * self.groups

    def copy(self, part, stage, step):
        r, s, i = self.refs, self.sems, self.index
        low, high = self.span(part)
        here = slice(self.first_unit + low, self.first_unit + high)
        device, slot = self.place.along(ORDERS[part][stage], step)
        if stage == 1:
            source = r.r1.at[0, here, slot]
            target = r.r2.at[step - 1, here]
        else:
            source = r.r2.at[0, here, slot]
            target = r.r3.at[step - 1, here]
        return remote(
            source, target, s.send.at[i, part, stage, step - 1], s.recv.at[i, part, stage, step - 1], device
        )

    def left_block(self, part, slot, group):
        at = self.refs.at
        rows = slice(group * 16, group * 16 + 16)
        if part == 0:
            blocks = [at[y // 2, :, y % 2, slot, rows] for y in range(4)]
        elif part == 1:
            blocks = [at[slot // 2, :, slot % 2, :, rows]]
        else:
            blocks = [at[:, slot, :, x, rows] for x in range(4)]
        blocks = [block.reshape(-1, block.shape[-1]) for block in blocks]
        return blocks[0] if len(blocks) == 1 else jnp.concatenate(blocks, axis=0)

    def products(self, part, slot, emit):
        low, high = self.bounds[part]
        for group in range(self.groups):
            left = self.left_block(part, slot, group)
            for tile in range(low, high, 2):
                width = min(2, high - tile)
                value = dot(left, self.refs.g[:, tile * LANES : (tile + width) * LANES])
                for i in range(width):
                    one = value[:, i * LANES : (i + 1) * LANES].reshape(4, 4, 16, LANES)
                    emit((tile + i) * self.groups + group, one)

    def relay(self, part, way):
        r, s, i = self.refs, self.sems, self.index
        low, high = self.span(part)
        here = slice(self.first_unit + low, self.first_unit + high)
        half = slice(way * 2, way * 2 + 2)
        device = self.place.along(ORDERS[part][0], 3 if way else 1)[0]
        source = r.s1.at[0, self.send_unit + low : self.send_unit + high, half]
        target = r.r1.at[2, here, half]
        return remote(source, target, s.send.at[i, part, 0, way], s.recv.at[i, part, 0, way], device)

    def direct(self, part, way):
        r, s, i = self.refs, self.sems, self.index
        low, high = self.span(part)
        here = slice(self.first_unit + low, self.first_unit + high)
        device = self.place.along(ORDERS[part][0], 3 if way else 1)[0]
        source = r.s1.at[1 + way, self.send_unit + low : self.send_unit + high]
        target = r.r1.at[way, here]
        return remote(source, target, s.send.at[i, part, 0, 2 + way], s.recv.at[i, part, 0, 2 + way], device)

    def whole(self, part, step):
        r, s, i = self.refs, self.sems, self.index
        low, high = self.span(part)
        here = slice(self.first_unit + low, self.first_unit + high)
        at = (1, 0, 2)[step - 1]
        source = r.s1.at[at, self.send_unit + low : self.send_unit + high]
        target = r.r1.at[step - 1, here]
        device = self.place.along(ORDERS[part][0], step)[0]
        return remote(source, target, s.send.at[i, part, 0, step], s.recv.at[i, part, 0, step], device)

    def first(self, parts=ALL):
        r = self.refs
        for part in parts:
            if part in self.whole_parts:
                for step in (1, 3, 2):
                    slot = self.place.along(ORDERS[part][0], step)[1]

                    def keep(unit, value, step=step):
                        r.s1[(1, 0, 2)[step - 1], self.send_unit + unit] = value.astype(BF16)

                    self.products(part, slot, keep)
                    self.whole(part, step).start()
                continue
            slot = self.place.along(ORDERS[part][0], 2)[1]

            def emit(unit, value):
                r.s1[0, self.send_unit + unit] = value.astype(BF16)

            self.products(part, slot, emit)
            for way in range(2):
                self.relay(part, way).start()

    def pass_on(self, parts=ALL):
        r = self.refs
        for part in parts:
            if part in self.whole_parts:
                continue
            for way in range(2):
                self.relay(part, way).wait_recv()
                slot = self.place.along(ORDERS[part][0], 3 if way else 1)[1]

                def emit(unit, value, way=way):
                    at = self.first_unit + unit
                    for half in range(2):
                        some = slice(half * 2, half * 2 + 2)
                        one = value[some]
                        if half == way:
                            one = one + r.r1[2, at, some].astype(F32)
                        r.s1[1 + way, self.send_unit + unit, some] = one.astype(BF16)

                self.products(part, slot, emit)
                self.direct(part, way).start()

    def relay_sent(self):
        for part in range(3):
            if part in self.whole_parts:
                self.whole(part, 2).wait_send()
                continue
            for way in range(2):
                self.relay(part, way).wait_send()

    def direct_sent(self):
        for part in range(3):
            for way in range(2):
                if part in self.whole_parts:
                    self.whole(part, 3 if way else 1).wait_send()
                else:
                    self.direct(part, way).wait_send()

    def second(self, parts=ALL):
        r = self.refs
        for part in parts:
            slot = self.place.along(ORDERS[part][0], 0)[1]
            terms = 2
            if part in self.whole_parts:
                terms = 3
                for step in (1, 2, 3):
                    self.whole(part, step).wait_recv()
            else:
                for way in range(2):
                    self.direct(part, way).wait_recv()

            def emit(unit, value, terms=terms):
                at = self.first_unit + unit
                for i in range(terms):
                    value = value + r.r1[i, at].astype(F32)
                r.r1[0, at] = value.astype(BF16)

            self.products(part, slot, emit)
            for step in (1, 2, 3):
                self.copy(part, 1, step).start()

    def third(self, parts=ALL):
        r = self.refs
        for part in parts:
            slot = self.place.along(ORDERS[part][1], 0)[1]
            for step in (1, 2, 3):
                self.copy(part, 1, step).wait_recv()

            def one(unit, carry, slot=slot):
                value = r.r1[0, unit, slot].astype(F32)
                for i in range(3):
                    value = value + r.r2[i, unit].astype(F32)
                r.r2[0, unit] = value.astype(BF16)
                return carry

            low, high = self.span(part)
            lax.fori_loop(self.first_unit + low, self.first_unit + high, one, 0)
            for step in (1, 2, 3):
                self.copy(part, 2, step).start()

    def mine(self):
        return self.place.y_hi * 4 + self.place.x

    def gather_copy(self, y_hi, x, slot):
        r, s, i, place = self.refs, self.sems, self.index, self.place
        target = r.out.at[slot // 4, slot % 4, :, lanes(place.core, self.half)]
        return remote(
            r.piece.at[place.y_hi], target, s.ag_send.at[i, y_hi * 4 + x], s.ag_recv.at[i, slot],
            place.device(y_hi=y_hi, x=x),
        )

    def twin_copy(self):
        r, s, i, place = self.refs, self.sems, self.index, self.place
        block = r.piece.at[place.y_hi]
        return remote(block, block, s.ag_send.at[i, 0], s.ag_recv.at[i, 0], place.device(y_hi=1 - place.y_hi))

    def line_copy(self, step):
        r, s, i, place = self.refs, self.sems, self.index, self.place
        target = r.out.at[:, place.x, :, lanes(place.core, self.half)]
        device = place.device(x=(place.x + step) % 4)
        return remote(r.piece, target, s.ag_send.at[i, step], s.ag_recv.at[i, step], device)

    def own_copy(self):
        place, i, piece = self.place, self.index, self.refs.piece
        columns = lanes(place.core, self.half)
        if self.straight:
            target = self.refs.out.at[place.y_hi, place.x, :, columns]
            return pltpu.make_async_copy(piece.at[place.y_hi], target, self.sems.local.at[i, 2])
        return pltpu.make_async_copy(piece, self.refs.out.at[:, place.x, :, columns], self.sems.local.at[i, 2])

    def others(self):
        place = self.place
        for y_step in (0, 1):
            y_hi = (place.y_hi + y_step) % 2
            for x_step in range(4):
                if y_step or x_step:
                    yield y_hi, (place.x + x_step) % 4

    def fourth(self, parts=ALL):
        r = self.refs
        for part in parts:
            slot = self.place.along(ORDERS[part][2], 0)[1]
            for step in (1, 2, 3):
                self.copy(part, 2, step).wait_recv()
            low, high = self.span(part)
            for unit in range(low, high):
                at = self.first_unit + unit
                value = r.r2[0, at, slot].astype(F32)
                for i in range(3):
                    value = value + r.r3[i, at].astype(F32)
                tile, group = unit // self.groups, unit % self.groups
                rows, columns = slice(group * 16, group * 16 + 16), slice(tile * LANES, tile * LANES + LANES)
                r.piece[self.place.y_hi, rows, columns] = value.astype(BF16)
    def gather(self):
        if self.straight:
            self.own_copy().start()
            for y_hi, x in self.others():
                self.gather_copy(y_hi, x, self.mine()).start()
        else:
            self.twin_copy().start()

    def spread(self):
        if not self.straight:
            self.twin_copy().wait_recv()
            self.own_copy().start()
            for step in (1, 2, 3):
                self.line_copy(step).start()

    def cross_copy(self):
        r, s, i, core = self.refs, self.sems, self.index, self.place.core
        block = r.out.at[:, :, :, lanes(core, self.half)]
        return remote(block, block, s.cross.at[i, 0], s.cross.at[i, 1], self.place.partner)

    def fifth(self):
        self.own_copy().wait()
        if self.straight:
            for y_hi, x in self.others():
                self.gather_copy(y_hi, x, y_hi * 4 + x).wait_recv()
        else:
            for step in (1, 2, 3):
                self.line_copy(step).wait_recv()
        self.cross_copy().start()

    def finish(self):
        self.cross_copy().wait()
        if self.straight:
            for y_hi, x in self.others():
                self.gather_copy(y_hi, x, self.mine()).wait_send()
        else:
            self.twin_copy().wait_send()
            for step in (1, 2, 3):
                self.line_copy(step).wait_send()
        for part in range(3):
            for stage in (1, 2):
                for step in (1, 2, 3):
                    self.copy(part, stage, step).wait_send()


GAIN1, SHIFT1, SPATIAL_BIAS, GAIN2, SHIFT2, TEMPORAL_BIAS, GAIN3, SHIFT3, INNER, OUTER = 8, 9, 10, 11, 12, 13, 14, 15, 16, 20


class SmallSums:
    def __init__(self, place, refs, sems):
        self.place, self.refs, self.sems = place, refs, sems

    def share(self, core):
        return slice(None), lanes(core, WIDTH // 2)

    def cross(self):
        r, core = self.refs, self.place.core
        return remote(
            r.sums.at[self.share(1 - core)], r.sums_core, self.sems.at[0, 0, 0], self.sems.at[1, 0, 0],
            self.place.partner,
        )

    def along(self, stage, step):
        device = self.place.along("xyz"[stage], step)[0]
        return remote(
            self.refs.sums_total.at[stage], self.refs.sums_recv.at[stage, step - 1],
            self.sems.at[0, stage + 1, step - 1], self.sems.at[1, stage + 1, step - 1], device,
        )

    def final(self):
        block = self.refs.sums_final.at[self.share(self.place.core)]
        return remote(block, block, self.sems.at[0, 4, 0], self.sems.at[1, 4, 0], self.place.partner)

    def begin(self):
        self.cross().start()

    def step0(self):
        r = self.refs
        self.cross().wait()
        r.sums_total[0] = r.sums[self.share(self.place.core)] + r.sums_core[...]
        for step in (1, 2, 3):
            self.along(0, step).start()

    def advance(self, stage):
        r = self.refs
        value = r.sums_total[stage]
        for step in (1, 2, 3):
            self.along(stage, step).wait_recv()
            value = value + r.sums_recv[stage, step - 1]
        if stage < 2:
            r.sums_total[stage + 1] = value
            for step in (1, 2, 3):
                self.along(stage + 1, step).start()
        else:
            r.sums_final[self.share(self.place.core)] = value
            self.final().start()

    def finish(self, out, sem):
        self.final().wait()
        copy = pltpu.make_async_copy(self.refs.sums_final, out, sem)
        copy.start()
        for stage in range(3):
            for step in (1, 2, 3):
                self.along(stage, step).wait_send()
        copy.wait()


BACK_OUTS = dict(
    big_grad=((128, WIDTH), F32),
    small_grad=((128, WIDTH), F32),
    small_sums=((24, WIDTH), F32),
)
SLOTS = 3
BACK_WORK = dict(
    s1=((3, 32, 4, 4, 16, LANES), BF16),
    r1=((3, 64, 4, 4, 16, LANES), BF16),
    r2=((3, 64, 4, 16, LANES), BF16),
    r3=((3, 64, 16, LANES), BF16),
    tall=((SLOTS, HIDE, WIDTH), BF16),
    broad=((SLOTS, WIDTH, HIDE), BF16),
    slope_in=((SLOTS, ROWS, HIDE), BF16),
    record=((SLOTS, SP_ROWS, LANES), BF16),
    resid=((ROWS, WIDTH), F32),
    grad=((ROWS, WIDTH), F32),
    total=((ROWS, WIDTH), F32),
    low3=((ROWS, WIDTH), BF16),
    low2=((ROWS, WIDTH), BF16),
    low1=((ROWS, WIDTH), BF16),
    hidden_low=((ROWS, HIDDEN), BF16),
    packed=((ROWS, 3 * WIDTH), BF16),
    swap_send=((ROWS, WIDTH), BF16),
    context_back=((ROWS, WIDTH), BF16),
    normed_back=((ROWS, WIDTH), BF16),
    context_grad=((2, 128, WIDTH), BF16),
    far_send=((ROWS, 2 * WIDTH), BF16),
    far_recv=((ROWS, 2 * WIDTH), BF16),
    inner_sums=((PAIRS, HIDE), F32),
    sums=((24, WIDTH), F32),
    sums_core=((24, WIDTH // 2), F32),
    sums_total=((3, 24, WIDTH // 2), F32),
    sums_recv=((3, 3, 24, WIDTH // 2), F32),
    sums_final=((24, WIDTH), F32),
    frame_sums=((8, WIDTH), F32),
    scale=((ROWS, LANES), F32),
    gains=((8, WIDTH), F32),
)


BACK_SEMS = dict(
    local=(6, 3),
    ex_send=(6, 2),
    ex_recv=(6, 2),
    send=(6, 3, 3, 4),
    recv=(6, 3, 3, 4),
    ag_send=(6, 8),
    ag_recv=(6, 8),
    cross=(6, 2),
    ring=(4, SLOTS),
    io=(5,),
    swap=(3, 2, 16),
    far=(2,),
    sums=(2, 5, 3),
)


def backward_kernel(in_keys, saved_keys, weight_keys, *refs):
    refs = list(refs)
    count = len(MATRICES)
    ins = named(in_keys, refs)
    gains = [refs.pop(0) for _ in range(3)]
    lefts = [refs.pop(0) for _ in range(count)]
    saved, weights, outs = named(saved_keys, refs), named(weight_keys, refs), named(BACK_OUTS, refs)
    matrix_outs = [refs.pop(0) for _ in range(count)]
    work = named(BACK_WORK, refs)
    ats, gs, pieces = ([refs.pop(0) for _ in range(count)] for _ in range(3))
    sems = named(BACK_SEMS, refs)
    ring_sems, io_sems, swap_sems, far_sems, sum_sems = sems.ring, sems.io, sems.swap, sems.far, sems.sums
    place = Place()
    frame = place.ta // 2
    sources = (work.low3, work.hidden_low, work.low2, work.packed, work.low1, work.packed)
    reductions = []
    for i in range(count):
        own = Names(at_in=lefts[i], at=ats[i], g=gs[i], piece=pieces[i], out=matrix_outs[i], source=sources[i])
        own.s1, own.r1, own.r2, own.r3 = work.s1, work.r1, work.r2, work.r3
        reductions.append(Reduction(place, i, own, sems))
    fout, fin, tout, tqkv, sout, sqkv = reductions
    small = SmallSums(place, work, sum_sems)

    def tall(source, base, index):
        slot = (base + index) % SLOTS
        rows = pl.ds(pl.multiple_of(index * HIDE, HIDE), HIDE)
        return pltpu.make_async_copy(source.at[rows], work.tall.at[slot], ring_sems.at[0, slot])

    def broad(source, base, index):
        slot = (base + index) % SLOTS
        return pltpu.make_async_copy(
            source.at[:, lanes(index, HIDE)], work.broad.at[slot], ring_sems.at[1, slot]
        )

    def slope(base, index):
        slot = (base + index) % SLOTS
        return pltpu.make_async_copy(saved.slope.at[index], work.slope_in.at[slot], ring_sems.at[2, slot])

    def record(source, base, index):
        slot = (base + index) % SLOTS
        return pltpu.make_async_copy(
            source.at[index], work.record.at[slot, pl.ds(0, source.shape[1])], ring_sems.at[3, slot]
        )

    def open_stream(maker, count):
        for index in range(min(SLOTS, count)):
            maker(index).start()

    def refill(maker, count, index):
        @pl.when(index + SLOTS < count)
        def _():
            maker(index + SLOTS).start()

    fout_tiles = functools.partial(tall, weights.w_fout, 0)
    tout_tiles = functools.partial(tall, weights.w_tout, 8)
    sout_tiles = functools.partial(tall, weights.w_sout, 10)
    fin_tiles = functools.partial(broad, weights.w_fin, 0)
    tqkv_tiles = functools.partial(broad, weights.w_tqkv, 8)
    sqkv_tiles = functools.partial(broad, weights.w_sqkv, 14)
    slopes = functools.partial(slope, 0)
    temporal_records = functools.partial(record, saved.temporal, 0)
    spatial_records = functools.partial(record, saved.spatial, 8)

    class Kept:
        def __init__(self, normals, scales):
            self.copies = (
                pltpu.make_async_copy(normals, work.resid, io_sems.at[0]),
                pltpu.make_async_copy(scales, work.scale, io_sems.at[4]),
            )
            for copy in self.copies:
                copy.start()

        def wait(self):
            for copy in self.copies:
                copy.wait()

    fout.lefts()
    open_stream(fout_tiles, 8)
    open_stream(slopes, 8)
    open_stream(fin_tiles, 8)
    work.sums[...] = jnp.zeros_like(work.sums)
    for row, gain in enumerate(gains):
        work.gains[row : row + 1] = gain[...].astype(F32).reshape(1, WIDTH)
    greet(place, True)

    grad, total = work.grad, work.total

    def start_rows(step, carry):
        near = pl.ds(pl.multiple_of(step * 16, 16), 16)
        big = ins.big_cot[near].astype(F32)
        little = ins.small_cot[near].astype(F32) * ins.live[step // 2].astype(F32)
        merged = interleave(big, little)
        rows = pl.ds(pl.multiple_of(step * 32, 32), 32)
        grad[rows] = merged
        work.low3[rows] = merged.astype(BF16)
        total[rows] = jnp.zeros_like(merged)
        work.sums[OUTER : OUTER + 1] += jnp.sum(merged, axis=0, keepdims=True)
        return carry

    lax.fori_loop(0, 8, start_rows, 0)
    fout.rights()
    fin.lefts()
    kept3 = Kept(saved.normal3, saved.scale3)

    def feed(step, carry):
        slopes(step).wait()
        fout_tiles(step).wait()
        fin_tiles(step).wait()
        slot = step % SLOTS
        down = dot_nt(work.low3[...], work.tall[slot]) * work.slope_in[slot].astype(F32)
        work.inner_sums[pl.ds(step, 1)] = jnp.sum(down, axis=0, keepdims=True)
        low = down.astype(BF16)
        work.hidden_low[:, lanes(step, HIDE)] = low
        for column in range(WIDTH // 256):
            at = slice(column * 256, column * 256 + 256)
            total[:, at] += dot_nt(low, work.broad[slot, at])
        refill(slopes, 8, step)
        refill(fout_tiles, 8, step)
        refill(fin_tiles, 8, step)
        return carry

    lax.fori_loop(0, 2, feed, 0)
    fout.loaded()
    fout.first()
    lax.fori_loop(2, 8, feed, 0)
    fin.rights()
    open_stream(temporal_records, 8)
    for one in (tout, tqkv, sout, sqkv):
        one.lefts()
    open_stream(tout_tiles, 2)
    open_stream(sout_tiles, 1)
    open_stream(tqkv_tiles, 6)
    for part in range(PAIRS):
        at = part % 2 * HIDE
        work.sums[INNER + part // 2 : INNER + part // 2 + 1, at : at + HIDE] = work.inner_sums[part : part + 1]

    def norm_back(gradient, gain_row, row, low, bias_row):
        gain = work.gains[gain_row : gain_row + 1]

        def one(step, carry):
            rows = rows16(step)
            error = gradient[rows].astype(F32)
            normal, scale = work.resid[rows], work.scale[rows, 0:1]
            scaled = error * gain
            mean_one = jnp.mean(scaled, axis=-1, keepdims=True)
            mean_two = jnp.mean(scaled * normal, axis=-1, keepdims=True)
            value = grad[rows] + (scaled - mean_one - normal * mean_two) * scale
            grad[rows] = value
            if low is not None:
                low[rows] = value.astype(BF16)
            gains = error * normal
            sums = [part[:8] + part[8:] for part in (gains, error, value)]
            return tuple(a + b for a, b in zip(carry, sums))

        zero = jnp.zeros((8, WIDTH), F32)
        sums = lax.fori_loop(0, 16, one, (zero, zero, zero), unroll=2)
        work.sums[row : row + 1] = jnp.sum(sums[0], axis=0, keepdims=True)
        work.sums[row + 1 : row + 2] = jnp.sum(sums[1], axis=0, keepdims=True)
        if bias_row is not None:
            work.sums[bias_row : bias_row + 1] = jnp.sum(sums[2], axis=0, keepdims=True)

    kept3.wait()
    norm_back(total, 2, GAIN3, work.low2, TEMPORAL_BIAS)
    kept2 = Kept(saved.normal2, saved.scale2)
    tout.rights()

    there = [Swap(place, work.swap_send, work.context_back, swap_sems, i, True, HALVES[i]) for i in range(2)]
    for index in range(2):
        tout_tiles(index).wait()
        slot = (8 + index) % SLOTS
        work.swap_send[:, HALVES[index]] = dot_nt(work.low2[...], work.tall[slot]).astype(BF16)
        there[index].start()
    sout_tiles(1).start()
    fout.pass_on(Z)
    fin.loaded()
    fin.first(Z)
    there[0].wait()
    fout.pass_on(XY)
    fin.first(XY)

    low_lanes = half_masks(128)

    def attention_back(probs, keys, values, queries, upstream):
        upstreams = jnp.concatenate(by_head(upstream, low_lanes), axis=0)
        prob = jnp.concatenate(probs, axis=1)
        wide = prob.astype(F32)
        back = dot_nt(values, upstreams)
        delta = jnp.sum(wide * back, axis=0, keepdims=True)
        error = (wide * (back - delta)).astype(BF16)
        key_grad = dot(error, jnp.concatenate(by_head(queries, low_lanes), axis=0))
        value_grad = dot(prob, upstreams)
        query_grad = join_heads(dot_tn(error, keys), low_lanes)
        return query_grad * 0.125, key_grad, value_grad

    def temporal_pair(pair, carry):
        temporal_records(pair).wait()
        slot = pair % SLOTS
        for half in range(2):
            base = half * 128

            def rows(start, half=half):
                return work.record[slot, start + half * 128 : start + half * 128 + 128]

            probs = [work.record[slot, (half * 2 + h) * 128 : (half * 2 + h) * 128 + 128] for h in range(2)]
            upstream = work.context_back[base : base + 128, lanes(pair, LANES)]
            grads = attention_back(probs, rows(TP_KEY), rows(TP_VALUE), rows(TP_QUERY), upstream)
            for i, value in enumerate(grads):
                work.packed[base : base + 128, lanes(pair + i * PAIRS, LANES)] = value.astype(BF16)
        refill(temporal_records, 8, pair)
        return carry

    lax.fori_loop(0, PAIRS // 2, temporal_pair, 0, unroll=2)
    there[1].wait()
    lax.fori_loop(PAIRS // 2, PAIRS, temporal_pair, 0, unroll=2)
    open_stream(spatial_records, 8)
    tqkv.rights()

    def project_back(maker, base, start, stop):
        def one(step, carry):
            maker(step).wait()
            slot = (base + step) % SLOTS
            low = work.packed[:, lanes(step, HIDE)]
            for column in range(WIDTH // 256):
                at = slice(column * 256, column * 256 + 256)
                value = dot_nt(low, work.broad[slot, at])
                total[:, at] += value
            refill(maker, 6, step)
            return carry

        if start == 0:
            total[...] = jnp.zeros_like(total)
        lax.fori_loop(start, stop, one, 0)

    project_back(tqkv_tiles, 8, 0, 3)
    fin.pass_on(Z)
    fout.relay_sent()
    tout.loaded()
    tout.first()
    tqkv.loaded()
    tqkv.first()
    project_back(tqkv_tiles, 8, 3, 6)
    open_stream(sqkv_tiles, 6)
    for one in there:
        one.sent()
    work.swap_send[...] = total[...].astype(BF16)
    back = Swap(place, work.swap_send, work.normed_back, swap_sems, 2, False)
    back.start()
    fout.second((1,))
    fout.direct_sent()
    back.wait()
    tout.pass_on()
    tqkv.pass_on()
    fin.pass_on(XY)
    fout.second((0, 2))

    kept2.wait()
    norm_back(work.normed_back, 1, GAIN2, work.low1, SPATIAL_BIAS)
    kept1 = Kept(saved.normal1, saved.scale1)
    sout.rights()
    for index in range(2):
        sout_tiles(index).wait()
        slot = (10 + index) % SLOTS
        at = slice(index * HIDE, index * HIDE + HIDE)
        value = dot_nt(work.low1[...], work.tall[slot])
        for which in range(2):
            work.context_grad[which, :, at] = family(value, which).astype(BF16)
    tqkv.rights_sent()

    def spatial_pair(pair, carry):
        spatial_records(pair).wait()
        slot = (8 + pair) % SLOTS
        all_grads = []
        for which in range(2):

            def rows(start, count, which=which):
                return work.record[slot, start + which * count : start + which * count + count]

            probs = [work.record[slot, (which * 2 + h) * 256 : (which * 2 + h) * 256 + 256] for h in range(2)]
            upstream = work.context_grad[which, :, lanes(pair, LANES)]
            all_grads.append(
                attention_back(
                    probs, rows(SP_KEY, 256), rows(SP_VALUE, 256), rows(SP_QUERY, 128), upstream
                )
            )
        for i in range(3):
            value = interleave(all_grads[0][i][:128], all_grads[1][i][:128])
            work.packed[:, lanes(pair + i * PAIRS, LANES)] = value.astype(BF16)
        for i in (1, 2):
            value = interleave(all_grads[0][i][128:], all_grads[1][i][128:])
            work.far_send[:, lanes(pair + (i - 1) * PAIRS, LANES)] = value.astype(BF16)
        refill(spatial_records, 8, pair)
        return carry

    lax.fori_loop(0, PAIRS // 2, spatial_pair, 0, unroll=2)
    fin.second(Z)
    lax.fori_loop(PAIRS // 2, PAIRS, spatial_pair, 0, unroll=2)
    far = remote(work.far_send, work.far_recv, far_sems.at[0], far_sems.at[1], place.partner)
    far.start()
    fin.relay_sent()
    sout.loaded()
    sout.first()
    fin.second(XY)
    far.wait()

    def join(step, carry):
        rows = rows16(step)
        value = work.packed[rows, WIDTH:].astype(F32) + work.far_recv[rows].astype(F32)
        work.packed[rows, WIDTH:] = value.astype(BF16)
        return carry

    lax.fori_loop(0, 16, join, 0)
    sqkv.rights()
    project_back(sqkv_tiles, 14, 0, 2)
    sqkv.loaded()
    sqkv.first()
    fout.third()
    project_back(sqkv_tiles, 14, 2, 4)
    fin.direct_sent()
    sqkv.pass_on()
    sout.pass_on()
    project_back(sqkv_tiles, 14, 4, 6)
    tout.second()
    tqkv.second()
    fout.fourth()
    fout.gather()
    kept1.wait()
    norm_back(total, 0, GAIN1, None, None)

    def finish_rows(step, carry):
        value = grad[pl.ds(pl.multiple_of(step * 32, 32), 32)]
        big, little = family(value, 0), family(value, 1)
        near = pl.ds(pl.multiple_of(step * 16, 16), 16)
        total[near] = big
        total[pl.ds(pl.multiple_of(128 + step * 16, 16), 16)] = little
        work.frame_sums[0:1] += jnp.sum(big, axis=0, keepdims=True)
        work.frame_sums[pl.ds(1 + step // 2, 1)] += jnp.sum(little, axis=0, keepdims=True)
        return carry

    work.frame_sums[...] = jnp.zeros_like(work.frame_sums)
    lax.fori_loop(0, 8, finish_rows, 0)
    out_copies = [
        pltpu.make_async_copy(total.at[:128], outs.big_grad, io_sems.at[1]),
        pltpu.make_async_copy(total.at[128:], outs.small_grad, io_sems.at[2]),
    ]
    for copy in out_copies:
        copy.start()
    table, at_row = jnp.zeros((8, WIDTH), F32), lax.broadcasted_iota(jnp.int32, (8, WIDTH), 0)
    for i in range(5):
        action = ins.big_actions[0, frame] if i == 0 else ins.small_actions[i - 1, frame]
        table = table + jnp.where(at_row == action, work.frame_sums[i : i + 1], 0.0)
    work.sums[0:8] = table
    small.begin()
    fin.third()
    small.step0()
    sqkv.second()
    sout.second()
    fout.spread()
    tout.third()
    tqkv.third()
    small.advance(0)
    fin.fourth()
    fin.gather()
    sqkv.third()
    sout.third()
    small.advance(1)
    tout.fourth()
    tout.gather()
    tqkv.fourth()
    tqkv.gather()
    fout.fifth()
    fin.spread()
    sqkv.fourth()
    sqkv.gather()
    sout.fourth()
    sout.gather()
    small.advance(2)
    tout.spread()
    tqkv.spread()
    fin.fifth()
    sqkv.fifth()
    sout.fifth()
    tout.fifth()
    tqkv.fifth()
    small.finish(outs.small_sums, io_sems.at[3])
    for one in reductions:
        one.finish()
    for one in (tout, tqkv, sout, sqkv):
        one.relay_sent()
        one.direct_sent()
    for one in (fout, fin, tout, sout, sqkv):
        one.rights_sent()
    back.sent()
    for copy in out_copies:
        copy.wait()


def backward(ins, scalars, gains, lefts, saved, weights):
    sem = pltpu.SemaphoreType.DMA
    count = len(MATRICES)
    work = [pltpu.VMEM(shape, dtype) for shape, dtype in BACK_WORK.values()]
    work += [pltpu.VMEM((2, 4, 2, 4, k // 64, 2 * ROWS), BF16) for k, _, _ in MATRICES]
    work += [pltpu.VMEM((2 * ROWS, n // 2), BF16) for _, n, _ in MATRICES]
    work += [pltpu.VMEM((2, k // 64, n // 2), BF16) for k, n, _ in MATRICES]
    work += [sem(shape) for shape in BACK_SEMS.values()]
    shapes = list(BACK_OUTS.values()) + [((2, 4, k // 64, n), BF16) for k, n, _ in MATRICES]
    in_keys, saved_keys, weight_keys = tuple(vars(ins)) + tuple(vars(scalars)), tuple(vars(saved)), tuple(vars(weights))
    return pl.pallas_call(
        functools.partial(backward_kernel, in_keys, saved_keys, weight_keys),
        out_shape=[jax.ShapeDtypeStruct(shape, dtype) for shape, dtype in shapes],
        in_specs=[VMEM] * len(vars(ins))
        + [SMEM] * len(vars(scalars))
        + [VMEM] * len(gains)
        + [ANY] * (count + len(saved_keys) + len(weight_keys)),
        out_specs=[ANY] * len(shapes),
        scratch_shapes=work,
        compiler_params=pltpu.CompilerParams(
            collective_id=2, has_side_effects=True, vmem_limit_bytes=63 * 2**20
        ),
        cost_estimate=pl.CostEstimate(flops=18 * 10**9, bytes_accessed=80 * 2**20, transcendentals=0),
        name="layer_backward",
    )(
        *vars(ins).values(),
        *vars(scalars).values(),
        *gains,
        *[left.reshape(2, 4, 2, 4, k // 64, 2 * ROWS) for left, (k, _, _) in zip(lefts, MATRICES)],
        *vars(saved).values(),
        *vars(weights).values(),
    )


SUM_VECTORS = (
    (GAIN1, 1),
    (SHIFT1, 1),
    (SPATIAL_BIAS, 1),
    (GAIN2, 1),
    (SHIFT2, 1),
    (TEMPORAL_BIAS, 1),
    (GAIN3, 1),
    (SHIFT3, 1),
    (INNER, 4),
    (OUTER, 1),
)


def widen_kernel(*refs):
    refs = list(refs)
    count, passed = len(MATRICES), 4
    narrow = [refs.pop(0) for _ in range(count)]
    plain = [refs.pop(0) for _ in range(passed)]
    sums = refs.pop(0)
    wide = [refs.pop(0) for _ in range(count)]
    plain_out = [refs.pop(0) for _ in range(passed)]
    table, vectors = refs.pop(0), [refs.pop(0) for _ in SUM_VECTORS]
    narrow_in, wide_out = refs[:count], refs[count : 2 * count]
    between, sems = refs[2 * count : 2 * count + passed], refs[2 * count + passed]
    loads = [pltpu.make_async_copy(narrow[i], narrow_in[i], sems.at[0, i]) for i in range(count)]
    stores = [pltpu.make_async_copy(wide_out[i], wide[i], sems.at[1, i]) for i in range(count)]
    reads = [pltpu.make_async_copy(plain[i], between[i], sems.at[2, i]) for i in range(passed)]
    moves = [pltpu.make_async_copy(between[i], plain_out[i], sems.at[3, i]) for i in range(passed)]
    for copy in loads + reads:
        copy.start()
    table[...] = sums[0:8]
    for (row, rows), vector in zip(SUM_VECTORS, vectors):
        for i in range(rows):
            vector[i * WIDTH : (i + 1) * WIDTH] = sums[row + i]
    for i in range(count):
        loads[i].wait()

        def one(step, carry, i=i):
            wide_out[i][rows16(step)] = narrow_in[i][rows16(step)].astype(F32)
            return carry

        lax.fori_loop(0, narrow_in[i].shape[0] // 16, one, 0, unroll=2)
        stores[i].start()
    for read, move in zip(reads, moves):
        read.wait()
        move.start()
    for copy in stores + moves:
        copy.wait()


def widen(matrices, plain, sums):
    count = len(matrices)
    vectors = [jax.ShapeDtypeStruct((rows * WIDTH,), F32) for _, rows in SUM_VECTORS]
    shapes = [jax.ShapeDtypeStruct(one.shape, F32) for one in matrices]
    scratch = [pltpu.VMEM(one.shape, BF16) for one in matrices] + [pltpu.VMEM(one.shape, F32) for one in matrices]
    scratch += [pltpu.VMEM(one.shape, one.dtype) for one in plain]
    results = pl.pallas_call(
        widen_kernel,
        out_shape=shapes
        + [jax.ShapeDtypeStruct(one.shape, one.dtype) for one in plain]
        + [jax.ShapeDtypeStruct((8, WIDTH), F32)]
        + vectors,
        in_specs=[ANY] * (count + len(plain)) + [VMEM],
        out_specs=[ANY] * (count + len(plain)) + [VMEM] * (1 + len(vectors)),
        scratch_shapes=scratch + [pltpu.SemaphoreType.DMA((4, count))],
        compiler_params=pltpu.CompilerParams(vmem_limit_bytes=62 * 2**20),
        cost_estimate=pl.CostEstimate(flops=0, bytes_accessed=14 * 2**20, transcendentals=0),
        name="widen",
    )(*matrices, *plain, sums)
    results = list(results)
    wide = [results.pop(0) for _ in range(count)]
    passed = [results.pop(0) for _ in plain]
    return wide, passed, results


def body(
    big_tokens,
    small_tokens,
    big_actions,
    small_actions,
    big_order,
    small_order,
    small_live,
    action_table,
    norm1_gain,
    norm1_bias,
    spatial_qkv,
    spatial_out,
    spatial_out_bias,
    norm2_gain,
    norm2_bias,
    temporal_qkv,
    temporal_out,
    temporal_out_bias,
    norm3_gain,
    norm3_bias,
    ffn_in,
    ffn_in_bias,
    ffn_out,
    ffn_out_bias,
    big_cotangent,
    small_cotangent,
):
    scalars = Names(
        big_actions=big_actions,
        small_actions=small_actions,
        big_order=big_order,
        small_order=small_order,
        live=small_live,
    )
    vectors = (
        norm1_gain,
        norm1_bias,
        spatial_out_bias,
        norm2_gain,
        norm2_bias,
        temporal_out_bias,
        norm3_gain,
        norm3_bias,
        ffn_out_bias,
    )
    weights = Names(
        w_sqkv=spatial_qkv,
        w_sout=spatial_out,
        w_tqkv=temporal_qkv,
        w_tout=temporal_out,
        w_fin=ffn_in,
        w_fout=ffn_out,
    )
    saved = forward(
        Names(
            big=big_tokens.reshape(128, WIDTH),
            small=small_tokens.reshape(128, WIDTH),
            table=action_table,
            inner_bias=ffn_in_bias,
        ),
        scalars,
        vectors,
        weights,
    )
    big_grad, small_grad, sums, *matrices = backward(
        Names(big_cot=big_cotangent.reshape(128, WIDTH), small_cot=small_cotangent.reshape(128, WIDTH)),
        Names(big_actions=big_actions, small_actions=small_actions, live=small_live),
        (norm1_gain, norm2_gain, norm3_gain),
        (saved.activated_t, saved.normed3_t, saved.context2_t, saved.normed2_t, saved.context1_t, saved.normed1_t),
        Names(
            normal1=saved.normal1,
            normal2=saved.normal2,
            normal3=saved.normal3,
            scale1=saved.scale1,
            scale2=saved.scale2,
            scale3=saved.scale3,
            spatial=saved.spatial,
            temporal=saved.temporal,
            slope=saved.slope,
        ),
        weights,
    )
    matrices = [one.reshape(-1, one.shape[-1]) for one in matrices]
    matrices, passed, small = widen(matrices, (saved.big_out, saved.small_out, big_grad, small_grad), sums)
    g_fout, g_fin, g_tout, g_tqkv, g_sout, g_sqkv = matrices
    table, gain1, shift1, bias_s, gain2, shift2, bias_t, gain3, shift3, bias_in, bias_out = small
    return (
        passed[0].reshape(1, 128, WIDTH),
        passed[1].reshape(4, 32, WIDTH),
        passed[2].reshape(1, 128, WIDTH),
        passed[3].reshape(4, 32, WIDTH),
        table,
        gain1,
        shift1,
        g_sqkv,
        g_sout,
        bias_s,
        gain2,
        shift2,
        g_tqkv,
        g_tout,
        bias_t,
        gain3,
        shift3,
        g_fin,
        bias_in,
        g_fout,
        bias_out,
    )


def solution(mesh):
    spread, by_col = P("col", "ta", None), P("col", None)
    return jax.shard_map(
        body,
        mesh=mesh,
        in_specs=(spread, spread, by_col, by_col, by_col, by_col, P("col")) + (P(),) * 17 + (spread, spread),
        out_specs=(spread,) * 4
        + (P(),) * 3
        + (by_col, by_col, P(), P(), P(), by_col, by_col, P(), P(), P(), by_col, P(), by_col, P()),
        check_vma=False,
    )
```

```python
import functools
from types import SimpleNamespace as Names

import jax
import jax.numpy as jnp
from jax import lax
from jax.experimental import pallas as pl
from jax.experimental.pallas import tpu as pltpu
from jax.sharding import PartitionSpec as P

HEAD_DIM = 64
EPSILON = 1e-05
MASKED_SCORE = -1e30
MESH = pl.DeviceIdType.MESH
ANY = pl.BlockSpec(memory_space=pl.ANY)
VMEM = pl.BlockSpec(memory_space=pltpu.VMEM)
SMEM = pl.BlockSpec(memory_space=pltpu.SMEM)
LANES = 128
F32, BF16 = jnp.float32, jnp.bfloat16
ROWS, WIDTH, HIDDEN = 256, 1024, 4096
PAIRS = WIDTH // LANES
HIDE = 512

SP_KEY, SP_VALUE, SP_QUERY, SP_ROWS = 1024, 1536, 2048, 2304
TP_KEY, TP_VALUE, TP_QUERY, TP_ROWS = 512, 768, 1024, 1280

ORDERS = (("x", "y", "z"), ("y", "z", "x"), ("z", "x", "y"))
MATRICES = (
    (HIDDEN, WIDTH, None, 0, 0),
    (WIDTH, HIDDEN, (4, 6, 6), 1, 0),
    (WIDTH, WIDTH, (1, 1, 2), 2, 0),
    (WIDTH, 3 * WIDTH, (4, 4, 4), 3, 0),
    (WIDTH, WIDTH, (1, 1, 2), 4, 0),
    (WIDTH, WIDTH, (1, 1, 2), 5, 0),
    (WIDTH, 2 * WIDTH, (3, 3, 2), 5, WIDTH),
)
GRADIENTS = (
    (HIDDEN, WIDTH),
    (WIDTH, HIDDEN),
    (WIDTH, WIDTH),
    (WIDTH, 3 * WIDTH),
    (WIDTH, WIDTH),
    (WIDTH, 3 * WIDTH),
)
ALL, XY, Z = (0, 1, 2), (0, 1), (2,)
SEND_UNITS = (0, 16, 12, 0, 28, 16, 20)


class Place:
    def __init__(self):
        ta, col = lax.axis_index("ta"), lax.axis_index("col")
        self.ta, self.col = ta, col
        self.y_hi, self.x, self.core = ta // 8, (ta // 2) % 4, ta % 2
        self.y_lo, self.z = col // 4, col % 4
        self.y = self.y_hi * 2 + self.y_lo
        self.partner = self.device(core=1 - self.core)

    def device(self, y_hi=None, x=None, core=None, y_lo=None, z=None):
        y_hi = self.y_hi if y_hi is None else y_hi
        x = self.x if x is None else x
        core = self.core if core is None else core
        y_lo = self.y_lo if y_lo is None else y_lo
        z = self.z if z is None else z
        return (y_hi * 8 + x * 2 + core, y_lo * 4 + z)

    def along(self, axis, step):
        if axis == "x":
            at = (self.x + step) % 4
            return self.device(x=at), at
        if axis == "z":
            at = (self.z + step) % 4
            return self.device(z=at), at
        at = (self.y + step) % 4
        return self.device(y_hi=at // 2, y_lo=at % 2), (at % 2) * 2 + at // 2

    def fellow(self, step):
        ta = (self.ta + step) % 16
        return (ta, self.col), ta


def greet(place, whole):
    barrier = pltpu.get_barrier_semaphore()

    def one(step, carry):
        pl.semaphore_signal(barrier, inc=1, device_id=place.fellow(step)[0], device_id_type=MESH)
        return carry

    lax.fori_loop(1, 16, one, 0)
    count = 15
    if whole:
        for axis, step in (("y", 1), ("y", 3), ("z", 1), ("z", 2), ("z", 3)):
            pl.semaphore_signal(barrier, inc=1, device_id=place.along(axis, step)[0], device_id_type=MESH)
            count += 1
    pl.semaphore_wait(barrier, count)


def remote(source, target, send, recv, device):
    return pltpu.make_async_remote_copy(source, target, send, recv, device_id=device, device_id_type=MESH)


def dot(left, right):
    return jnp.dot(left, right, preferred_element_type=F32)


def dot_nt(left, right):
    return lax.dot_general(left, right, (((1,), (1,)), ((), ())), preferred_element_type=F32)


def dot_tn(left, right):
    return lax.dot_general(left, right, (((0,), (0,)), ((), ())), preferred_element_type=F32)


def rows16(step):
    return pl.ds(pl.multiple_of(step * 16, 16), 16)


def lanes(step, width):
    return pl.ds(pl.multiple_of(step * width, width), width)


def interleave(big, small):
    width = big.shape[-1]
    pair = [one.reshape(-1, 1, 8, width) for one in (big, small)]
    return jnp.concatenate(pair, axis=1).reshape(-1, width)


def family(rows, which):
    width = rows.shape[-1]
    return rows.reshape(-1, 2, 8, width)[:, which].reshape(-1, width)


def half_masks(rows):
    lane = lax.broadcasted_iota(jnp.int32, (rows, LANES), 1)
    return lane < HEAD_DIM


def by_head(value, low):
    zero = jnp.zeros_like(value)
    return jnp.where(low, value, zero), jnp.where(low, zero, value)


def join_heads(value, low):
    return jnp.where(low, value[:128], value[128:])


def statistics(rows):
    mean = jnp.mean(rows, axis=-1, keepdims=True)
    centered = rows - mean
    variance = jnp.mean(centered * centered, axis=-1, keepdims=True)
    scale = lax.rsqrt(variance + EPSILON)
    return centered * scale, scale


def norm_forward(source, gain, shift, target, normals, scales, after=None):
    def one(step, carry):
        rows = rows16(step)
        normal, scale = statistics(source[rows])
        target[rows] = (normal * gain + shift).astype(BF16)
        normals[rows] = normal
        scales[rows] = jnp.broadcast_to(scale, (16, LANES))
        if after is not None:
            after(step)
        return carry

    lax.fori_loop(0, 16, one, 0, unroll=4)


def transpose_into(source, target):
    def one(step, carry):
        target[step] = source[:, lanes(step, LANES)].T
        return carry

    lax.fori_loop(0, PAIRS, one, 0, unroll=4)


class Swap:
    def __init__(self, place, send, recv, sems, index, to_positions, columns=slice(0, WIDTH)):
        self.place, self.send, self.recv, self.sems, self.index = place, send, recv, sems, index
        self.to_positions, self.columns = to_positions, columns

    def rows(self, ta):
        frames = rows16(ta)
        positions = rows16((ta % 2) * 8 + ta // 2)
        return (frames, positions) if self.to_positions else (positions, frames)

    def copy(self, step):
        device, ta = self.place.fellow(step)
        source = self.send.at[self.rows(ta)[0], self.columns]
        target = self.recv.at[self.rows(self.place.ta)[1], self.columns]
        return remote(source, target, self.sems.at[self.index, 0, step], self.sems.at[self.index, 1, step], device)

    def own(self):
        rows = self.rows(self.place.ta)
        source, target = self.send.at[rows[0], self.columns], self.recv.at[rows[1], self.columns]
        return pltpu.make_async_copy(source, target, self.sems.at[self.index, 0, 0])

    def start_block(self, ta):
        step = (ta - self.place.ta + 16) % 16

        @pl.when(step > 0)
        def _():
            self.copy(step).start()

        @pl.when(step == 0)
        def _():
            self.own().start()

    def start(self):
        def one(step, carry):
            self.copy(step).start()
            return carry

        lax.fori_loop(1, 16, one, 0)
        self.own().start()

    def wait(self):
        def one(step, carry):
            self.copy(step).wait_recv()
            return carry

        self.own().wait()
        lax.fori_loop(1, 16, one, 0)

    def sent(self):
        def one(step, carry):
            self.copy(step).wait_send()
            return carry

        lax.fori_loop(1, 16, one, 0)


HALVES = (slice(0, WIDTH // 2), slice(WIDTH // 2, WIDTH))


FORWARD_OUTS = dict(
    big_out=((128, WIDTH), BF16),
    small_out=((128, WIDTH), BF16),
    normal1=((ROWS, WIDTH), F32),
    normal2=((ROWS, WIDTH), F32),
    normal3=((ROWS, WIDTH), F32),
    scale1=((ROWS, LANES), F32),
    scale2=((ROWS, LANES), F32),
    scale3=((ROWS, LANES), F32),
    spatial=((PAIRS, SP_ROWS, LANES), BF16),
    temporal=((PAIRS, TP_ROWS, LANES), BF16),
    slope=((PAIRS, ROWS, HIDE), BF16),
)
FORWARD_LEFTS = dict(
    activated_t=((PAIRS, HIDE, ROWS), BF16),
    normed3_t=((PAIRS, LANES, ROWS), BF16),
    context2_t=((PAIRS, LANES, ROWS), BF16),
    normed2_t=((PAIRS, LANES, ROWS), BF16),
    context1_t=((PAIRS, LANES, ROWS), BF16),
    normed1_t=((PAIRS, LANES, ROWS), BF16),
)
FORWARD_WORK = dict(
    w_sqkv=((WIDTH, 3 * WIDTH), BF16),
    w_sout=((WIDTH, WIDTH), BF16),
    w_tqkv=((WIDTH, 3 * WIDTH), BF16),
    w_tout=((WIDTH, WIDTH), BF16),
    w_fin=((WIDTH, HIDDEN), BF16),
    w_fout=((HIDDEN, WIDTH), BF16),
    normed=((ROWS, WIDTH), BF16),
    context=((ROWS, WIDTH), BF16),
    arranged=((ROWS, WIDTH), BF16),
    context_send=((ROWS, WIDTH), BF16),
    context_back=((ROWS, WIDTH), BF16),
    normed3=((ROWS, WIDTH), BF16),
    total=((ROWS, WIDTH), F32),
    hidden=((2, ROWS, HIDE), F32),
    params=((16, WIDTH), F32),
    inner_bias=((PAIRS, HIDE), F32),
    table=((8, WIDTH), F32),
)


def named(keys, refs):
    return Names(**{key: refs.pop(0) for key in keys})


def forward_kernel(in_keys, vector_count, weight_keys, *refs):
    refs = list(refs)
    ins = named(in_keys, refs)
    vectors = [refs.pop(0) for _ in range(vector_count)]
    weights = named(weight_keys, refs)
    kept = FORWARD_OUTS | FORWARD_LEFTS
    outs, keep, work = named(kept, refs), named(kept, refs), named(FORWARD_WORK, refs)
    w_sems, out_sems, swap_sems, far_sems, pair_sems, feed_sems = refs
    place = Place()
    params = work.params

    def param(row):
        return params[row : row + 1]

    loads = Names()
    for i, key in enumerate(weight_keys):
        setattr(loads, key, pltpu.make_async_copy(getattr(weights, key), getattr(work, key), w_sems.at[i]))
    loads.w_sqkv.start()
    for row, vector in enumerate(vectors):
        params[row : row + 1] = vector[...].astype(F32).reshape(1, WIDTH)
    for row in range(PAIRS):
        at = slice(row * HIDE, row * HIDE + HIDE)
        work.inner_bias[row : row + 1] = ins.inner_bias[at].astype(F32).reshape(1, HIDE)
    work.table[...] = ins.table[...].astype(F32)
    frame = place.ta // 2
    copies = []

    def save(source, target):
        copy = pltpu.make_async_copy(source, target, out_sems.at[len(copies)])
        copy.start()
        copies.append(copy)

    shared = []

    def share(source, target):
        save(source, target.at[:, :, :ROWS])
        i = len(shared)
        copy = remote(source, target.at[:, :, ROWS:], pair_sems.at[0, i], pair_sems.at[1, i], place.partner)
        copy.start()
        shared.append(copy)

    resid0, resid1, resid2 = keep.normal2, keep.normal3, work.total
    big_row = work.table[pl.ds(ins.big_actions[0, frame], 1)]

    def start_rows(step, carry):
        near = pl.ds(pl.multiple_of(step * 16, 16), 16)
        big = ins.big[near].astype(F32) + big_row
        small = ins.small[near].astype(F32) + work.table[pl.ds(ins.small_actions[step // 2, frame], 1)]
        rows = pl.ds(pl.multiple_of(step * 32, 32), 32)
        merged = interleave(big, small)
        resid0[rows] = merged
        normal, scale = statistics(merged)
        work.normed[rows] = (normal * param(0) + param(1)).astype(BF16)
        keep.normal1[rows] = normal
        keep.scale1[rows] = jnp.broadcast_to(scale, (32, LANES))
        return carry

    lax.fori_loop(0, 8, start_rows, 0)
    save(keep.normal1, outs.normal1)
    save(keep.scale1, outs.scale1)
    greet(place, False)

    spatial = keep.spatial
    loads.w_sqkv.wait()
    for key in weight_keys[1:]:
        getattr(loads, key).start()

    def spatial_project(column, base, per_family, scale):
        def one(step, carry):
            at = column + step
            value = dot(work.normed[...], work.w_sqkv[:, lanes(at, 256)]) * scale
            for which in range(2):
                one_family = family(value, which).astype(BF16)
                rows = pl.ds(base + which * per_family, 128)
                spatial[step * 2, rows] = one_family[:, :LANES]
                spatial[step * 2 + 1, rows] = one_family[:, LANES:]
            return carry

        lax.fori_loop(0, 4, one, 0, unroll=2)

    spatial_project(4, SP_KEY, 256, 1.0)
    spatial_project(8, SP_VALUE, 256, 1.0)
    far = []
    for i, base in enumerate((SP_KEY, SP_KEY + 256, SP_VALUE, SP_VALUE + 256)):
        far.append(
            remote(
                spatial.at[:, pl.ds(base, 128)], spatial.at[:, pl.ds(base + 128, 128)],
                far_sems.at[0, i], far_sems.at[1, i], place.partner,
            )
        )
    for copy in far:
        copy.start()
    spatial_project(0, SP_QUERY, 128, 0.125)
    transpose_into(work.normed, keep.normed1_t)
    share(keep.normed1_t, outs.normed1_t)
    for copy in far:
        copy.wait()

    low_q = half_masks(128)
    key_slot = (lax.broadcasted_iota(jnp.int32, (256, 256), 0) % 128) // 32
    query_slot = (lax.broadcasted_iota(jnp.int32, (256, 256), 1) % 128) // 32
    same_slot = key_slot == query_slot

    def softmax(scores):
        weights_ = jnp.exp(scores - jnp.max(scores, axis=0, keepdims=True))
        return (weights_ * (1.0 / jnp.sum(weights_, axis=0, keepdims=True))).astype(BF16)

    def attend(keys, values, queries, visible):
        scores = dot_nt(keys, jnp.concatenate(by_head(queries, low_q), axis=0))
        if visible is not None:
            scores = jnp.where(visible, scores, MASKED_SCORE)
        probs = softmax(scores)
        return (probs[:, :LANES], probs[:, LANES:]), join_heads(dot_tn(probs, values), low_q)

    def spatial_pairs(step, carry):
        loaded = []
        for pair in (step * 2, step * 2 + 1):
            for which in range(2):
                keys = spatial[pair, SP_KEY + which * 256 : SP_KEY + which * 256 + 256]
                values = spatial[pair, SP_VALUE + which * 256 : SP_VALUE + which * 256 + 256]
                queries = spatial[pair, SP_QUERY + which * 128 : SP_QUERY + which * 128 + 128]
                loaded.append((keys, values, queries, same_slot if which else None))
        done = [attend(*one) for one in loaded]
        for i in range(2):
            pair = step * 2 + i
            for which in range(2):
                for head in range(2):
                    at = (which * 2 + head) * 256
                    spatial[pair, at : at + 256] = done[i * 2 + which][0][head]
            value = interleave(done[i * 2][1], done[i * 2 + 1][1])
            work.context[:, lanes(pair, LANES)] = value.astype(BF16)
        return carry

    lax.fori_loop(0, PAIRS // 2, spatial_pairs, 0)
    save(keep.spatial, outs.spatial)

    def project_into(source, weight, bias, before, target):
        def one(step, carry):
            at = lanes(step, 256)
            target[:, at] = dot(source[...], weight[:, at]) + params[bias : bias + 1, at] + before[:, at]
            return carry

        lax.fori_loop(0, WIDTH // 256, one, 0, unroll=2)

    loads.w_sout.wait()
    project_into(work.context, work.w_sout, 2, resid0, resid1)
    there = Swap(place, work.normed, work.arranged, swap_sems, 0, True)
    norm_forward(resid1, param(3), param(4), work.normed, keep.normal2, keep.scale2, there.start_block)
    save(keep.normal2, outs.normal2)
    save(keep.scale2, outs.scale2)
    transpose_into(work.context, keep.context1_t)
    share(keep.context1_t, outs.context1_t)
    loads.w_tqkv.wait()
    there.wait()

    temporal = keep.temporal

    def temporal_project(column, base, scale):
        def one(step, carry):
            value = dot(work.arranged[...], work.w_tqkv[:, lanes(column + step, 256)]) * scale
            value = value.astype(BF16)
            temporal[step * 2, base : base + ROWS] = value[:, :LANES]
            temporal[step * 2 + 1, base : base + ROWS] = value[:, LANES:]
            return carry

        lax.fori_loop(0, 4, one, 0, unroll=2)

    temporal_project(0, TP_QUERY, 0.125)
    temporal_project(4, TP_KEY, 1.0)
    temporal_project(8, TP_VALUE, 1.0)
    key_row = lax.broadcasted_iota(jnp.int32, (128, 256), 0)
    query_row = lax.broadcasted_iota(jnp.int32, (128, 256), 1) % 128
    key_rank, query_rank = jnp.zeros_like(key_row), jnp.zeros_like(query_row)
    for at in range(8):
        big_rank, small_rank = ins.big_order[0, at], ins.small_order[place.ta // 4, at]
        key_rank = jnp.where(key_row // 16 == at, jnp.where(key_row % 16 < 8, big_rank, small_rank), key_rank)
        query_rank = jnp.where(query_row // 16 == at, jnp.where(query_row % 16 < 8, big_rank, small_rank), query_rank)
    seen = (key_row % 16 == query_row % 16) & (key_rank <= query_rank)

    def temporal_pairs(step, carry):
        loaded = []
        for pair in (step * 2, step * 2 + 1):
            for half in range(2):
                keys = temporal[pair, TP_KEY + half * 128 : TP_KEY + half * 128 + 128]
                values = temporal[pair, TP_VALUE + half * 128 : TP_VALUE + half * 128 + 128]
                queries = temporal[pair, TP_QUERY + half * 128 : TP_QUERY + half * 128 + 128]
                loaded.append((keys, values, queries, seen))
        done = [attend(*one) for one in loaded]
        for i in range(2):
            pair = step * 2 + i
            for half in range(2):
                for head in range(2):
                    at = (half * 2 + head) * 128
                    temporal[pair, at : at + 128] = done[i * 2 + half][0][head]
                at = slice(half * 128, half * 128 + 128)
                work.context_send[at, lanes(pair, LANES)] = done[i * 2 + half][1].astype(BF16)
        return carry

    back = [Swap(place, work.context_send, work.context_back, swap_sems, 1 + i, False, HALVES[i]) for i in range(2)]
    lax.fori_loop(0, PAIRS // 4, temporal_pairs, 0)
    back[0].start()
    lax.fori_loop(PAIRS // 4, PAIRS // 2, temporal_pairs, 0)
    back[1].start()
    save(keep.temporal, outs.temporal)
    transpose_into(work.arranged, keep.normed2_t)
    share(keep.normed2_t, outs.normed2_t)
    loads.w_tout.wait()
    for i in range(2):
        back[i].wait()

        def add_half(step, carry, i=i):
            at = lanes(step, 256)
            value = dot(work.context_back[:, HALVES[i]], work.w_tout[HALVES[i], at])
            if i == 0:
                resid2[:, at] = value + params[5:6, at] + resid1[:, at]
            else:
                resid2[:, at] += value
            return carry

        lax.fori_loop(0, WIDTH // 256, add_half, 0, unroll=2)
    norm_forward(resid2, param(6), param(7), work.normed3, keep.normal3, keep.scale3)
    save(keep.normal3, outs.normal3)
    save(keep.scale3, outs.scale3)
    transpose_into(work.context_back, keep.context2_t)
    share(keep.context2_t, outs.context2_t)
    transpose_into(work.normed3, keep.normed3_t)
    share(keep.normed3_t, outs.normed3_t)

    total, hidden, slope = work.total, work.hidden, keep.slope
    total[...] += param(8)
    loads.w_fin.wait()
    loads.w_fout.wait()
    root = 0.7978845608028654

    def inner(step, slot):
        hidden[slot] = dot(work.normed3[...], work.w_fin[:, lanes(step, HIDE)])

    def feed_copies(step):
        here, there_ = keep.activated_t.at[step], outs.activated_t.at[step]
        return (
            pltpu.make_async_copy(here, there_.at[:, :ROWS], feed_sems.at[0, step]),
            remote(here, there_.at[:, ROWS:], feed_sems.at[1, step], feed_sems.at[2, step], place.partner),
            pltpu.make_async_copy(slope.at[step], outs.slope.at[step], feed_sems.at[3, step]),
        )

    def feed(step, slot, ahead):
        value = hidden[slot] + work.inner_bias[pl.ds(step, 1)]
        if ahead:
            inner(step + 1, 1 - slot)
        square = value * value
        bent = jnp.tanh(root * value * (1.0 + 0.044715 * square))
        half = 0.5 * (1.0 + bent)
        active = (value * half).astype(BF16)
        rise = half + 0.5 * value * (1.0 - bent * bent) * (root * (1.0 + 0.134145 * square))
        slope[step] = rise.astype(BF16)
        for block in range(HIDE // LANES):
            at = slice(block * LANES, block * LANES + LANES)
            keep.activated_t[step, at] = active[:, at].T
        down = work.w_fout.at[pl.ds(pl.multiple_of(step * HIDE, HIDE), HIDE)]
        for column in range(WIDTH // 256):
            at = slice(column * 256, column * 256 + 256)
            total[:, at] += dot(active, down[:, at])
        for copy in feed_copies(step):
            copy.start()

    def feed_two(step, carry):
        feed(step * 2, 0, True)
        feed(step * 2 + 1, 1, True)
        return carry

    for one in back:
        one.sent()
    inner(0, 0)
    lax.fori_loop(0, PAIRS // 2 - 1, feed_two, 0)
    feed(PAIRS - 2, 0, True)
    feed(PAIRS - 1, 1, False)

    def finish_rows(step, carry):
        value = total[pl.ds(pl.multiple_of(step * 32, 32), 32)]
        near = pl.ds(pl.multiple_of(step * 16, 16), 16)
        keep.big_out[near] = family(value, 0).astype(BF16)
        keep.small_out[near] = (family(value, 1) * ins.live[step // 2].astype(F32)).astype(BF16)
        return carry

    lax.fori_loop(0, 8, finish_rows, 0)
    save(keep.big_out, outs.big_out)
    save(keep.small_out, outs.small_out)
    there.sent()
    for copy in copies + shared + [one for step in range(PAIRS) for one in feed_copies(step)]:
        copy.wait()


def forward(ins, scalars, vectors, weights):
    sem = pltpu.SemaphoreType.DMA
    lefts, work = list(FORWARD_LEFTS.values()), list(FORWARD_WORK.values())
    kept = list(FORWARD_OUTS.values()) + lefts
    results = list(FORWARD_OUTS.values()) + [((rows, depth, 2 * columns), dtype) for (rows, depth, columns), dtype in lefts]
    in_keys, weight_keys = tuple(vars(ins)) + tuple(vars(scalars)), tuple(vars(weights))
    results = pl.pallas_call(
        functools.partial(forward_kernel, in_keys, len(vectors), weight_keys),
        out_shape=[jax.ShapeDtypeStruct(shape, dtype) for shape, dtype in results],
        in_specs=[VMEM] * len(vars(ins)) + [SMEM] * len(vars(scalars)) + [VMEM] * len(vectors) + [ANY] * len(weight_keys),
        out_specs=[ANY] * len(kept),
        scratch_shapes=[pltpu.VMEM(shape, dtype) for shape, dtype in kept + work]
        + [sem((len(weight_keys),)), sem((len(kept),)), sem((3, 2, 16)), sem((2, 4)), sem((2, 6)), sem((4, PAIRS))],
        compiler_params=pltpu.CompilerParams(
            collective_id=1, has_side_effects=True, vmem_limit_bytes=62 * 2**20
        ),
        cost_estimate=pl.CostEstimate(flops=9 * 10**9, bytes_accessed=60 * 2**20, transcendentals=4 * 10**6),
        name="layer_forward",
    )(*vars(ins).values(), *vars(scalars).values(), *vectors, *vars(weights).values())
    return named(FORWARD_OUTS | FORWARD_LEFTS, list(results))


class Reduction:
    def __init__(self, place, index, refs, sems):
        self.place, self.index, self.refs, self.sems = place, index, refs, sems
        k, n, shares, unused_output, self.column = MATRICES[index]
        self.half = n // 2
        self.depth = k // 64
        self.groups = self.depth // 16
        if shares is None:
            self.blocks = [[(part, 0, 4), (3, part, part + 1 + part // 2)] for part in range(3)]
        else:
            ends = [sum(shares[: part + 1]) for part in range(3)]
            self.blocks = [[(0, end - share, end)] for share, end in zip(shares, ends)]
        self.cells = [[(g, t) for g, low, high in part for t in range(low, high)] for part in self.blocks]
        self.spans, start = [], 0
        for cells in self.cells:
            self.spans.append((start, start + len(cells)))
            start += len(cells)
        self.first_unit = sum(m[1] // 2 // LANES * (m[0] // 1024) for m in MATRICES[:index])
        self.send_unit = SEND_UNITS[index]
        self.local_done = self.left_done = False
        self.straight = index >= 4
        self.whole_parts = ()

    def columns(self, core):
        return pl.ds(pl.multiple_of(self.column + core * self.half, LANES), self.half)

    def left_local(self):
        return pltpu.make_async_copy(self.refs.at_in, self.refs.at, self.sems.local.at[self.index, 0])

    def right_local(self):
        r, s, i, core = self.refs, self.sems, self.index, self.place.core
        source = r.source.at[:, self.columns(core)]
        return pltpu.make_async_copy(source, r.g.at[:ROWS], s.local.at[i, 1])

    def right_far(self):
        r, s, i, core = self.refs, self.sems, self.index, self.place.core
        source = r.source.at[:, self.columns(1 - core)]
        return remote(source, r.g.at[ROWS:], s.ex_send.at[i, 1], s.ex_recv.at[i, 1], self.place.partner)

    def lefts(self):
        self.left_local().start()

    def rights(self):
        self.right_far().start()
        self.right_local().start()

    def right_local_done(self):
        if not self.local_done:
            self.right_local().wait()
            self.local_done = True

    def rights_sent(self):
        self.right_local_done()
        self.right_far().wait_send()

    def loaded(self):
        self.right_far().wait_recv()
        if not self.left_done:
            self.left_local().wait()
        self.right_local_done()

    def span(self, part):
        return self.spans[part]

    def copy(self, part, stage, step):
        r, s, i = self.refs, self.sems, self.index
        low, high = self.span(part)
        here = slice(self.first_unit + low, self.first_unit + high)
        device, slot = self.place.along(ORDERS[part][stage], step)
        if stage == 1:
            source = r.r1.at[0, here, slot]
            target = r.r2.at[step - 1, here]
        else:
            source = r.r2.at[0, here, slot]
            target = r.r3.at[step - 1, here]
        return remote(
            source, target, s.send.at[i, part, stage, step - 1], s.recv.at[i, part, stage, step - 1], device
        )

    def left_block(self, part, slot, group):
        at = self.refs.at
        rows = slice(group * 16, group * 16 + 16)
        if part == 0:
            blocks = [at[y // 2, :, y % 2, slot, rows] for y in range(4)]
        elif part == 1:
            blocks = [at[slot // 2, :, slot % 2, :, rows]]
        else:
            blocks = [at[:, slot, :, x, rows] for x in range(4)]
        blocks = [block.reshape(-1, block.shape[-1]) for block in blocks]
        return blocks[0] if len(blocks) == 1 else jnp.concatenate(blocks, axis=0)

    def products(self, part, slot, emit):
        unit = self.spans[part][0]
        for group, low, high in self.blocks[part]:
            left = self.left_block(part, slot, group)
            for tile in range(low, high, 2):
                width = min(2, high - tile)
                value = dot(left, self.refs.g[:, tile * LANES : (tile + width) * LANES])
                for i in range(width):
                    emit(unit, value[:, i * LANES : (i + 1) * LANES].reshape(4, 4, 16, LANES))
                    unit += 1

    def relay(self, part, way):
        r, s, i = self.refs, self.sems, self.index
        low, high = self.span(part)
        here = slice(self.first_unit + low, self.first_unit + high)
        half = slice(way * 2, way * 2 + 2)
        device = self.place.along(ORDERS[part][0], 3 if way else 1)[0]
        source = r.s1.at[0, self.send_unit + low : self.send_unit + high, half]
        target = r.r1.at[2, here, half]
        return remote(source, target, s.send.at[i, part, 0, way], s.recv.at[i, part, 0, way], device)

    def direct(self, part, way):
        r, s, i = self.refs, self.sems, self.index
        low, high = self.span(part)
        here = slice(self.first_unit + low, self.first_unit + high)
        device = self.place.along(ORDERS[part][0], 3 if way else 1)[0]
        source = r.s1.at[1 + way, self.send_unit + low : self.send_unit + high]
        target = r.r1.at[way, here]
        return remote(source, target, s.send.at[i, part, 0, 2 + way], s.recv.at[i, part, 0, 2 + way], device)

    def whole(self, part, step):
        r, s, i = self.refs, self.sems, self.index
        low, high = self.span(part)
        here = slice(self.first_unit + low, self.first_unit + high)
        at = (1, 0, 2)[step - 1]
        source = r.s1.at[at, self.send_unit + low : self.send_unit + high]
        target = r.r1.at[step - 1, here]
        device = self.place.along(ORDERS[part][0], step)[0]
        return remote(source, target, s.send.at[i, part, 0, step], s.recv.at[i, part, 0, step], device)

    def first(self, parts=ALL):
        r = self.refs
        for part in parts:
            if part in self.whole_parts:
                for step in (1, 3, 2):
                    slot = self.place.along(ORDERS[part][0], step)[1]

                    def keep(unit, value, step=step):
                        r.s1[(1, 0, 2)[step - 1], self.send_unit + unit] = value.astype(BF16)

                    self.products(part, slot, keep)
                    self.whole(part, step).start()
                continue
            slot = self.place.along(ORDERS[part][0], 2)[1]

            def emit(unit, value):
                r.s1[0, self.send_unit + unit] = value.astype(BF16)

            self.products(part, slot, emit)
            for way in range(2):
                self.relay(part, way).start()

    def pass_on(self, parts=ALL):
        r = self.refs
        for part in parts:
            if part in self.whole_parts:
                continue
            for way in range(2):
                self.relay(part, way).wait_recv()
                slot = self.place.along(ORDERS[part][0], 3 if way else 1)[1]

                def emit(unit, value, way=way):
                    at = self.first_unit + unit
                    for half in range(2):
                        some = slice(half * 2, half * 2 + 2)
                        one = value[some]
                        if half == way:
                            one = one + r.r1[2, at, some].astype(F32)
                        r.s1[1 + way, self.send_unit + unit, some] = one.astype(BF16)

                self.products(part, slot, emit)
                self.direct(part, way).start()

    def relay_sent(self):
        for part in range(3):
            if part in self.whole_parts:
                self.whole(part, 2).wait_send()
                continue
            for way in range(2):
                self.relay(part, way).wait_send()

    def direct_sent(self):
        for part in range(3):
            for way in range(2):
                if part in self.whole_parts:
                    self.whole(part, 3 if way else 1).wait_send()
                else:
                    self.direct(part, way).wait_send()

    def second(self, parts=ALL):
        r = self.refs
        for part in parts:
            slot = self.place.along(ORDERS[part][0], 0)[1]
            terms = 2
            if part in self.whole_parts:
                terms = 3
                for step in (1, 2, 3):
                    self.whole(part, step).wait_recv()
            else:
                for way in range(2):
                    self.direct(part, way).wait_recv()

            def emit(unit, value, terms=terms):
                at = self.first_unit + unit
                for i in range(terms):
                    value = value + r.r1[i, at].astype(F32)
                r.r1[0, at] = value.astype(BF16)

            self.products(part, slot, emit)
            for step in (1, 2, 3):
                self.copy(part, 1, step).start()

    def third(self, parts=ALL):
        r = self.refs
        for part in parts:
            slot = self.place.along(ORDERS[part][1], 0)[1]
            for step in (1, 2, 3):
                self.copy(part, 1, step).wait_recv()

            def one(unit, carry, slot=slot):
                value = r.r1[0, unit, slot].astype(F32)
                for i in range(3):
                    value = value + r.r2[i, unit].astype(F32)
                r.r2[0, unit] = value.astype(BF16)
                return carry

            low, high = self.span(part)
            lax.fori_loop(self.first_unit + low, self.first_unit + high, one, 0)
            for step in (1, 2, 3):
                self.copy(part, 2, step).start()

    def mine(self):
        return self.place.y_hi * 4 + self.place.x

    def gather_copy(self, y_hi, x, slot):
        r, s, i, place = self.refs, self.sems, self.index, self.place
        target = r.out.at[slot // 4, slot % 4, :, self.columns(place.core)]
        return remote(
            r.piece.at[place.y_hi], target, s.ag_send.at[i, y_hi * 4 + x], s.ag_recv.at[i, slot],
            place.device(y_hi=y_hi, x=x),
        )

    def twin_copy(self):
        r, s, i, place = self.refs, self.sems, self.index, self.place
        block = r.piece.at[place.y_hi]
        return remote(block, block, s.ag_send.at[i, 0], s.ag_recv.at[i, 0], place.device(y_hi=1 - place.y_hi))

    def line_copy(self, step):
        r, s, i, place = self.refs, self.sems, self.index, self.place
        target = r.out.at[:, place.x, :, self.columns(place.core)]
        device = place.device(x=(place.x + step) % 4)
        return remote(r.piece, target, s.ag_send.at[i, step], s.ag_recv.at[i, step], device)

    def own_copy(self):
        place, i, piece = self.place, self.index, self.refs.piece
        columns = self.columns(place.core)
        if self.straight:
            target = self.refs.out.at[place.y_hi, place.x, :, columns]
            return pltpu.make_async_copy(piece.at[place.y_hi], target, self.sems.local.at[i, 2])
        return pltpu.make_async_copy(piece, self.refs.out.at[:, place.x, :, columns], self.sems.local.at[i, 2])

    def others(self):
        place = self.place
        for y_step in (0, 1):
            y_hi = (place.y_hi + y_step) % 2
            for x_step in range(4):
                if y_step or x_step:
                    yield y_hi, (place.x + x_step) % 4

    def fourth(self, parts=ALL):
        r = self.refs
        for part in parts:
            slot = self.place.along(ORDERS[part][2], 0)[1]
            for step in (1, 2, 3):
                self.copy(part, 2, step).wait_recv()
            for cell, (group, tile) in enumerate(self.cells[part]):
                at = self.first_unit + self.spans[part][0] + cell
                value = r.r2[0, at, slot].astype(F32)
                for i in range(3):
                    value = value + r.r3[i, at].astype(F32)
                rows, columns = slice(group * 16, group * 16 + 16), slice(tile * LANES, tile * LANES + LANES)
                r.piece[self.place.y_hi, rows, columns] = value.astype(BF16)
    def gather(self):
        if self.straight:
            self.own_copy().start()
            for y_hi, x in self.others():
                self.gather_copy(y_hi, x, self.mine()).start()
        else:
            self.twin_copy().start()

    def spread(self):
        if not self.straight:
            self.twin_copy().wait_recv()
            self.own_copy().start()
            for step in (1, 2, 3):
                self.line_copy(step).start()

    def cross_copy(self):
        r, s, i, core = self.refs, self.sems, self.index, self.place.core
        block = r.out.at[:, :, :, self.columns(core)]
        return remote(block, block, s.cross.at[i, 0], s.cross.at[i, 1], self.place.partner)

    def fifth(self):
        self.own_copy().wait()
        if self.straight:
            for y_hi, x in self.others():
                self.gather_copy(y_hi, x, y_hi * 4 + x).wait_recv()
        else:
            for step in (1, 2, 3):
                self.line_copy(step).wait_recv()
        self.cross_copy().start()

    def finish(self):
        self.cross_copy().wait()
        if self.straight:
            for y_hi, x in self.others():
                self.gather_copy(y_hi, x, self.mine()).wait_send()
        else:
            self.twin_copy().wait_send()
            for step in (1, 2, 3):
                self.line_copy(step).wait_send()
        for part in range(3):
            for stage in (1, 2):
                for step in (1, 2, 3):
                    self.copy(part, stage, step).wait_send()


GAIN1, SHIFT1, SPATIAL_BIAS, GAIN2, SHIFT2, TEMPORAL_BIAS, GAIN3, SHIFT3, INNER, OUTER = 8, 9, 10, 11, 12, 13, 14, 15, 16, 20


class SmallSums:
    def __init__(self, place, refs, sems):
        self.place, self.refs, self.sems = place, refs, sems

    def share(self, core):
        return slice(None), lanes(core, WIDTH // 2)

    def cross(self):
        r, core = self.refs, self.place.core
        return remote(
            r.sums.at[self.share(1 - core)], r.sums_core, self.sems.at[0, 0, 0], self.sems.at[1, 0, 0],
            self.place.partner,
        )

    def along(self, stage, step):
        device = self.place.along("xyz"[stage], step)[0]
        return remote(
            self.refs.sums_total.at[stage], self.refs.sums_recv.at[stage, step - 1],
            self.sems.at[0, stage + 1, step - 1], self.sems.at[1, stage + 1, step - 1], device,
        )

    def final(self):
        block = self.refs.sums_final.at[self.share(self.place.core)]
        return remote(block, block, self.sems.at[0, 4, 0], self.sems.at[1, 4, 0], self.place.partner)

    def begin(self):
        self.cross().start()

    def step0(self):
        r = self.refs
        self.cross().wait()
        r.sums_total[0] = r.sums[self.share(self.place.core)] + r.sums_core[...]
        for step in (1, 2, 3):
            self.along(0, step).start()

    def advance(self, stage):
        r = self.refs
        value = r.sums_total[stage]
        for step in (1, 2, 3):
            self.along(stage, step).wait_recv()
            value = value + r.sums_recv[stage, step - 1]
        if stage < 2:
            r.sums_total[stage + 1] = value
            for step in (1, 2, 3):
                self.along(stage + 1, step).start()
        else:
            r.sums_final[self.share(self.place.core)] = value
            self.final().start()

    def finish(self, out, sem):
        self.final().wait()
        copy = pltpu.make_async_copy(self.refs.sums_final, out, sem)
        copy.start()
        for stage in range(3):
            for step in (1, 2, 3):
                self.along(stage, step).wait_send()
        copy.wait()


BACK_OUTS = dict(
    big_grad=((128, WIDTH), F32),
    small_grad=((128, WIDTH), F32),
    small_sums=((24, WIDTH), F32),
)
SLOTS = 3
BACK_WORK = dict(
    s1=((3, 32, 4, 4, 16, LANES), BF16),
    r1=((3, 64, 4, 4, 16, LANES), BF16),
    r2=((3, 64, 4, 16, LANES), BF16),
    r3=((3, 64, 16, LANES), BF16),
    tall=((SLOTS, HIDE, WIDTH), BF16),
    broad=((SLOTS, WIDTH, HIDE), BF16),
    slope_in=((SLOTS, ROWS, HIDE), BF16),
    record=((SLOTS, SP_ROWS, LANES), BF16),
    resid=((ROWS, WIDTH), F32),
    grad=((ROWS, WIDTH), F32),
    total=((ROWS, WIDTH), F32),
    low3=((ROWS, WIDTH), BF16),
    low2=((ROWS, WIDTH), BF16),
    low1=((ROWS, WIDTH), BF16),
    hidden_low=((ROWS, HIDDEN), BF16),
    packed=((ROWS, 3 * WIDTH), BF16),
    swap_send=((ROWS, WIDTH), BF16),
    context_back=((ROWS, WIDTH), BF16),
    normed_back=((ROWS, WIDTH), BF16),
    context_grad=((2, 128, WIDTH), BF16),
    far_send=((ROWS, 2 * WIDTH), BF16),
    far_recv=((ROWS, 2 * WIDTH), BF16),
    inner_sums=((PAIRS, HIDE), F32),
    sums=((24, WIDTH), F32),
    sums_core=((24, WIDTH // 2), F32),
    sums_total=((3, 24, WIDTH // 2), F32),
    sums_recv=((3, 3, 24, WIDTH // 2), F32),
    sums_final=((24, WIDTH), F32),
    frame_sums=((8, WIDTH), F32),
    scale=((ROWS, LANES), F32),
    gains=((8, WIDTH), F32),
)


BACK_SEMS = dict(
    local=(7, 3),
    ex_send=(7, 2),
    ex_recv=(7, 2),
    send=(7, 3, 3, 4),
    recv=(7, 3, 3, 4),
    ag_send=(7, 8),
    ag_recv=(7, 8),
    cross=(7, 2),
    ring=(4, SLOTS),
    io=(5,),
    swap=(3, 2, 16),
    far=(2,),
    sums=(2, 5, 3),
)


def backward_kernel(in_keys, saved_keys, weight_keys, *refs):
    refs = list(refs)
    ins = named(in_keys, refs)
    gains = [refs.pop(0) for _ in range(3)]
    lefts = [refs.pop(0) for _ in GRADIENTS]
    saved, weights, outs = named(saved_keys, refs), named(weight_keys, refs), named(BACK_OUTS, refs)
    matrix_outs = [refs.pop(0) for _ in GRADIENTS]
    work = named(BACK_WORK, refs)
    ats = [refs.pop(0) for _ in GRADIENTS]
    gs, pieces = ([refs.pop(0) for _ in MATRICES] for _ in range(2))
    sems = named(BACK_SEMS, refs)
    ring_sems, io_sems, swap_sems, far_sems, sum_sems = sems.ring, sems.io, sems.swap, sems.far, sems.sums
    place = Place()
    frame = place.ta // 2
    sources = (work.low3, work.hidden_low, work.low2, work.packed, work.low1, work.packed, work.packed)
    reductions = []
    for i, (_, _, _, output, _) in enumerate(MATRICES):
        own = Names(at_in=lefts[output], at=ats[output], g=gs[i], piece=pieces[i], out=matrix_outs[output])
        own.source = sources[i]
        own.s1, own.r1, own.r2, own.r3 = work.s1, work.r1, work.r2, work.r3
        reductions.append(Reduction(place, i, own, sems))
    fout, fin, tout, tqkv, sout, sq, skv = reductions
    skv.left_done = True
    small = SmallSums(place, work, sum_sems)

    def tall(source, base, index):
        slot = (base + index) % SLOTS
        rows = pl.ds(pl.multiple_of(index * HIDE, HIDE), HIDE)
        return pltpu.make_async_copy(source.at[rows], work.tall.at[slot], ring_sems.at[0, slot])

    def broad(source, base, index):
        slot = (base + index) % SLOTS
        return pltpu.make_async_copy(
            source.at[:, lanes(index, HIDE)], work.broad.at[slot], ring_sems.at[1, slot]
        )

    def slope(base, index):
        slot = (base + index) % SLOTS
        return pltpu.make_async_copy(saved.slope.at[index], work.slope_in.at[slot], ring_sems.at[2, slot])

    def record(source, base, index):
        slot = (base + index) % SLOTS
        return pltpu.make_async_copy(
            source.at[index], work.record.at[slot, pl.ds(0, source.shape[1])], ring_sems.at[3, slot]
        )

    def open_stream(maker, count):
        for index in range(min(SLOTS, count)):
            maker(index).start()

    def refill(maker, count, index):
        @pl.when(index + SLOTS < count)
        def _():
            maker(index + SLOTS).start()

    fout_tiles = functools.partial(tall, weights.w_fout, 0)
    tout_tiles = functools.partial(tall, weights.w_tout, 8)
    sout_tiles = functools.partial(tall, weights.w_sout, 10)
    fin_tiles = functools.partial(broad, weights.w_fin, 0)
    tqkv_tiles = functools.partial(broad, weights.w_tqkv, 8)
    sqkv_tiles = functools.partial(broad, weights.w_sqkv, 14)
    slopes = functools.partial(slope, 0)
    temporal_records = functools.partial(record, saved.temporal, 0)
    spatial_records = functools.partial(record, saved.spatial, 8)

    class Kept:
        def __init__(self, normals, scales):
            self.copies = (
                pltpu.make_async_copy(normals, work.resid, io_sems.at[0]),
                pltpu.make_async_copy(scales, work.scale, io_sems.at[4]),
            )
            for copy in self.copies:
                copy.start()

        def wait(self):
            for copy in self.copies:
                copy.wait()

    fout.lefts()
    open_stream(fout_tiles, 8)
    open_stream(slopes, 8)
    open_stream(fin_tiles, 8)
    work.sums[...] = jnp.zeros_like(work.sums)
    for row, gain in enumerate(gains):
        work.gains[row : row + 1] = gain[...].astype(F32).reshape(1, WIDTH)
    greet(place, True)

    grad, total = work.grad, work.total

    def start_rows(step, carry):
        near = pl.ds(pl.multiple_of(step * 16, 16), 16)
        big = ins.big_cot[near].astype(F32)
        little = ins.small_cot[near].astype(F32) * ins.live[step // 2].astype(F32)
        merged = interleave(big, little)
        rows = pl.ds(pl.multiple_of(step * 32, 32), 32)
        grad[rows] = merged
        work.low3[rows] = merged.astype(BF16)
        total[rows] = jnp.zeros_like(merged)
        work.sums[OUTER : OUTER + 1] += jnp.sum(merged, axis=0, keepdims=True)
        return carry

    lax.fori_loop(0, 8, start_rows, 0)
    fout.rights()
    fin.lefts()
    kept3 = Kept(saved.normal3, saved.scale3)

    def feed(step, carry):
        slopes(step).wait()
        fout_tiles(step).wait()
        fin_tiles(step).wait()
        slot = step % SLOTS
        down = dot_nt(work.low3[...], work.tall[slot]) * work.slope_in[slot].astype(F32)
        work.inner_sums[pl.ds(step, 1)] = jnp.sum(down, axis=0, keepdims=True)
        low = down.astype(BF16)
        work.hidden_low[:, lanes(step, HIDE)] = low
        for column in range(WIDTH // 256):
            at = slice(column * 256, column * 256 + 256)
            total[:, at] += dot_nt(low, work.broad[slot, at])
        refill(slopes, 8, step)
        refill(fout_tiles, 8, step)
        refill(fin_tiles, 8, step)
        return carry

    lax.fori_loop(0, 2, feed, 0)
    fout.loaded()
    fout.first()
    lax.fori_loop(2, 8, feed, 0)
    fin.rights()
    open_stream(temporal_records, 8)
    for one in (tout, tqkv, sout, sq):
        one.lefts()
    open_stream(tout_tiles, 2)
    open_stream(sout_tiles, 1)
    open_stream(tqkv_tiles, 6)
    for part in range(PAIRS):
        at = part % 2 * HIDE
        work.sums[INNER + part // 2 : INNER + part // 2 + 1, at : at + HIDE] = work.inner_sums[part : part + 1]

    def norm_back(gradient, gain_row, row, low, bias_row):
        gain = work.gains[gain_row : gain_row + 1]

        def one(step, carry):
            rows = rows16(step)
            error = gradient[rows].astype(F32)
            normal, scale = work.resid[rows], work.scale[rows, 0:1]
            scaled = error * gain
            mean_one = jnp.mean(scaled, axis=-1, keepdims=True)
            mean_two = jnp.mean(scaled * normal, axis=-1, keepdims=True)
            value = grad[rows] + (scaled - mean_one - normal * mean_two) * scale
            grad[rows] = value
            if low is not None:
                low[rows] = value.astype(BF16)
            gains = error * normal
            sums = [part[:8] + part[8:] for part in (gains, error, value)]
            return tuple(a + b for a, b in zip(carry, sums))

        zero = jnp.zeros((8, WIDTH), F32)
        sums = lax.fori_loop(0, 16, one, (zero, zero, zero), unroll=2)
        work.sums[row : row + 1] = jnp.sum(sums[0], axis=0, keepdims=True)
        work.sums[row + 1 : row + 2] = jnp.sum(sums[1], axis=0, keepdims=True)
        if bias_row is not None:
            work.sums[bias_row : bias_row + 1] = jnp.sum(sums[2], axis=0, keepdims=True)

    kept3.wait()
    norm_back(total, 2, GAIN3, work.low2, TEMPORAL_BIAS)
    kept2 = Kept(saved.normal2, saved.scale2)
    tout.rights()

    there = [Swap(place, work.swap_send, work.context_back, swap_sems, i, True, HALVES[i]) for i in range(2)]
    for index in range(2):
        tout_tiles(index).wait()
        slot = (8 + index) % SLOTS
        work.swap_send[:, HALVES[index]] = dot_nt(work.low2[...], work.tall[slot]).astype(BF16)
        there[index].start()
    sout_tiles(1).start()
    fout.pass_on(Z)
    fin.loaded()
    fin.first(Z)
    there[0].wait()
    fout.pass_on(XY)
    fin.first(XY)

    low_lanes = half_masks(128)

    def attention_back(probs, keys, values, queries, upstream):
        upstreams = jnp.concatenate(by_head(upstream, low_lanes), axis=0)
        prob = jnp.concatenate(probs, axis=1)
        wide = prob.astype(F32)
        back = dot_nt(values, upstreams)
        delta = jnp.sum(wide * back, axis=0, keepdims=True)
        error = (wide * (back - delta)).astype(BF16)
        key_grad = dot(error, jnp.concatenate(by_head(queries, low_lanes), axis=0))
        value_grad = dot(prob, upstreams)
        query_grad = join_heads(dot_tn(error, keys), low_lanes)
        return query_grad * 0.125, key_grad, value_grad

    def temporal_pair(pair, carry):
        temporal_records(pair).wait()
        slot = pair % SLOTS
        for half in range(2):
            base = half * 128

            def rows(start, half=half):
                return work.record[slot, start + half * 128 : start + half * 128 + 128]

            probs = [work.record[slot, (half * 2 + h) * 128 : (half * 2 + h) * 128 + 128] for h in range(2)]
            upstream = work.context_back[base : base + 128, lanes(pair, LANES)]
            grads = attention_back(probs, rows(TP_KEY), rows(TP_VALUE), rows(TP_QUERY), upstream)
            for i, value in enumerate(grads):
                work.packed[base : base + 128, lanes(pair + i * PAIRS, LANES)] = value.astype(BF16)
        refill(temporal_records, 8, pair)
        return carry

    lax.fori_loop(0, PAIRS // 2, temporal_pair, 0, unroll=2)
    there[1].wait()
    lax.fori_loop(PAIRS // 2, PAIRS, temporal_pair, 0, unroll=2)
    open_stream(spatial_records, 8)
    tqkv.rights()

    def project_back(maker, base, start, stop):
        def one(step, carry):
            maker(step).wait()
            slot = (base + step) % SLOTS
            low = work.packed[:, lanes(step, HIDE)]
            for column in range(WIDTH // 256):
                at = slice(column * 256, column * 256 + 256)
                value = dot_nt(low, work.broad[slot, at])
                total[:, at] += value
            refill(maker, 6, step)
            return carry

        if start == 0:
            total[...] = jnp.zeros_like(total)
        lax.fori_loop(start, stop, one, 0)

    project_back(tqkv_tiles, 8, 0, 3)
    fin.pass_on(Z)
    fout.relay_sent()
    tout.loaded()
    tout.first()
    tqkv.loaded()
    tqkv.first()
    project_back(tqkv_tiles, 8, 3, 6)
    open_stream(sqkv_tiles, 6)
    for one in there:
        one.sent()
    work.swap_send[...] = total[...].astype(BF16)
    back = Swap(place, work.swap_send, work.normed_back, swap_sems, 2, False)
    back.start()
    fout.second((1,))
    fout.direct_sent()
    back.wait()
    tout.pass_on()
    tqkv.pass_on()
    fin.pass_on(XY)
    fout.second((0, 2))

    kept2.wait()
    norm_back(work.normed_back, 1, GAIN2, work.low1, SPATIAL_BIAS)
    kept1 = Kept(saved.normal1, saved.scale1)
    sout.rights()
    for index in range(2):
        sout_tiles(index).wait()
        slot = (10 + index) % SLOTS
        at = slice(index * HIDE, index * HIDE + HIDE)
        value = dot_nt(work.low1[...], work.tall[slot])
        for which in range(2):
            work.context_grad[which, :, at] = family(value, which).astype(BF16)
    tqkv.rights_sent()

    def spatial_pair(pair, carry):
        spatial_records(pair).wait()
        slot = (8 + pair) % SLOTS
        all_grads = []
        for which in range(2):

            def rows(start, count, which=which):
                return work.record[slot, start + which * count : start + which * count + count]

            probs = [work.record[slot, (which * 2 + h) * 256 : (which * 2 + h) * 256 + 256] for h in range(2)]
            upstream = work.context_grad[which, :, lanes(pair, LANES)]
            all_grads.append(
                attention_back(
                    probs, rows(SP_KEY, 256), rows(SP_VALUE, 256), rows(SP_QUERY, 128), upstream
                )
            )
        for i in range(3):
            value = interleave(all_grads[0][i][:128], all_grads[1][i][:128])
            work.packed[:, lanes(pair + i * PAIRS, LANES)] = value.astype(BF16)
        for i in (1, 2):
            value = interleave(all_grads[0][i][128:], all_grads[1][i][128:])
            work.far_send[:, lanes(pair + (i - 1) * PAIRS, LANES)] = value.astype(BF16)
        refill(spatial_records, 8, pair)
        return carry

    lax.fori_loop(0, PAIRS // 2, spatial_pair, 0, unroll=2)
    fin.second(Z)
    lax.fori_loop(PAIRS // 2, PAIRS, spatial_pair, 0, unroll=2)
    far = remote(work.far_send, work.far_recv, far_sems.at[0], far_sems.at[1], place.partner)
    far.start()
    sq.rights()
    fin.relay_sent()
    sout.loaded()
    sout.first()
    sq.loaded()
    sq.first()
    fin.second(XY)
    far.wait()

    def join(step, carry):
        rows = rows16(step)
        value = work.packed[rows, WIDTH:].astype(F32) + work.far_recv[rows].astype(F32)
        work.packed[rows, WIDTH:] = value.astype(BF16)
        return carry

    lax.fori_loop(0, 16, join, 0)
    skv.rights()
    project_back(sqkv_tiles, 14, 0, 2)
    skv.loaded()
    skv.first()
    fout.third()
    fin.direct_sent()
    sout.pass_on()
    sq.pass_on()
    project_back(sqkv_tiles, 14, 2, 4)
    skv.pass_on()
    project_back(sqkv_tiles, 14, 4, 6)
    tout.second()
    tqkv.second()
    fout.fourth()
    fout.gather()
    kept1.wait()
    norm_back(total, 0, GAIN1, None, None)

    def finish_rows(step, carry):
        value = grad[pl.ds(pl.multiple_of(step * 32, 32), 32)]
        big, little = family(value, 0), family(value, 1)
        near = pl.ds(pl.multiple_of(step * 16, 16), 16)
        total[near] = big
        total[pl.ds(pl.multiple_of(128 + step * 16, 16), 16)] = little
        work.frame_sums[0:1] += jnp.sum(big, axis=0, keepdims=True)
        work.frame_sums[pl.ds(1 + step // 2, 1)] += jnp.sum(little, axis=0, keepdims=True)
        return carry

    work.frame_sums[...] = jnp.zeros_like(work.frame_sums)
    lax.fori_loop(0, 8, finish_rows, 0)
    out_copies = [
        pltpu.make_async_copy(total.at[:128], outs.big_grad, io_sems.at[1]),
        pltpu.make_async_copy(total.at[128:], outs.small_grad, io_sems.at[2]),
    ]
    for copy in out_copies:
        copy.start()
    table, at_row = jnp.zeros((8, WIDTH), F32), lax.broadcasted_iota(jnp.int32, (8, WIDTH), 0)
    for i in range(5):
        action = ins.big_actions[0, frame] if i == 0 else ins.small_actions[i - 1, frame]
        table = table + jnp.where(at_row == action, work.frame_sums[i : i + 1], 0.0)
    work.sums[0:8] = table
    small.begin()
    fin.third()
    sq.second()
    sout.second()
    small.step0()
    skv.second()
    fout.spread()
    tout.third()
    tqkv.third()
    small.advance(0)
    sq.third()
    sout.third()
    skv.third()
    fin.fourth()
    fin.gather()
    small.advance(1)
    sq.fourth()
    sq.gather()
    sout.fourth()
    sout.gather()
    skv.fourth()
    skv.gather()
    tout.fourth()
    tout.gather()
    tqkv.fourth()
    tqkv.gather()
    fout.fifth()
    fin.spread()
    small.advance(2)
    sq.fifth()
    sout.fifth()
    tout.spread()
    tqkv.spread()
    skv.fifth()
    fin.fifth()
    tout.fifth()
    tqkv.fifth()
    small.finish(outs.small_sums, io_sems.at[3])
    for one in reductions:
        one.finish()
    for one in (tout, tqkv, sout, sq, skv):
        one.relay_sent()
        one.direct_sent()
    for one in (fout, fin, tout, sout, sq, skv):
        one.rights_sent()
    back.sent()
    for copy in out_copies:
        copy.wait()


def backward(ins, scalars, gains, lefts, saved, weights):
    sem = pltpu.SemaphoreType.DMA
    count = len(GRADIENTS)
    work = [pltpu.VMEM(shape, dtype) for shape, dtype in BACK_WORK.values()]
    work += [pltpu.VMEM((2, 4, 2, 4, k // 64, 2 * ROWS), BF16) for k, _ in GRADIENTS]
    work += [pltpu.VMEM((2 * ROWS, n // 2), BF16) for _, n, _, _, _ in MATRICES]
    work += [pltpu.VMEM((2, k // 64, n // 2), BF16) for k, n, _, _, _ in MATRICES]
    work += [sem(shape) for shape in BACK_SEMS.values()]
    shapes = list(BACK_OUTS.values()) + [((2, 4, k // 64, n), BF16) for k, n in GRADIENTS]
    in_keys, saved_keys, weight_keys = tuple(vars(ins)) + tuple(vars(scalars)), tuple(vars(saved)), tuple(vars(weights))
    return pl.pallas_call(
        functools.partial(backward_kernel, in_keys, saved_keys, weight_keys),
        out_shape=[jax.ShapeDtypeStruct(shape, dtype) for shape, dtype in shapes],
        in_specs=[VMEM] * len(vars(ins))
        + [SMEM] * len(vars(scalars))
        + [VMEM] * len(gains)
        + [ANY] * (count + len(saved_keys) + len(weight_keys)),
        out_specs=[ANY] * len(shapes),
        scratch_shapes=work,
        compiler_params=pltpu.CompilerParams(
            collective_id=2, has_side_effects=True, vmem_limit_bytes=63 * 2**20
        ),
        cost_estimate=pl.CostEstimate(flops=18 * 10**9, bytes_accessed=80 * 2**20, transcendentals=0),
        name="layer_backward",
    )(
        *vars(ins).values(),
        *vars(scalars).values(),
        *gains,
        *[left.reshape(2, 4, 2, 4, k // 64, 2 * ROWS) for left, (k, _) in zip(lefts, GRADIENTS)],
        *vars(saved).values(),
        *vars(weights).values(),
    )


SUM_VECTORS = (
    (GAIN1, 1),
    (SHIFT1, 1),
    (SPATIAL_BIAS, 1),
    (GAIN2, 1),
    (SHIFT2, 1),
    (TEMPORAL_BIAS, 1),
    (GAIN3, 1),
    (SHIFT3, 1),
    (INNER, 4),
    (OUTER, 1),
)


def widen_kernel(*refs):
    refs = list(refs)
    count, passed = len(GRADIENTS), 4
    narrow = [refs.pop(0) for _ in range(count)]
    plain = [refs.pop(0) for _ in range(passed)]
    sums = refs.pop(0)
    wide = [refs.pop(0) for _ in range(count)]
    plain_out = [refs.pop(0) for _ in range(passed)]
    table, vectors = refs.pop(0), [refs.pop(0) for _ in SUM_VECTORS]
    narrow_in, wide_out = refs[:count], refs[count : 2 * count]
    between, sems = refs[2 * count : 2 * count + passed], refs[2 * count + passed]
    loads = [pltpu.make_async_copy(narrow[i], narrow_in[i], sems.at[0, i]) for i in range(count)]
    stores = [pltpu.make_async_copy(wide_out[i], wide[i], sems.at[1, i]) for i in range(count)]
    reads = [pltpu.make_async_copy(plain[i], between[i], sems.at[2, i]) for i in range(passed)]
    moves = [pltpu.make_async_copy(between[i], plain_out[i], sems.at[3, i]) for i in range(passed)]
    for copy in loads + reads:
        copy.start()
    table[...] = sums[0:8]
    for (row, rows), vector in zip(SUM_VECTORS, vectors):
        for i in range(rows):
            vector[i * WIDTH : (i + 1) * WIDTH] = sums[row + i]
    for i in range(count):
        loads[i].wait()

        def one(step, carry, i=i):
            wide_out[i][rows16(step)] = narrow_in[i][rows16(step)].astype(F32)
            return carry

        lax.fori_loop(0, narrow_in[i].shape[0] // 16, one, 0, unroll=2)
        stores[i].start()
    for read, move in zip(reads, moves):
        read.wait()
        move.start()
    for copy in stores + moves:
        copy.wait()


def widen(matrices, plain, sums):
    count = len(matrices)
    vectors = [jax.ShapeDtypeStruct((rows * WIDTH,), F32) for _, rows in SUM_VECTORS]
    shapes = [jax.ShapeDtypeStruct(one.shape, F32) for one in matrices]
    scratch = [pltpu.VMEM(one.shape, BF16) for one in matrices] + [pltpu.VMEM(one.shape, F32) for one in matrices]
    scratch += [pltpu.VMEM(one.shape, one.dtype) for one in plain]
    results = pl.pallas_call(
        widen_kernel,
        out_shape=shapes
        + [jax.ShapeDtypeStruct(one.shape, one.dtype) for one in plain]
        + [jax.ShapeDtypeStruct((8, WIDTH), F32)]
        + vectors,
        in_specs=[ANY] * (count + len(plain)) + [VMEM],
        out_specs=[ANY] * (count + len(plain)) + [VMEM] * (1 + len(vectors)),
        scratch_shapes=scratch + [pltpu.SemaphoreType.DMA((4, count))],
        compiler_params=pltpu.CompilerParams(vmem_limit_bytes=62 * 2**20),
        cost_estimate=pl.CostEstimate(flops=0, bytes_accessed=14 * 2**20, transcendentals=0),
        name="widen",
    )(*matrices, *plain, sums)
    results = list(results)
    wide = [results.pop(0) for _ in range(count)]
    passed = [results.pop(0) for _ in plain]
    return wide, passed, results


def body(
    big_tokens,
    small_tokens,
    big_actions,
    small_actions,
    big_order,
    small_order,
    small_live,
    action_table,
    norm1_gain,
    norm1_bias,
    spatial_qkv,
    spatial_out,
    spatial_out_bias,
    norm2_gain,
    norm2_bias,
    temporal_qkv,
    temporal_out,
    temporal_out_bias,
    norm3_gain,
    norm3_bias,
    ffn_in,
    ffn_in_bias,
    ffn_out,
    ffn_out_bias,
    big_cotangent,
    small_cotangent,
):
    scalars = Names(
        big_actions=big_actions,
        small_actions=small_actions,
        big_order=big_order,
        small_order=small_order,
        live=small_live,
    )
    vectors = (
        norm1_gain,
        norm1_bias,
        spatial_out_bias,
        norm2_gain,
        norm2_bias,
        temporal_out_bias,
        norm3_gain,
        norm3_bias,
        ffn_out_bias,
    )
    weights = Names(
        w_sqkv=spatial_qkv,
        w_sout=spatial_out,
        w_tqkv=temporal_qkv,
        w_tout=temporal_out,
        w_fin=ffn_in,
        w_fout=ffn_out,
    )
    saved = forward(
        Names(
            big=big_tokens.reshape(128, WIDTH),
            small=small_tokens.reshape(128, WIDTH),
            table=action_table,
            inner_bias=ffn_in_bias,
        ),
        scalars,
        vectors,
        weights,
    )
    big_grad, small_grad, sums, *matrices = backward(
        Names(big_cot=big_cotangent.reshape(128, WIDTH), small_cot=small_cotangent.reshape(128, WIDTH)),
        Names(big_actions=big_actions, small_actions=small_actions, live=small_live),
        (norm1_gain, norm2_gain, norm3_gain),
        (saved.activated_t, saved.normed3_t, saved.context2_t, saved.normed2_t, saved.context1_t, saved.normed1_t),
        Names(
            normal1=saved.normal1,
            normal2=saved.normal2,
            normal3=saved.normal3,
            scale1=saved.scale1,
            scale2=saved.scale2,
            scale3=saved.scale3,
            spatial=saved.spatial,
            temporal=saved.temporal,
            slope=saved.slope,
        ),
        weights,
    )
    matrices = [one.reshape(-1, one.shape[-1]) for one in matrices]
    matrices, passed, small = widen(matrices, (saved.big_out, saved.small_out, big_grad, small_grad), sums)
    g_fout, g_fin, g_tout, g_tqkv, g_sout, g_sqkv = matrices
    table, gain1, shift1, bias_s, gain2, shift2, bias_t, gain3, shift3, bias_in, bias_out = small
    return (
        passed[0].reshape(1, 128, WIDTH),
        passed[1].reshape(4, 32, WIDTH),
        passed[2].reshape(1, 128, WIDTH),
        passed[3].reshape(4, 32, WIDTH),
        table,
        gain1,
        shift1,
        g_sqkv,
        g_sout,
        bias_s,
        gain2,
        shift2,
        g_tqkv,
        g_tout,
        bias_t,
        gain3,
        shift3,
        g_fin,
        bias_in,
        g_fout,
        bias_out,
    )


def solution(mesh):
    spread, by_col = P("col", "ta", None), P("col", None)
    return jax.shard_map(
        body,
        mesh=mesh,
        in_specs=(spread, spread, by_col, by_col, by_col, by_col, P("col")) + (P(),) * 17 + (spread, spread),
        out_specs=(spread,) * 4
        + (P(),) * 3
        + (by_col, by_col, P(), P(), P(), by_col, by_col, P(), P(), P(), by_col, P(), by_col, P()),
        check_vma=False,
    )
```

```python
import functools
from types import SimpleNamespace as Names

import jax
import jax.numpy as jnp
from jax import lax
from jax.experimental import pallas as pl
from jax.experimental.pallas import tpu as pltpu
from jax.sharding import PartitionSpec as P

HEAD_DIM = 64
EPSILON = 1e-05
MASKED_SCORE = -1e30
MESH = pl.DeviceIdType.MESH
ANY = pl.BlockSpec(memory_space=pl.ANY)
VMEM = pl.BlockSpec(memory_space=pltpu.VMEM)
SMEM = pl.BlockSpec(memory_space=pltpu.SMEM)
LANES = 128
F32, BF16 = jnp.float32, jnp.bfloat16
ROWS, WIDTH, HIDDEN = 256, 1024, 4096
PAIRS = WIDTH // LANES
HIDE = 512

SP_KEY, SP_VALUE, SP_QUERY, SP_ROWS = 1024, 1536, 2048, 2304
TP_KEY, TP_VALUE, TP_QUERY, TP_ROWS = 512, 768, 1024, 1280

ORDERS = (("x", "y", "z"), ("y", "z", "x"), ("z", "x", "y"))
MATRICES = (
    (HIDDEN, WIDTH, None, 0, 0),
    (WIDTH, HIDDEN, (4, 6, 6), 1, 0),
    (WIDTH, WIDTH, (1, 1, 2), 2, 0),
    (WIDTH, 3 * WIDTH, (4, 4, 4), 3, 0),
    (WIDTH, WIDTH, (1, 1, 2), 4, 0),
    (WIDTH, WIDTH, (1, 1, 2), 5, 0),
    (WIDTH, 2 * WIDTH, (3, 3, 2), 5, WIDTH),
)
GRADIENTS = (
    (HIDDEN, WIDTH),
    (WIDTH, HIDDEN),
    (WIDTH, WIDTH),
    (WIDTH, 3 * WIDTH),
    (WIDTH, WIDTH),
    (WIDTH, 3 * WIDTH),
)
ALL, XY, Z = (0, 1, 2), (0, 1), (2,)
SEND_UNITS = (0, 16, 12, 0, 28, 16, 20)


class Place:
    def __init__(self):
        ta, col = lax.axis_index("ta"), lax.axis_index("col")
        self.ta, self.col = ta, col
        self.y_hi, self.x, self.core = ta // 8, (ta // 2) % 4, ta % 2
        self.y_lo, self.z = col // 4, col % 4
        self.y = self.y_hi * 2 + self.y_lo
        self.partner = self.device(core=1 - self.core)

    def device(self, y_hi=None, x=None, core=None, y_lo=None, z=None):
        y_hi = self.y_hi if y_hi is None else y_hi
        x = self.x if x is None else x
        core = self.core if core is None else core
        y_lo = self.y_lo if y_lo is None else y_lo
        z = self.z if z is None else z
        return (y_hi * 8 + x * 2 + core, y_lo * 4 + z)

    def along(self, axis, step):
        if axis == "x":
            at = (self.x + step) % 4
            return self.device(x=at), at
        if axis == "z":
            at = (self.z + step) % 4
            return self.device(z=at), at
        at = (self.y + step) % 4
        return self.device(y_hi=at // 2, y_lo=at % 2), (at % 2) * 2 + at // 2

    def fellow(self, step):
        ta = (self.ta + step) % 16
        return (ta, self.col), ta


def greet(place, whole):
    barrier = pltpu.get_barrier_semaphore()

    def one(step, carry):
        pl.semaphore_signal(barrier, inc=1, device_id=place.fellow(step)[0], device_id_type=MESH)
        return carry

    lax.fori_loop(1, 16, one, 0)
    count = 15
    if whole:
        for axis, step in (("y", 1), ("y", 3), ("z", 1), ("z", 2), ("z", 3)):
            pl.semaphore_signal(barrier, inc=1, device_id=place.along(axis, step)[0], device_id_type=MESH)
            count += 1
    pl.semaphore_wait(barrier, count)


def remote(source, target, send, recv, device):
    return pltpu.make_async_remote_copy(source, target, send, recv, device_id=device, device_id_type=MESH)


def dot(left, right):
    return jnp.dot(left, right, preferred_element_type=F32)


def dot_nt(left, right):
    return lax.dot_general(left, right, (((1,), (1,)), ((), ())), preferred_element_type=F32)


def dot_tn(left, right):
    return lax.dot_general(left, right, (((0,), (0,)), ((), ())), preferred_element_type=F32)


def rows16(step):
    return pl.ds(pl.multiple_of(step * 16, 16), 16)


def lanes(step, width):
    return pl.ds(pl.multiple_of(step * width, width), width)


def interleave(big, small):
    width = big.shape[-1]
    pair = [one.reshape(-1, 1, 8, width) for one in (big, small)]
    return jnp.concatenate(pair, axis=1).reshape(-1, width)


def family(rows, which):
    width = rows.shape[-1]
    return rows.reshape(-1, 2, 8, width)[:, which].reshape(-1, width)


def half_masks(rows):
    lane = lax.broadcasted_iota(jnp.int32, (rows, LANES), 1)
    return lane < HEAD_DIM


def by_head(value, low):
    zero = jnp.zeros_like(value)
    return jnp.where(low, value, zero), jnp.where(low, zero, value)


def join_heads(value, low):
    return jnp.where(low, value[:128], value[128:])


def statistics(rows):
    mean = jnp.mean(rows, axis=-1, keepdims=True)
    centered = rows - mean
    variance = jnp.mean(centered * centered, axis=-1, keepdims=True)
    scale = lax.rsqrt(variance + EPSILON)
    return centered * scale, scale


def norm_forward(source, gain, shift, target, normals, scales, after=None):
    def one(step, carry):
        rows = rows16(step)
        normal, scale = statistics(source[rows])
        target[rows] = (normal * gain + shift).astype(BF16)
        normals[rows] = normal
        scales[rows] = jnp.broadcast_to(scale, (16, LANES))
        if after is not None:
            after(step)
        return carry

    lax.fori_loop(0, 16, one, 0, unroll=4)


def transpose_into(source, target):
    def one(step, carry):
        target[step] = source[:, lanes(step, LANES)].T
        return carry

    lax.fori_loop(0, PAIRS, one, 0, unroll=4)


class Swap:
    def __init__(self, place, send, recv, sems, index, to_positions, columns=slice(0, WIDTH)):
        self.place, self.send, self.recv, self.sems, self.index = place, send, recv, sems, index
        self.to_positions, self.columns = to_positions, columns

    def rows(self, ta):
        frames = rows16(ta)
        positions = rows16((ta % 2) * 8 + ta // 2)
        return (frames, positions) if self.to_positions else (positions, frames)

    def copy(self, step):
        device, ta = self.place.fellow(step)
        source = self.send.at[self.rows(ta)[0], self.columns]
        target = self.recv.at[self.rows(self.place.ta)[1], self.columns]
        return remote(source, target, self.sems.at[self.index, 0, step], self.sems.at[self.index, 1, step], device)

    def own(self):
        rows = self.rows(self.place.ta)
        source, target = self.send.at[rows[0], self.columns], self.recv.at[rows[1], self.columns]
        return pltpu.make_async_copy(source, target, self.sems.at[self.index, 0, 0])

    def start_block(self, ta):
        step = (ta - self.place.ta + 16) % 16

        @pl.when(step > 0)
        def _():
            self.copy(step).start()

        @pl.when(step == 0)
        def _():
            self.own().start()

    def start(self):
        def one(step, carry):
            self.copy(step).start()
            return carry

        lax.fori_loop(1, 16, one, 0)
        self.own().start()

    def wait(self):
        def one(step, carry):
            self.copy(step).wait_recv()
            return carry

        self.own().wait()
        lax.fori_loop(1, 16, one, 0)

    def sent(self):
        def one(step, carry):
            self.copy(step).wait_send()
            return carry

        lax.fori_loop(1, 16, one, 0)


HALVES = (slice(0, WIDTH // 2), slice(WIDTH // 2, WIDTH))


FORWARD_OUTS = dict(
    big_out=((128, WIDTH), BF16),
    small_out=((128, WIDTH), BF16),
    normal1=((ROWS, WIDTH), F32),
    normal2=((ROWS, WIDTH), F32),
    normal3=((ROWS, WIDTH), F32),
    scale1=((ROWS, LANES), F32),
    scale2=((ROWS, LANES), F32),
    scale3=((ROWS, LANES), F32),
    spatial=((PAIRS, SP_ROWS, LANES), BF16),
    temporal=((PAIRS, TP_ROWS, LANES), BF16),
    slope=((PAIRS, ROWS, HIDE), BF16),
)
FORWARD_LEFTS = dict(
    activated_t=((PAIRS, HIDE, ROWS), BF16),
    normed3_t=((PAIRS, LANES, ROWS), BF16),
    context2_t=((PAIRS, LANES, ROWS), BF16),
    normed2_t=((PAIRS, LANES, ROWS), BF16),
    context1_t=((PAIRS, LANES, ROWS), BF16),
    normed1_t=((PAIRS, LANES, ROWS), BF16),
)
FORWARD_WORK = dict(
    w_sqkv=((WIDTH, 3 * WIDTH), BF16),
    w_sout=((WIDTH, WIDTH), BF16),
    w_tqkv=((WIDTH, 3 * WIDTH), BF16),
    w_tout=((WIDTH, WIDTH), BF16),
    w_fin=((WIDTH, HIDDEN), BF16),
    w_fout=((HIDDEN, WIDTH), BF16),
    normed=((ROWS, WIDTH), BF16),
    context=((ROWS, WIDTH), BF16),
    arranged=((ROWS, WIDTH), BF16),
    context_send=((ROWS, WIDTH), BF16),
    context_back=((ROWS, WIDTH), BF16),
    normed3=((ROWS, WIDTH), BF16),
    total=((ROWS, WIDTH), F32),
    hidden=((2, ROWS, HIDE), F32),
    params=((16, WIDTH), F32),
    inner_bias=((PAIRS, HIDE), F32),
    table=((8, WIDTH), F32),
)


def named(keys, refs):
    return Names(**{key: refs.pop(0) for key in keys})


def forward_kernel(in_keys, vector_count, weight_keys, *refs):
    refs = list(refs)
    ins = named(in_keys, refs)
    vectors = [refs.pop(0) for _ in range(vector_count)]
    weights = named(weight_keys, refs)
    kept = FORWARD_OUTS | FORWARD_LEFTS
    outs, keep, work = named(kept, refs), named(kept, refs), named(FORWARD_WORK, refs)
    w_sems, out_sems, swap_sems, far_sems, pair_sems, feed_sems = refs
    place = Place()
    params = work.params

    def param(row):
        return params[row : row + 1]

    loads = Names()
    for i, key in enumerate(weight_keys):
        setattr(loads, key, pltpu.make_async_copy(getattr(weights, key), getattr(work, key), w_sems.at[i]))
    loads.w_sqkv.start()
    for row, vector in enumerate(vectors):
        params[row : row + 1] = vector[...].astype(F32).reshape(1, WIDTH)
    for row in range(PAIRS):
        at = slice(row * HIDE, row * HIDE + HIDE)
        work.inner_bias[row : row + 1] = ins.inner_bias[at].astype(F32).reshape(1, HIDE)
    work.table[...] = ins.table[...].astype(F32)
    frame = place.ta // 2
    copies = []

    def save(source, target):
        copy = pltpu.make_async_copy(source, target, out_sems.at[len(copies)])
        copy.start()
        copies.append(copy)

    shared = []

    def share(source, target):
        save(source, target.at[:, :, :ROWS])
        i = len(shared)
        copy = remote(source, target.at[:, :, ROWS:], pair_sems.at[0, i], pair_sems.at[1, i], place.partner)
        copy.start()
        shared.append(copy)

    resid0, resid1, resid2 = keep.normal2, keep.normal3, work.total
    big_row = work.table[pl.ds(ins.big_actions[0, frame], 1)]

    def start_rows(step, carry):
        near = pl.ds(pl.multiple_of(step * 16, 16), 16)
        big = ins.big[near].astype(F32) + big_row
        small = ins.small[near].astype(F32) + work.table[pl.ds(ins.small_actions[step // 2, frame], 1)]
        rows = pl.ds(pl.multiple_of(step * 32, 32), 32)
        merged = interleave(big, small)
        resid0[rows] = merged
        normal, scale = statistics(merged)
        work.normed[rows] = (normal * param(0) + param(1)).astype(BF16)
        keep.normal1[rows] = normal
        keep.scale1[rows] = jnp.broadcast_to(scale, (32, LANES))
        return carry

    lax.fori_loop(0, 8, start_rows, 0)
    save(keep.normal1, outs.normal1)
    save(keep.scale1, outs.scale1)
    greet(place, False)

    spatial = keep.spatial
    loads.w_sqkv.wait()
    for key in weight_keys[1:]:
        getattr(loads, key).start()

    def spatial_project(column, base, per_family, scale):
        def one(step, carry):
            at = column + step
            value = dot(work.normed[...], work.w_sqkv[:, lanes(at, 256)]) * scale
            for which in range(2):
                one_family = family(value, which).astype(BF16)
                rows = pl.ds(base + which * per_family, 128)
                spatial[step * 2, rows] = one_family[:, :LANES]
                spatial[step * 2 + 1, rows] = one_family[:, LANES:]
            return carry

        lax.fori_loop(0, 4, one, 0, unroll=2)

    spatial_project(4, SP_KEY, 256, 1.0)
    spatial_project(8, SP_VALUE, 256, 1.0)
    far = []
    for i, base in enumerate((SP_KEY, SP_KEY + 256, SP_VALUE, SP_VALUE + 256)):
        far.append(
            remote(
                spatial.at[:, pl.ds(base, 128)], spatial.at[:, pl.ds(base + 128, 128)],
                far_sems.at[0, i], far_sems.at[1, i], place.partner,
            )
        )
    for copy in far:
        copy.start()
    spatial_project(0, SP_QUERY, 128, 0.125)
    transpose_into(work.normed, keep.normed1_t)
    share(keep.normed1_t, outs.normed1_t)
    for copy in far:
        copy.wait()

    low_q = half_masks(128)
    key_slot = (lax.broadcasted_iota(jnp.int32, (256, 256), 0) % 128) // 32
    query_slot = (lax.broadcasted_iota(jnp.int32, (256, 256), 1) % 128) // 32
    same_slot = key_slot == query_slot

    def softmax(scores):
        weights_ = jnp.exp(scores - jnp.max(scores, axis=0, keepdims=True))
        return (weights_ * (1.0 / jnp.sum(weights_, axis=0, keepdims=True))).astype(BF16)

    def attend(keys, values, queries, visible):
        scores = dot_nt(keys, jnp.concatenate(by_head(queries, low_q), axis=0))
        if visible is not None:
            scores = jnp.where(visible, scores, MASKED_SCORE)
        probs = softmax(scores)
        return (probs[:, :LANES], probs[:, LANES:]), join_heads(dot_tn(probs, values), low_q)

    def spatial_pairs(step, carry):
        loaded = []
        for pair in (step * 2, step * 2 + 1):
            for which in range(2):
                keys = spatial[pair, SP_KEY + which * 256 : SP_KEY + which * 256 + 256]
                values = spatial[pair, SP_VALUE + which * 256 : SP_VALUE + which * 256 + 256]
                queries = spatial[pair, SP_QUERY + which * 128 : SP_QUERY + which * 128 + 128]
                loaded.append((keys, values, queries, same_slot if which else None))
        done = [attend(*one) for one in loaded]
        for i in range(2):
            pair = step * 2 + i
            for which in range(2):
                for head in range(2):
                    at = (which * 2 + head) * 256
                    spatial[pair, at : at + 256] = done[i * 2 + which][0][head]
            value = interleave(done[i * 2][1], done[i * 2 + 1][1])
            work.context[:, lanes(pair, LANES)] = value.astype(BF16)
        return carry

    lax.fori_loop(0, PAIRS // 2, spatial_pairs, 0)
    save(keep.spatial, outs.spatial)

    def project_into(source, weight, bias, before, target):
        def one(step, carry):
            at = lanes(step, 256)
            target[:, at] = dot(source[...], weight[:, at]) + params[bias : bias + 1, at] + before[:, at]
            return carry

        lax.fori_loop(0, WIDTH // 256, one, 0, unroll=2)

    loads.w_sout.wait()
    project_into(work.context, work.w_sout, 2, resid0, resid1)
    there = Swap(place, work.normed, work.arranged, swap_sems, 0, True)
    norm_forward(resid1, param(3), param(4), work.normed, keep.normal2, keep.scale2, there.start_block)
    save(keep.normal2, outs.normal2)
    save(keep.scale2, outs.scale2)
    transpose_into(work.context, keep.context1_t)
    share(keep.context1_t, outs.context1_t)
    loads.w_tqkv.wait()
    there.wait()

    temporal = keep.temporal

    def temporal_project(column, base, scale):
        def one(step, carry):
            value = dot(work.arranged[...], work.w_tqkv[:, lanes(column + step, 256)]) * scale
            value = value.astype(BF16)
            temporal[step * 2, base : base + ROWS] = value[:, :LANES]
            temporal[step * 2 + 1, base : base + ROWS] = value[:, LANES:]
            return carry

        lax.fori_loop(0, 4, one, 0, unroll=2)

    temporal_project(0, TP_QUERY, 0.125)
    temporal_project(4, TP_KEY, 1.0)
    temporal_project(8, TP_VALUE, 1.0)
    key_row = lax.broadcasted_iota(jnp.int32, (128, 256), 0)
    query_row = lax.broadcasted_iota(jnp.int32, (128, 256), 1) % 128
    key_rank, query_rank = jnp.zeros_like(key_row), jnp.zeros_like(query_row)
    for at in range(8):
        big_rank, small_rank = ins.big_order[0, at], ins.small_order[place.ta // 4, at]
        key_rank = jnp.where(key_row // 16 == at, jnp.where(key_row % 16 < 8, big_rank, small_rank), key_rank)
        query_rank = jnp.where(query_row // 16 == at, jnp.where(query_row % 16 < 8, big_rank, small_rank), query_rank)
    seen = (key_row % 16 == query_row % 16) & (key_rank <= query_rank)

    def temporal_pairs(step, carry):
        loaded = []
        for pair in (step * 2, step * 2 + 1):
            for half in range(2):
                keys = temporal[pair, TP_KEY + half * 128 : TP_KEY + half * 128 + 128]
                values = temporal[pair, TP_VALUE + half * 128 : TP_VALUE + half * 128 + 128]
                queries = temporal[pair, TP_QUERY + half * 128 : TP_QUERY + half * 128 + 128]
                loaded.append((keys, values, queries, seen))
        done = [attend(*one) for one in loaded]
        for i in range(2):
            pair = step * 2 + i
            for half in range(2):
                for head in range(2):
                    at = (half * 2 + head) * 128
                    temporal[pair, at : at + 128] = done[i * 2 + half][0][head]
                at = slice(half * 128, half * 128 + 128)
                work.context_send[at, lanes(pair, LANES)] = done[i * 2 + half][1].astype(BF16)
        return carry

    back = [Swap(place, work.context_send, work.context_back, swap_sems, 1 + i, False, HALVES[i]) for i in range(2)]
    lax.fori_loop(0, PAIRS // 4, temporal_pairs, 0)
    back[0].start()
    lax.fori_loop(PAIRS // 4, PAIRS // 2, temporal_pairs, 0)
    back[1].start()
    save(keep.temporal, outs.temporal)
    transpose_into(work.arranged, keep.normed2_t)
    share(keep.normed2_t, outs.normed2_t)
    loads.w_tout.wait()
    for i in range(2):
        back[i].wait()

        def add_half(step, carry, i=i):
            at = lanes(step, 256)
            value = dot(work.context_back[:, HALVES[i]], work.w_tout[HALVES[i], at])
            if i == 0:
                resid2[:, at] = value + params[5:6, at] + resid1[:, at]
            else:
                resid2[:, at] += value
            return carry

        lax.fori_loop(0, WIDTH // 256, add_half, 0, unroll=2)
    norm_forward(resid2, param(6), param(7), work.normed3, keep.normal3, keep.scale3)
    save(keep.normal3, outs.normal3)
    save(keep.scale3, outs.scale3)
    transpose_into(work.context_back, keep.context2_t)
    share(keep.context2_t, outs.context2_t)
    transpose_into(work.normed3, keep.normed3_t)
    share(keep.normed3_t, outs.normed3_t)

    total, hidden, slope = work.total, work.hidden, keep.slope
    total[...] += param(8)
    loads.w_fin.wait()
    loads.w_fout.wait()
    root = 0.7978845608028654

    def inner(step, slot):
        hidden[slot] = dot(work.normed3[...], work.w_fin[:, lanes(step, HIDE)])

    def feed_copies(step):
        here, there_ = keep.activated_t.at[step], outs.activated_t.at[step]
        return (
            pltpu.make_async_copy(here, there_.at[:, :ROWS], feed_sems.at[0, step]),
            remote(here, there_.at[:, ROWS:], feed_sems.at[1, step], feed_sems.at[2, step], place.partner),
            pltpu.make_async_copy(slope.at[step], outs.slope.at[step], feed_sems.at[3, step]),
        )

    def feed(step, slot, ahead):
        value = hidden[slot] + work.inner_bias[pl.ds(step, 1)]
        if ahead:
            inner(step + 1, 1 - slot)
        square = value * value
        bent = jnp.tanh(root * value * (1.0 + 0.044715 * square))
        half = 0.5 * (1.0 + bent)
        active = (value * half).astype(BF16)
        rise = half + 0.5 * value * (1.0 - bent * bent) * (root * (1.0 + 0.134145 * square))
        slope[step] = rise.astype(BF16)
        for block in range(HIDE // LANES):
            at = slice(block * LANES, block * LANES + LANES)
            keep.activated_t[step, at] = active[:, at].T
        down = work.w_fout.at[pl.ds(pl.multiple_of(step * HIDE, HIDE), HIDE)]
        for column in range(WIDTH // 256):
            at = slice(column * 256, column * 256 + 256)
            total[:, at] += dot(active, down[:, at])
        for copy in feed_copies(step):
            copy.start()

    def feed_two(step, carry):
        feed(step * 2, 0, True)
        feed(step * 2 + 1, 1, True)
        return carry

    for one in back:
        one.sent()
    inner(0, 0)
    lax.fori_loop(0, PAIRS // 2 - 1, feed_two, 0)
    feed(PAIRS - 2, 0, True)
    feed(PAIRS - 1, 1, False)

    def finish_rows(step, carry):
        value = total[pl.ds(pl.multiple_of(step * 32, 32), 32)]
        near = pl.ds(pl.multiple_of(step * 16, 16), 16)
        keep.big_out[near] = family(value, 0).astype(BF16)
        keep.small_out[near] = (family(value, 1) * ins.live[step // 2].astype(F32)).astype(BF16)
        return carry

    lax.fori_loop(0, 8, finish_rows, 0)
    save(keep.big_out, outs.big_out)
    save(keep.small_out, outs.small_out)
    there.sent()
    for copy in copies + shared + [one for step in range(PAIRS) for one in feed_copies(step)]:
        copy.wait()


def forward(ins, scalars, vectors, weights):
    sem = pltpu.SemaphoreType.DMA
    lefts, work = list(FORWARD_LEFTS.values()), list(FORWARD_WORK.values())
    kept = list(FORWARD_OUTS.values()) + lefts
    results = list(FORWARD_OUTS.values()) + [((rows, depth, 2 * columns), dtype) for (rows, depth, columns), dtype in lefts]
    in_keys, weight_keys = tuple(vars(ins)) + tuple(vars(scalars)), tuple(vars(weights))
    results = pl.pallas_call(
        functools.partial(forward_kernel, in_keys, len(vectors), weight_keys),
        out_shape=[jax.ShapeDtypeStruct(shape, dtype) for shape, dtype in results],
        in_specs=[VMEM] * len(vars(ins)) + [SMEM] * len(vars(scalars)) + [VMEM] * len(vectors) + [ANY] * len(weight_keys),
        out_specs=[ANY] * len(kept),
        scratch_shapes=[pltpu.VMEM(shape, dtype) for shape, dtype in kept + work]
        + [sem((len(weight_keys),)), sem((len(kept),)), sem((3, 2, 16)), sem((2, 4)), sem((2, 6)), sem((4, PAIRS))],
        compiler_params=pltpu.CompilerParams(
            collective_id=1, has_side_effects=True, vmem_limit_bytes=62 * 2**20
        ),
        cost_estimate=pl.CostEstimate(flops=9 * 10**9, bytes_accessed=60 * 2**20, transcendentals=4 * 10**6),
        name="layer_forward",
    )(*vars(ins).values(), *vars(scalars).values(), *vectors, *vars(weights).values())
    return named(FORWARD_OUTS | FORWARD_LEFTS, list(results))


class Reduction:
    def __init__(self, place, index, refs, sems):
        self.place, self.index, self.refs, self.sems = place, index, refs, sems
        k, n, shares, unused_output, self.column = MATRICES[index]
        self.half = n // 2
        self.depth = k // 64
        self.groups = self.depth // 16
        if shares is None:
            self.blocks = [[(part, 0, 4), (3, part, part + 1 + part // 2)] for part in range(3)]
        else:
            ends = [sum(shares[: part + 1]) for part in range(3)]
            self.blocks = [[(0, end - share, end)] for share, end in zip(shares, ends)]
        self.cells = [[(g, t) for g, low, high in part for t in range(low, high)] for part in self.blocks]
        self.spans, start = [], 0
        for cells in self.cells:
            self.spans.append((start, start + len(cells)))
            start += len(cells)
        self.first_unit = sum(m[1] // 2 // LANES * (m[0] // 1024) for m in MATRICES[:index])
        self.send_unit = SEND_UNITS[index]
        self.local_done = self.left_done = False
        self.straight = index >= 4
        self.whole_parts = ()

    def columns(self, core):
        return pl.ds(pl.multiple_of(self.column + core * self.half, LANES), self.half)

    def left_local(self):
        return pltpu.make_async_copy(self.refs.at_in, self.refs.at, self.sems.local.at[self.index, 0])

    def right_local(self):
        r, s, i, core = self.refs, self.sems, self.index, self.place.core
        source = r.source.at[:, self.columns(core)]
        return pltpu.make_async_copy(source, r.g.at[:ROWS], s.local.at[i, 1])

    def right_far(self):
        r, s, i, core = self.refs, self.sems, self.index, self.place.core
        source = r.source.at[:, self.columns(1 - core)]
        return remote(source, r.g.at[ROWS:], s.ex_send.at[i, 1], s.ex_recv.at[i, 1], self.place.partner)

    def lefts(self):
        self.left_local().start()

    def rights(self):
        self.right_far().start()
        self.right_local().start()

    def right_local_done(self):
        if not self.local_done:
            self.right_local().wait()
            self.local_done = True

    def rights_sent(self):
        self.right_local_done()
        self.right_far().wait_send()

    def loaded(self):
        self.right_far().wait_recv()
        if not self.left_done:
            self.left_local().wait()
        self.right_local_done()

    def span(self, part):
        return self.spans[part]

    def copy(self, part, stage, step):
        r, s, i = self.refs, self.sems, self.index
        low, high = self.span(part)
        here = slice(self.first_unit + low, self.first_unit + high)
        device, slot = self.place.along(ORDERS[part][stage], step)
        if stage == 1:
            source = r.r1.at[0, here, slot]
            target = r.r2.at[step - 1, here]
        else:
            source = r.r2.at[0, here, slot]
            target = r.r3.at[step - 1, here]
        return remote(
            source, target, s.send.at[i, part, stage, step - 1], s.recv.at[i, part, stage, step - 1], device
        )

    def left_block(self, part, slot, group):
        at = self.refs.at
        rows = slice(group * 16, group * 16 + 16)
        if part == 0:
            blocks = [at[y // 2, :, y % 2, slot, rows] for y in range(4)]
        elif part == 1:
            blocks = [at[slot // 2, :, slot % 2, :, rows]]
        else:
            blocks = [at[:, slot, :, x, rows] for x in range(4)]
        blocks = [block.reshape(-1, block.shape[-1]) for block in blocks]
        return blocks[0] if len(blocks) == 1 else jnp.concatenate(blocks, axis=0)

    def products(self, part, slot, emit):
        unit = self.spans[part][0]
        for group, low, high in self.blocks[part]:
            left = self.left_block(part, slot, group)
            for tile in range(low, high, 2):
                width = min(2, high - tile)
                value = dot(left, self.refs.g[:, tile * LANES : (tile + width) * LANES])
                for i in range(width):
                    emit(unit, value[:, i * LANES : (i + 1) * LANES].reshape(4, 4, 16, LANES))
                    unit += 1

    def relay(self, part, way):
        r, s, i = self.refs, self.sems, self.index
        low, high = self.span(part)
        here = slice(self.first_unit + low, self.first_unit + high)
        half = slice(way * 2, way * 2 + 2)
        device = self.place.along(ORDERS[part][0], 3 if way else 1)[0]
        source = r.s1.at[0, self.send_unit + low : self.send_unit + high, half]
        target = r.r1.at[2, here, half]
        return remote(source, target, s.send.at[i, part, 0, way], s.recv.at[i, part, 0, way], device)

    def direct(self, part, way):
        r, s, i = self.refs, self.sems, self.index
        low, high = self.span(part)
        here = slice(self.first_unit + low, self.first_unit + high)
        device = self.place.along(ORDERS[part][0], 3 if way else 1)[0]
        source = r.s1.at[1 + way, self.send_unit + low : self.send_unit + high]
        target = r.r1.at[way, here]
        return remote(source, target, s.send.at[i, part, 0, 2 + way], s.recv.at[i, part, 0, 2 + way], device)

    def whole(self, part, step):
        r, s, i = self.refs, self.sems, self.index
        low, high = self.span(part)
        here = slice(self.first_unit + low, self.first_unit + high)
        at = (1, 0, 2)[step - 1]
        source = r.s1.at[at, self.send_unit + low : self.send_unit + high]
        target = r.r1.at[step - 1, here]
        device = self.place.along(ORDERS[part][0], step)[0]
        return remote(source, target, s.send.at[i, part, 0, step], s.recv.at[i, part, 0, step], device)

    def first(self, parts=ALL):
        r = self.refs
        for part in parts:
            if part in self.whole_parts:
                for step in (1, 3, 2):
                    slot = self.place.along(ORDERS[part][0], step)[1]

                    def keep(unit, value, step=step):
                        r.s1[(1, 0, 2)[step - 1], self.send_unit + unit] = value.astype(BF16)

                    self.products(part, slot, keep)
                    self.whole(part, step).start()
                continue
            slot = self.place.along(ORDERS[part][0], 2)[1]

            def emit(unit, value):
                r.s1[0, self.send_unit + unit] = value.astype(BF16)

            self.products(part, slot, emit)
            for way in range(2):
                self.relay(part, way).start()

    def pass_on(self, parts=ALL):
        r = self.refs
        for part in parts:
            if part in self.whole_parts:
                continue
            for way in range(2):
                self.relay(part, way).wait_recv()
                slot = self.place.along(ORDERS[part][0], 3 if way else 1)[1]

                def emit(unit, value, way=way):
                    at = self.first_unit + unit
                    for half in range(2):
                        some = slice(half * 2, half * 2 + 2)
                        one = value[some]
                        if half == way:
                            one = one + r.r1[2, at, some].astype(F32)
                        r.s1[1 + way, self.send_unit + unit, some] = one.astype(BF16)

                self.products(part, slot, emit)
                self.direct(part, way).start()

    def relay_sent(self):
        for part in range(3):
            if part in self.whole_parts:
                self.whole(part, 2).wait_send()
                continue
            for way in range(2):
                self.relay(part, way).wait_send()

    def direct_sent(self):
        for part in range(3):
            for way in range(2):
                if part in self.whole_parts:
                    self.whole(part, 3 if way else 1).wait_send()
                else:
                    self.direct(part, way).wait_send()

    def second(self, parts=ALL):
        r = self.refs
        for part in parts:
            slot = self.place.along(ORDERS[part][0], 0)[1]
            terms = 2
            if part in self.whole_parts:
                terms = 3
                for step in (1, 2, 3):
                    self.whole(part, step).wait_recv()
            else:
                for way in range(2):
                    self.direct(part, way).wait_recv()

            def emit(unit, value, terms=terms):
                at = self.first_unit + unit
                for i in range(terms):
                    value = value + r.r1[i, at].astype(F32)
                r.r1[0, at] = value.astype(BF16)

            self.products(part, slot, emit)
            for step in (1, 2, 3):
                self.copy(part, 1, step).start()

    def third(self, parts=ALL):
        r = self.refs
        for part in parts:
            slot = self.place.along(ORDERS[part][1], 0)[1]
            for step in (1, 2, 3):
                self.copy(part, 1, step).wait_recv()

            def one(unit, carry, slot=slot):
                value = r.r1[0, unit, slot].astype(F32)
                for i in range(3):
                    value = value + r.r2[i, unit].astype(F32)
                r.r2[0, unit] = value.astype(BF16)
                return carry

            low, high = self.span(part)
            lax.fori_loop(self.first_unit + low, self.first_unit + high, one, 0)
            for step in (1, 2, 3):
                self.copy(part, 2, step).start()

    def mine(self):
        return self.place.y_hi * 4 + self.place.x

    def gather_copy(self, y_hi, x, slot):
        r, s, i, place = self.refs, self.sems, self.index, self.place
        target = r.out.at[slot // 4, slot % 4, :, self.columns(place.core)]
        return remote(
            r.piece.at[place.y_hi], target, s.ag_send.at[i, y_hi * 4 + x], s.ag_recv.at[i, slot],
            place.device(y_hi=y_hi, x=x),
        )

    def twin_copy(self):
        r, s, i, place = self.refs, self.sems, self.index, self.place
        block = r.piece.at[place.y_hi]
        return remote(block, block, s.ag_send.at[i, 0], s.ag_recv.at[i, 0], place.device(y_hi=1 - place.y_hi))

    def line_copy(self, step):
        r, s, i, place = self.refs, self.sems, self.index, self.place
        target = r.out.at[:, place.x, :, self.columns(place.core)]
        device = place.device(x=(place.x + step) % 4)
        return remote(r.piece, target, s.ag_send.at[i, step], s.ag_recv.at[i, step], device)

    def own_copy(self):
        place, i, piece = self.place, self.index, self.refs.piece
        columns = self.columns(place.core)
        if self.straight:
            target = self.refs.out.at[place.y_hi, place.x, :, columns]
            return pltpu.make_async_copy(piece.at[place.y_hi], target, self.sems.local.at[i, 2])
        return pltpu.make_async_copy(piece, self.refs.out.at[:, place.x, :, columns], self.sems.local.at[i, 2])

    def others(self):
        place = self.place
        for y_step in (0, 1):
            y_hi = (place.y_hi + y_step) % 2
            for x_step in range(4):
                if y_step or x_step:
                    yield y_hi, (place.x + x_step) % 4

    def fourth(self, parts=ALL):
        r = self.refs
        for part in parts:
            slot = self.place.along(ORDERS[part][2], 0)[1]
            for step in (1, 2, 3):
                self.copy(part, 2, step).wait_recv()
            for cell, (group, tile) in enumerate(self.cells[part]):
                at = self.first_unit + self.spans[part][0] + cell
                value = r.r2[0, at, slot].astype(F32)
                for i in range(3):
                    value = value + r.r3[i, at].astype(F32)
                rows, columns = slice(group * 16, group * 16 + 16), slice(tile * LANES, tile * LANES + LANES)
                r.piece[self.place.y_hi, rows, columns] = value.astype(BF16)
    def gather(self):
        if self.straight:
            self.own_copy().start()
            for y_hi, x in self.others():
                self.gather_copy(y_hi, x, self.mine()).start()
        else:
            self.twin_copy().start()

    def spread(self):
        if not self.straight:
            self.twin_copy().wait_recv()
            self.own_copy().start()
            for step in (1, 2, 3):
                self.line_copy(step).start()

    def cross_copy(self):
        r, s, i, core = self.refs, self.sems, self.index, self.place.core
        block = r.out.at[:, :, :, self.columns(core)]
        return remote(block, block, s.cross.at[i, 0], s.cross.at[i, 1], self.place.partner)

    def fifth(self):
        self.own_copy().wait()
        if self.straight:
            for y_hi, x in self.others():
                self.gather_copy(y_hi, x, y_hi * 4 + x).wait_recv()
        else:
            for step in (1, 2, 3):
                self.line_copy(step).wait_recv()
        self.cross_copy().start()

    def finish(self):
        self.cross_copy().wait()
        if self.straight:
            for y_hi, x in self.others():
                self.gather_copy(y_hi, x, self.mine()).wait_send()
        else:
            self.twin_copy().wait_send()
            for step in (1, 2, 3):
                self.line_copy(step).wait_send()
        for part in range(3):
            for stage in (1, 2):
                for step in (1, 2, 3):
                    self.copy(part, stage, step).wait_send()


GAIN1, SHIFT1, SPATIAL_BIAS, GAIN2, SHIFT2, TEMPORAL_BIAS, GAIN3, SHIFT3, INNER, OUTER = 8, 9, 10, 11, 12, 13, 14, 15, 16, 20


class SmallSums:
    def __init__(self, place, refs, sems):
        self.place, self.refs, self.sems = place, refs, sems

    def share(self, core):
        return slice(None), lanes(core, WIDTH // 2)

    def cross(self):
        r, core = self.refs, self.place.core
        return remote(
            r.sums.at[self.share(1 - core)], r.sums_core, self.sems.at[0, 0, 0], self.sems.at[1, 0, 0],
            self.place.partner,
        )

    def along(self, stage, step):
        device = self.place.along("xyz"[stage], step)[0]
        return remote(
            self.refs.sums_total.at[stage], self.refs.sums_recv.at[stage, step - 1],
            self.sems.at[0, stage + 1, step - 1], self.sems.at[1, stage + 1, step - 1], device,
        )

    def final(self):
        block = self.refs.sums_final.at[self.share(self.place.core)]
        return remote(block, block, self.sems.at[0, 4, 0], self.sems.at[1, 4, 0], self.place.partner)

    def begin(self):
        self.cross().start()

    def step0(self):
        r = self.refs
        self.cross().wait()
        r.sums_total[0] = r.sums[self.share(self.place.core)] + r.sums_core[...]
        for step in (1, 2, 3):
            self.along(0, step).start()

    def advance(self, stage):
        r = self.refs
        value = r.sums_total[stage]
        for step in (1, 2, 3):
            self.along(stage, step).wait_recv()
            value = value + r.sums_recv[stage, step - 1]
        if stage < 2:
            r.sums_total[stage + 1] = value
            for step in (1, 2, 3):
                self.along(stage + 1, step).start()
        else:
            r.sums_final[self.share(self.place.core)] = value
            self.final().start()

    def finish(self, out, sem):
        self.final().wait()
        copy = pltpu.make_async_copy(self.refs.sums_final, out, sem)
        copy.start()
        for stage in range(3):
            for step in (1, 2, 3):
                self.along(stage, step).wait_send()
        copy.wait()


BACK_OUTS = dict(
    big_grad=((128, WIDTH), F32),
    small_grad=((128, WIDTH), F32),
    small_sums=((24, WIDTH), F32),
)
SLOTS = 3
BACK_WORK = dict(
    s1=((3, 32, 4, 4, 16, LANES), BF16),
    r1=((3, 64, 4, 4, 16, LANES), BF16),
    r2=((3, 64, 4, 16, LANES), BF16),
    r3=((3, 64, 16, LANES), BF16),
    tall=((SLOTS, HIDE, WIDTH), BF16),
    broad=((SLOTS, WIDTH, HIDE), BF16),
    slope_in=((SLOTS, ROWS, HIDE), BF16),
    record=((SLOTS, SP_ROWS, LANES), BF16),
    resid=((ROWS, WIDTH), F32),
    grad=((ROWS, WIDTH), F32),
    total=((ROWS, WIDTH), F32),
    low3=((ROWS, WIDTH), BF16),
    low2=((ROWS, WIDTH), BF16),
    low1=((ROWS, WIDTH), BF16),
    hidden_low=((ROWS, HIDDEN), BF16),
    packed=((ROWS, 3 * WIDTH), BF16),
    swap_send=((ROWS, WIDTH), BF16),
    context_back=((ROWS, WIDTH), BF16),
    normed_back=((ROWS, WIDTH), BF16),
    context_grad=((2, 128, WIDTH), BF16),
    far_send=((ROWS, 2 * WIDTH), BF16),
    far_recv=((ROWS, 2 * WIDTH), BF16),
    inner_sums=((PAIRS, HIDE), F32),
    sums=((24, WIDTH), F32),
    sums_core=((24, WIDTH // 2), F32),
    sums_total=((3, 24, WIDTH // 2), F32),
    sums_recv=((3, 3, 24, WIDTH // 2), F32),
    sums_final=((24, WIDTH), F32),
    frame_sums=((8, WIDTH), F32),
    scale=((ROWS, LANES), F32),
    gains=((8, WIDTH), F32),
)


BACK_SEMS = dict(
    local=(7, 3),
    ex_send=(7, 2),
    ex_recv=(7, 2),
    send=(7, 3, 3, 4),
    recv=(7, 3, 3, 4),
    ag_send=(7, 8),
    ag_recv=(7, 8),
    cross=(7, 2),
    ring=(4, SLOTS),
    io=(5,),
    swap=(3, 2, 16),
    far=(2,),
    sums=(2, 5, 3),
)


def backward_kernel(in_keys, saved_keys, weight_keys, *refs):
    refs = list(refs)
    ins = named(in_keys, refs)
    gains = [refs.pop(0) for _ in range(3)]
    lefts = [refs.pop(0) for _ in GRADIENTS]
    saved, weights, outs = named(saved_keys, refs), named(weight_keys, refs), named(BACK_OUTS, refs)
    matrix_outs = [refs.pop(0) for _ in GRADIENTS]
    work = named(BACK_WORK, refs)
    ats = [refs.pop(0) for _ in GRADIENTS]
    gs, pieces = ([refs.pop(0) for _ in MATRICES] for _ in range(2))
    sems = named(BACK_SEMS, refs)
    ring_sems, io_sems, swap_sems, far_sems, sum_sems = sems.ring, sems.io, sems.swap, sems.far, sems.sums
    place = Place()
    frame = place.ta // 2
    sources = (work.low3, work.hidden_low, work.low2, work.packed, work.low1, work.packed, work.packed)
    reductions = []
    for i, (_, _, _, output, _) in enumerate(MATRICES):
        own = Names(at_in=lefts[output], at=ats[output], g=gs[i], piece=pieces[i], out=matrix_outs[output])
        own.source = sources[i]
        own.s1, own.r1, own.r2, own.r3 = work.s1, work.r1, work.r2, work.r3
        reductions.append(Reduction(place, i, own, sems))
    fout, fin, tout, tqkv, sout, sq, skv = reductions
    skv.left_done = True
    small = SmallSums(place, work, sum_sems)

    def tall(source, base, index):
        slot = (base + index) % SLOTS
        rows = pl.ds(pl.multiple_of(index * HIDE, HIDE), HIDE)
        return pltpu.make_async_copy(source.at[rows], work.tall.at[slot], ring_sems.at[0, slot])

    def broad(source, base, index):
        slot = (base + index) % SLOTS
        return pltpu.make_async_copy(
            source.at[:, lanes(index, HIDE)], work.broad.at[slot], ring_sems.at[1, slot]
        )

    def slope(base, index):
        slot = (base + index) % SLOTS
        return pltpu.make_async_copy(saved.slope.at[index], work.slope_in.at[slot], ring_sems.at[2, slot])

    def record(source, base, index):
        slot = (base + index) % SLOTS
        return pltpu.make_async_copy(
            source.at[index], work.record.at[slot, pl.ds(0, source.shape[1])], ring_sems.at[3, slot]
        )

    def open_stream(maker, count):
        for index in range(min(SLOTS, count)):
            maker(index).start()

    def refill(maker, count, index):
        @pl.when(index + SLOTS < count)
        def _():
            maker(index + SLOTS).start()

    fout_tiles = functools.partial(tall, weights.w_fout, 0)
    tout_tiles = functools.partial(tall, weights.w_tout, 8)
    sout_tiles = functools.partial(tall, weights.w_sout, 10)
    fin_tiles = functools.partial(broad, weights.w_fin, 0)
    tqkv_tiles = functools.partial(broad, weights.w_tqkv, 8)
    sqkv_tiles = functools.partial(broad, weights.w_sqkv, 14)
    slopes = functools.partial(slope, 0)
    temporal_records = functools.partial(record, saved.temporal, 0)
    spatial_records = functools.partial(record, saved.spatial, 8)

    class Kept:
        def __init__(self, normals, scales):
            self.copies = (
                pltpu.make_async_copy(normals, work.resid, io_sems.at[0]),
                pltpu.make_async_copy(scales, work.scale, io_sems.at[4]),
            )
            for copy in self.copies:
                copy.start()

        def wait(self):
            for copy in self.copies:
                copy.wait()

    fout.lefts()
    open_stream(fout_tiles, 8)
    open_stream(slopes, 8)
    open_stream(fin_tiles, 8)
    work.sums[...] = jnp.zeros_like(work.sums)
    for row, gain in enumerate(gains):
        work.gains[row : row + 1] = gain[...].astype(F32).reshape(1, WIDTH)
    greet(place, True)

    grad, total = work.grad, work.total

    def start_rows(step, carry):
        near = pl.ds(pl.multiple_of(step * 16, 16), 16)
        big = ins.big_cot[near].astype(F32)
        little = ins.small_cot[near].astype(F32) * ins.live[step // 2].astype(F32)
        merged = interleave(big, little)
        rows = pl.ds(pl.multiple_of(step * 32, 32), 32)
        grad[rows] = merged
        work.low3[rows] = merged.astype(BF16)
        total[rows] = jnp.zeros_like(merged)
        work.sums[OUTER : OUTER + 1] += jnp.sum(merged, axis=0, keepdims=True)
        return carry

    lax.fori_loop(0, 8, start_rows, 0)
    fout.rights()
    fin.lefts()
    kept3 = Kept(saved.normal3, saved.scale3)

    def feed(step, carry):
        slopes(step).wait()
        fout_tiles(step).wait()
        fin_tiles(step).wait()
        slot = step % SLOTS
        down = dot_nt(work.low3[...], work.tall[slot]) * work.slope_in[slot].astype(F32)
        work.inner_sums[pl.ds(step, 1)] = jnp.sum(down, axis=0, keepdims=True)
        low = down.astype(BF16)
        work.hidden_low[:, lanes(step, HIDE)] = low
        for column in range(WIDTH // 256):
            at = slice(column * 256, column * 256 + 256)
            total[:, at] += dot_nt(low, work.broad[slot, at])
        refill(slopes, 8, step)
        refill(fout_tiles, 8, step)
        refill(fin_tiles, 8, step)
        return carry

    lax.fori_loop(0, 2, feed, 0)
    fout.loaded()
    fout.first()
    lax.fori_loop(2, 8, feed, 0)
    fin.rights()
    open_stream(temporal_records, 8)
    for one in (tout, tqkv, sout, sq):
        one.lefts()
    open_stream(tout_tiles, 2)
    open_stream(sout_tiles, 1)
    open_stream(tqkv_tiles, 6)
    for part in range(PAIRS):
        at = part % 2 * HIDE
        work.sums[INNER + part // 2 : INNER + part // 2 + 1, at : at + HIDE] = work.inner_sums[part : part + 1]

    def norm_back(gradient, gain_row, row, low, bias_row):
        gain = work.gains[gain_row : gain_row + 1]

        def one(step, carry):
            rows = rows16(step)
            error = gradient[rows].astype(F32)
            normal, scale = work.resid[rows], work.scale[rows, 0:1]
            scaled = error * gain
            mean_one = jnp.mean(scaled, axis=-1, keepdims=True)
            mean_two = jnp.mean(scaled * normal, axis=-1, keepdims=True)
            value = grad[rows] + (scaled - mean_one - normal * mean_two) * scale
            grad[rows] = value
            if low is not None:
                low[rows] = value.astype(BF16)
            gains = error * normal
            sums = [part[:8] + part[8:] for part in (gains, error, value)]
            return tuple(a + b for a, b in zip(carry, sums))

        zero = jnp.zeros((8, WIDTH), F32)
        sums = lax.fori_loop(0, 16, one, (zero, zero, zero), unroll=4)
        work.sums[row : row + 1] = jnp.sum(sums[0], axis=0, keepdims=True)
        work.sums[row + 1 : row + 2] = jnp.sum(sums[1], axis=0, keepdims=True)
        if bias_row is not None:
            work.sums[bias_row : bias_row + 1] = jnp.sum(sums[2], axis=0, keepdims=True)

    kept3.wait()
    norm_back(total, 2, GAIN3, work.low2, TEMPORAL_BIAS)
    kept2 = Kept(saved.normal2, saved.scale2)
    tout.rights()

    there = [Swap(place, work.swap_send, work.context_back, swap_sems, i, True, HALVES[i]) for i in range(2)]
    for index in range(2):
        tout_tiles(index).wait()
        slot = (8 + index) % SLOTS
        work.swap_send[:, HALVES[index]] = dot_nt(work.low2[...], work.tall[slot]).astype(BF16)
        there[index].start()
    sout_tiles(1).start()
    fout.pass_on(Z)
    fin.loaded()
    fin.first(Z)
    there[0].wait()
    fout.pass_on(XY)
    fin.first(XY)

    low_lanes = half_masks(128)

    def attention_back(probs, keys, values, queries, upstream):
        upstreams = jnp.concatenate(by_head(upstream, low_lanes), axis=0)
        prob = jnp.concatenate(probs, axis=1)
        wide = prob.astype(F32)
        back = dot_nt(values, upstreams)
        delta = jnp.sum(wide * back, axis=0, keepdims=True)
        error = (wide * (back - delta)).astype(BF16)
        key_grad = dot(error, jnp.concatenate(by_head(queries, low_lanes), axis=0))
        value_grad = dot(prob, upstreams)
        query_grad = join_heads(dot_tn(error, keys), low_lanes)
        return query_grad * 0.125, key_grad, value_grad

    def temporal_pair(pair, carry):
        temporal_records(pair).wait()
        slot = pair % SLOTS
        for half in range(2):
            base = half * 128

            def rows(start, half=half):
                return work.record[slot, start + half * 128 : start + half * 128 + 128]

            probs = [work.record[slot, (half * 2 + h) * 128 : (half * 2 + h) * 128 + 128] for h in range(2)]
            upstream = work.context_back[base : base + 128, lanes(pair, LANES)]
            grads = attention_back(probs, rows(TP_KEY), rows(TP_VALUE), rows(TP_QUERY), upstream)
            for i, value in enumerate(grads):
                work.packed[base : base + 128, lanes(pair + i * PAIRS, LANES)] = value.astype(BF16)
        refill(temporal_records, 8, pair)
        return carry

    lax.fori_loop(0, PAIRS // 2, temporal_pair, 0, unroll=2)
    there[1].wait()
    lax.fori_loop(PAIRS // 2, PAIRS, temporal_pair, 0, unroll=2)
    open_stream(spatial_records, 8)
    tqkv.rights()

    def project_back(maker, base, start, stop):
        def one(step, carry):
            maker(step).wait()
            slot = (base + step) % SLOTS
            low = work.packed[:, lanes(step, HIDE)]
            for column in range(WIDTH // 256):
                at = slice(column * 256, column * 256 + 256)
                value = dot_nt(low, work.broad[slot, at])
                total[:, at] += value
            refill(maker, 6, step)
            return carry

        if start == 0:
            total[...] = jnp.zeros_like(total)
        lax.fori_loop(start, stop, one, 0)

    project_back(tqkv_tiles, 8, 0, 3)
    project_back(tqkv_tiles, 8, 3, 6)
    open_stream(sqkv_tiles, 6)
    for one in there:
        one.sent()
    work.swap_send[...] = total[...].astype(BF16)
    back = Swap(place, work.swap_send, work.normed_back, swap_sems, 2, False)
    back.start()
    fin.pass_on(Z)
    back.wait()
    fout.relay_sent()
    tout.loaded()
    tout.first()
    tqkv.loaded()
    tqkv.first()
    fout.second()
    fin.pass_on(XY)
    fout.direct_sent()

    kept2.wait()
    norm_back(work.normed_back, 1, GAIN2, work.low1, SPATIAL_BIAS)
    kept1 = Kept(saved.normal1, saved.scale1)
    sout.rights()
    for index in range(2):
        sout_tiles(index).wait()
        slot = (10 + index) % SLOTS
        at = slice(index * HIDE, index * HIDE + HIDE)
        value = dot_nt(work.low1[...], work.tall[slot])
        for which in range(2):
            work.context_grad[which, :, at] = family(value, which).astype(BF16)
    tqkv.rights_sent()

    def spatial_pair(pair, carry):
        spatial_records(pair).wait()
        slot = (8 + pair) % SLOTS
        all_grads = []
        for which in range(2):

            def rows(start, count, which=which):
                return work.record[slot, start + which * count : start + which * count + count]

            probs = [work.record[slot, (which * 2 + h) * 256 : (which * 2 + h) * 256 + 256] for h in range(2)]
            upstream = work.context_grad[which, :, lanes(pair, LANES)]
            all_grads.append(
                attention_back(
                    probs, rows(SP_KEY, 256), rows(SP_VALUE, 256), rows(SP_QUERY, 128), upstream
                )
            )
        for i in range(3):
            value = interleave(all_grads[0][i][:128], all_grads[1][i][:128])
            work.packed[:, lanes(pair + i * PAIRS, LANES)] = value.astype(BF16)
        for i in (1, 2):
            value = interleave(all_grads[0][i][128:], all_grads[1][i][128:])
            work.far_send[:, lanes(pair + (i - 1) * PAIRS, LANES)] = value.astype(BF16)
        refill(spatial_records, 8, pair)
        return carry

    lax.fori_loop(0, PAIRS // 2, spatial_pair, 0, unroll=2)
    tout.pass_on()
    tqkv.pass_on()
    fin.second(Z)
    lax.fori_loop(PAIRS // 2, PAIRS, spatial_pair, 0, unroll=2)
    far = remote(work.far_send, work.far_recv, far_sems.at[0], far_sems.at[1], place.partner)
    far.start()
    sq.rights()
    fin.relay_sent()
    sout.loaded()
    sout.first()
    sq.loaded()
    sq.first()
    fin.second(XY)
    far.wait()

    def join(step, carry):
        rows = rows16(step)
        value = work.packed[rows, WIDTH:].astype(F32) + work.far_recv[rows].astype(F32)
        work.packed[rows, WIDTH:] = value.astype(BF16)
        return carry

    lax.fori_loop(0, 16, join, 0, unroll=4)
    skv.rights()
    project_back(sqkv_tiles, 14, 0, 2)
    skv.loaded()
    skv.first()
    fout.third()
    fin.direct_sent()
    sout.pass_on()
    sq.pass_on()
    project_back(sqkv_tiles, 14, 2, 4)
    skv.pass_on()
    project_back(sqkv_tiles, 14, 4, 6)
    tout.second()
    tqkv.second()
    fout.fourth()
    fout.gather()
    kept1.wait()
    norm_back(total, 0, GAIN1, None, None)

    def finish_rows(step, carry):
        value = grad[pl.ds(pl.multiple_of(step * 32, 32), 32)]
        big, little = family(value, 0), family(value, 1)
        near = pl.ds(pl.multiple_of(step * 16, 16), 16)
        total[near] = big
        total[pl.ds(pl.multiple_of(128 + step * 16, 16), 16)] = little
        work.frame_sums[0:1] += jnp.sum(big, axis=0, keepdims=True)
        work.frame_sums[pl.ds(1 + step // 2, 1)] += jnp.sum(little, axis=0, keepdims=True)
        return carry

    work.frame_sums[...] = jnp.zeros_like(work.frame_sums)
    lax.fori_loop(0, 8, finish_rows, 0)
    out_copies = [
        pltpu.make_async_copy(total.at[:128], outs.big_grad, io_sems.at[1]),
        pltpu.make_async_copy(total.at[128:], outs.small_grad, io_sems.at[2]),
    ]
    for copy in out_copies:
        copy.start()
    table, at_row = jnp.zeros((8, WIDTH), F32), lax.broadcasted_iota(jnp.int32, (8, WIDTH), 0)
    for i in range(5):
        action = ins.big_actions[0, frame] if i == 0 else ins.small_actions[i - 1, frame]
        table = table + jnp.where(at_row == action, work.frame_sums[i : i + 1], 0.0)
    work.sums[0:8] = table
    small.begin()
    fin.third()
    sq.second()
    sout.second()
    small.step0()
    skv.second()
    fout.spread()
    tout.third()
    tqkv.third()
    small.advance(0)
    sq.third()
    sout.third()
    skv.third()
    fin.fourth()
    fin.gather()
    small.advance(1)
    sq.fourth()
    sq.gather()
    sout.fourth()
    sout.gather()
    skv.fourth()
    skv.gather()
    tout.fourth()
    tout.gather()
    tqkv.fourth()
    tqkv.gather()
    fout.fifth()
    fin.spread()
    small.advance(2)
    sq.fifth()
    sout.fifth()
    tout.spread()
    tqkv.spread()
    skv.fifth()
    fin.fifth()
    tout.fifth()
    tqkv.fifth()
    small.finish(outs.small_sums, io_sems.at[3])
    for one in reductions:
        one.finish()
    for one in (tout, tqkv, sout, sq, skv):
        one.relay_sent()
        one.direct_sent()
    for one in (fout, fin, tout, sout, sq, skv):
        one.rights_sent()
    back.sent()
    for copy in out_copies:
        copy.wait()


def backward(ins, scalars, gains, lefts, saved, weights):
    sem = pltpu.SemaphoreType.DMA
    count = len(GRADIENTS)
    work = [pltpu.VMEM(shape, dtype) for shape, dtype in BACK_WORK.values()]
    work += [pltpu.VMEM((2, 4, 2, 4, k // 64, 2 * ROWS), BF16) for k, _ in GRADIENTS]
    work += [pltpu.VMEM((2 * ROWS, n // 2), BF16) for _, n, _, _, _ in MATRICES]
    work += [pltpu.VMEM((2, k // 64, n // 2), BF16) for k, n, _, _, _ in MATRICES]
    work += [sem(shape) for shape in BACK_SEMS.values()]
    shapes = list(BACK_OUTS.values()) + [((2, 4, k // 64, n), BF16) for k, n in GRADIENTS]
    in_keys, saved_keys, weight_keys = tuple(vars(ins)) + tuple(vars(scalars)), tuple(vars(saved)), tuple(vars(weights))
    return pl.pallas_call(
        functools.partial(backward_kernel, in_keys, saved_keys, weight_keys),
        out_shape=[jax.ShapeDtypeStruct(shape, dtype) for shape, dtype in shapes],
        in_specs=[VMEM] * len(vars(ins))
        + [SMEM] * len(vars(scalars))
        + [VMEM] * len(gains)
        + [ANY] * (count + len(saved_keys) + len(weight_keys)),
        out_specs=[ANY] * len(shapes),
        scratch_shapes=work,
        compiler_params=pltpu.CompilerParams(
            collective_id=2, has_side_effects=True, vmem_limit_bytes=63 * 2**20
        ),
        cost_estimate=pl.CostEstimate(flops=18 * 10**9, bytes_accessed=80 * 2**20, transcendentals=0),
        name="layer_backward",
    )(
        *vars(ins).values(),
        *vars(scalars).values(),
        *gains,
        *[left.reshape(2, 4, 2, 4, k // 64, 2 * ROWS) for left, (k, _) in zip(lefts, GRADIENTS)],
        *vars(saved).values(),
        *vars(weights).values(),
    )


SUM_VECTORS = (
    (GAIN1, 1),
    (SHIFT1, 1),
    (SPATIAL_BIAS, 1),
    (GAIN2, 1),
    (SHIFT2, 1),
    (TEMPORAL_BIAS, 1),
    (GAIN3, 1),
    (SHIFT3, 1),
    (INNER, 4),
    (OUTER, 1),
)


def widen_kernel(*refs):
    refs = list(refs)
    count, passed = len(GRADIENTS), 4
    narrow = [refs.pop(0) for _ in range(count)]
    plain = [refs.pop(0) for _ in range(passed)]
    sums = refs.pop(0)
    wide = [refs.pop(0) for _ in range(count)]
    plain_out = [refs.pop(0) for _ in range(passed)]
    table, vectors = refs.pop(0), [refs.pop(0) for _ in SUM_VECTORS]
    narrow_in, wide_out = refs[:count], refs[count : 2 * count]
    between, sems = refs[2 * count : 2 * count + passed], refs[2 * count + passed]
    loads = [pltpu.make_async_copy(narrow[i], narrow_in[i], sems.at[0, i]) for i in range(count)]
    stores = [pltpu.make_async_copy(wide_out[i], wide[i], sems.at[1, i]) for i in range(count)]
    reads = [pltpu.make_async_copy(plain[i], between[i], sems.at[2, i]) for i in range(passed)]
    moves = [pltpu.make_async_copy(between[i], plain_out[i], sems.at[3, i]) for i in range(passed)]
    for copy in loads + reads:
        copy.start()
    table[...] = sums[0:8]
    for (row, rows), vector in zip(SUM_VECTORS, vectors):
        for i in range(rows):
            vector[i * WIDTH : (i + 1) * WIDTH] = sums[row + i]
    for i in range(count):
        loads[i].wait()

        def one(step, carry, i=i):
            wide_out[i][rows16(step)] = narrow_in[i][rows16(step)].astype(F32)
            return carry

        lax.fori_loop(0, narrow_in[i].shape[0] // 16, one, 0, unroll=2)
        stores[i].start()
    for read, move in zip(reads, moves):
        read.wait()
        move.start()
    for copy in stores + moves:
        copy.wait()


def widen(matrices, plain, sums):
    count = len(matrices)
    vectors = [jax.ShapeDtypeStruct((rows * WIDTH,), F32) for _, rows in SUM_VECTORS]
    shapes = [jax.ShapeDtypeStruct(one.shape, F32) for one in matrices]
    scratch = [pltpu.VMEM(one.shape, BF16) for one in matrices] + [pltpu.VMEM(one.shape, F32) for one in matrices]
    scratch += [pltpu.VMEM(one.shape, one.dtype) for one in plain]
    results = pl.pallas_call(
        widen_kernel,
        out_shape=shapes
        + [jax.ShapeDtypeStruct(one.shape, one.dtype) for one in plain]
        + [jax.ShapeDtypeStruct((8, WIDTH), F32)]
        + vectors,
        in_specs=[ANY] * (count + len(plain)) + [VMEM],
        out_specs=[ANY] * (count + len(plain)) + [VMEM] * (1 + len(vectors)),
        scratch_shapes=scratch + [pltpu.SemaphoreType.DMA((4, count))],
        compiler_params=pltpu.CompilerParams(vmem_limit_bytes=62 * 2**20),
        cost_estimate=pl.CostEstimate(flops=0, bytes_accessed=14 * 2**20, transcendentals=0),
        name="widen",
    )(*matrices, *plain, sums)
    results = list(results)
    wide = [results.pop(0) for _ in range(count)]
    passed = [results.pop(0) for _ in plain]
    return wide, passed, results


def body(
    big_tokens,
    small_tokens,
    big_actions,
    small_actions,
    big_order,
    small_order,
    small_live,
    action_table,
    norm1_gain,
    norm1_bias,
    spatial_qkv,
    spatial_out,
    spatial_out_bias,
    norm2_gain,
    norm2_bias,
    temporal_qkv,
    temporal_out,
    temporal_out_bias,
    norm3_gain,
    norm3_bias,
    ffn_in,
    ffn_in_bias,
    ffn_out,
    ffn_out_bias,
    big_cotangent,
    small_cotangent,
):
    scalars = Names(
        big_actions=big_actions,
        small_actions=small_actions,
        big_order=big_order,
        small_order=small_order,
        live=small_live,
    )
    vectors = (
        norm1_gain,
        norm1_bias,
        spatial_out_bias,
        norm2_gain,
        norm2_bias,
        temporal_out_bias,
        norm3_gain,
        norm3_bias,
        ffn_out_bias,
    )
    weights = Names(
        w_sqkv=spatial_qkv,
        w_sout=spatial_out,
        w_tqkv=temporal_qkv,
        w_tout=temporal_out,
        w_fin=ffn_in,
        w_fout=ffn_out,
    )
    saved = forward(
        Names(
            big=big_tokens.reshape(128, WIDTH),
            small=small_tokens.reshape(128, WIDTH),
            table=action_table,
            inner_bias=ffn_in_bias,
        ),
        scalars,
        vectors,
        weights,
    )
    big_grad, small_grad, sums, *matrices = backward(
        Names(big_cot=big_cotangent.reshape(128, WIDTH), small_cot=small_cotangent.reshape(128, WIDTH)),
        Names(big_actions=big_actions, small_actions=small_actions, live=small_live),
        (norm1_gain, norm2_gain, norm3_gain),
        (saved.activated_t, saved.normed3_t, saved.context2_t, saved.normed2_t, saved.context1_t, saved.normed1_t),
        Names(
            normal1=saved.normal1,
            normal2=saved.normal2,
            normal3=saved.normal3,
            scale1=saved.scale1,
            scale2=saved.scale2,
            scale3=saved.scale3,
            spatial=saved.spatial,
            temporal=saved.temporal,
            slope=saved.slope,
        ),
        weights,
    )
    matrices = [one.reshape(-1, one.shape[-1]) for one in matrices]
    matrices, passed, small = widen(matrices, (saved.big_out, saved.small_out, big_grad, small_grad), sums)
    g_fout, g_fin, g_tout, g_tqkv, g_sout, g_sqkv = matrices
    table, gain1, shift1, bias_s, gain2, shift2, bias_t, gain3, shift3, bias_in, bias_out = small
    return (
        passed[0].reshape(1, 128, WIDTH),
        passed[1].reshape(4, 32, WIDTH),
        passed[2].reshape(1, 128, WIDTH),
        passed[3].reshape(4, 32, WIDTH),
        table,
        gain1,
        shift1,
        g_sqkv,
        g_sout,
        bias_s,
        gain2,
        shift2,
        g_tqkv,
        g_tout,
        bias_t,
        gain3,
        shift3,
        g_fin,
        bias_in,
        g_fout,
        bias_out,
    )


def solution(mesh):
    spread, by_col = P("col", "ta", None), P("col", None)
    return jax.shard_map(
        body,
        mesh=mesh,
        in_specs=(spread, spread, by_col, by_col, by_col, by_col, P("col")) + (P(),) * 17 + (spread, spread),
        out_specs=(spread,) * 4
        + (P(),) * 3
        + (by_col, by_col, P(), P(), P(), by_col, by_col, P(), P(), P(), by_col, P(), by_col, P()),
        check_vma=False,
    )
```
